32 devices in a mesh: gx: 4 (over y, core), gy: 8 (over z, x).
Axes of the slice: x: 2, y: 2, z: 4, core: 2. Of those that a mesh axis runs over, the one named last changes fastest.
Arguments:
- displacement: float32 [3, 96, 64, 128], P(None, 'gx', 'gy'), may hold values from -6 to 6
- velocity: float32 [3, 96, 64, 128], P(None, 'gx', 'gy'), may hold values from -6 to 6
- external_force: float32 [3, 96, 64, 128], P(None, 'gx', 'gy'), may hold values from -6 to 6
- node_mass: float32 [96, 64, 128], P('gx', 'gy'), may hold values from 0.5 to 2
- stiffness: float32 [96, 64, 128], P('gx', 'gy'), may hold values from 0.5 to 2
- cloak_list: int32 [4, 8, 48], P('gx'), may hold values from -1 to 191, as said below
- micro_state: float32 [4, 8, 128, 48, 128], P('gx', 'gy'), may hold values from -6 to 6
- localization: float32 [256, 6], replicated, may hold values from -3.6 to 3.6
- modes: float32 [256, 128], replicated, may hold values from -0.5 to 0.5
- point_weight: float32 [256], replicated, may hold values from 0.5 to 2
- point_modulus: float32 [256], replicated, may hold values from 1 to 10
- softening: float32 [256], replicated, may hold values from 0.2 to 2
Outputs:
- displacement_next: float32 [3, 96, 64, 128], P(None, 'gx', 'gy')
- velocity_next: float32 [3, 96, 64, 128], P(None, 'gx', 'gy')
- micro_state_next: float32 [4, 8, 128, 48, 128], P('gx', 'gy')
The draws below stay inside these ranges and needn't reach their ends.
Inputs may be any that keep to these rules, and one draw needn't show every extreme that they name: cloak_list[p, t, :] holds distinct pencil indices x * 8 + y of tile (p, t) in ascending order followed by -1; in every gx index exactly one tile lists 48 pencils and every other tile lists between 20 and 24 pencils, 20 reached in every gx index; the tiles sharing a gx index list exactly 192 pencils together.
All inputs are finite; a program needn't handle non-finite values.
Results may differ from the reference program's by a relative error of at most 0.0003.
Values sent between devices are 32-bit elements; how exact they have to be, the bound alone decides.
No kernel may reach another device: no remote copies, remote signals or barrier semaphores. Data moves between devices by JAX's collectives and lax.ppermute only.
A program may use at most 64 MiB of HBM per device.

```python
import math
import jax
import jax.numpy as jnp
from jax import lax

CX = 24
CY = 8
LZ = 128
P_SIZE = 256
M = 128
ITERS = 3
NX = 96
NY = 64
OWN = 24
CMAX = 48
N_GX = 4
N_GY = 8


def tile_list(subkey, listed_count):
    shuffled = jax.random.permutation(subkey, CX * CY)
    marked = jnp.where(jnp.arange(CX * CY) < listed_count, shuffled, CX * CY)
    ranked = jnp.sort(marked)[:CMAX]
    return jnp.where(ranked >= CX * CY, -1, ranked).astype(jnp.int32)


def row_lists(subkey):
    busiest = jax.random.randint(jax.random.fold_in(subkey, 1), (), 0, N_GY)
    others_count = N_GY - 1
    base_short = OWN // others_count
    extra_short = OWN % others_count
    order = jax.random.permutation(jax.random.fold_in(subkey, 2), others_count)
    shortfall = base_short + (order < extra_short).astype(jnp.int32)
    others = OWN - shortfall
    column = jnp.arange(N_GY)
    shifted = jnp.minimum(jnp.where(column > busiest, column - 1, column), N_GY - 2)
    tile_counts = jnp.where(column == busiest, CMAX, others[shifted])
    tile_keys = jax.vmap(jax.random.fold_in, in_axes=(None, 0))(subkey, column + 100)
    return jax.vmap(tile_list)(tile_keys, tile_counts)


def draw_cloak_list(key, part):
    row_index = jnp.arange(N_GX)
    row_keys = jax.vmap(jax.random.fold_in, in_axes=(None, 0))(key, row_index * 1000 + 7)
    return jax.vmap(row_lists)(row_keys)


def levels(rng, extent, pieces, low, high):
    def one(dim, parts):
        draws = jax.random.uniform(jax.random.fold_in(jax.random.fold_in(rng, 6), dim), (parts,), jnp.float32, low / len(pieces), high / len(pieces))
        return jnp.repeat(jnp.exp(draws), extent[dim] // parts).reshape((-1,) + (1,) * (len(extent) - dim - 1))

    factor_of = one(*pieces[0])
    for cut in pieces[1:]:
        factor_of = factor_of * one(*cut)
    return factor_of


def noise(rng, extent, width, reach, split=(), held_as=jnp.bfloat16):
    loudness = levels(rng, extent, split, -0.22, 0.18) if split else 1.0
    result = jax.random.normal(rng, extent, jnp.float32) * width * loudness
    return jnp.minimum(jnp.maximum(result, -reach), reach).astype(held_as)


def setup_inputs(seed: int = 0) -> dict:
    splits = jax.random.split(jax.random.key(seed), 13)
    displacement = noise(splits[0], (3, NX, NY, LZ), 1.0, 6.0, ((1, 4), (2, 8)), jnp.float32)
    velocity = noise(splits[1], (3, NX, NY, LZ), 1.0, 6.0, ((1, 4), (2, 8)), jnp.float32)
    external_force = noise(splits[2], (3, NX, NY, LZ), 1.0, 6.0, ((1, 4), (2, 8)), jnp.float32)
    node_mass = jnp.clip(jnp.exp(math.log(2.0) - 1.3862944 * jax.random.uniform(splits[3], (NX, NY, LZ), jnp.float32) ** levels(splits[3], (NX, NY, LZ), ((0, 4), (1, 8)), -0.2, 0.2)), 0.5, 2.0)
    stiffness = jnp.clip(jnp.exp(math.log(2.0) - 1.3862944 * jax.random.uniform(splits[4], (NX, NY, LZ), jnp.float32) ** levels(splits[4], (NX, NY, LZ), ((0, 4), (1, 8)), -0.2, 0.2)), 0.5, 2.0)
    cloak_list = draw_cloak_list(jax.random.fold_in(splits[12], 71), 0)
    micro_state = noise(splits[6], (N_GX, N_GY, M, CMAX, LZ), 1.0, 6.0, ((0, 4), (1, 8)), jnp.float32)
    localization = noise(splits[7], (P_SIZE, 6), 0.6, 3.6, (), jnp.float32)
    modes = noise(splits[8], (P_SIZE, M), M ** -0.5, 0.5, (), jnp.float32)
    point_weight = jnp.clip(jnp.exp(jax.random.uniform(splits[9], (P_SIZE,), jnp.float32, math.log(0.5), math.log(2.0))), 0.5, 2.0)
    point_modulus = jnp.clip(jnp.exp(jax.random.uniform(splits[10], (P_SIZE,), jnp.float32, math.log(1.0), math.log(10.0))), 1.0, 10.0)
    softening = jnp.clip(jnp.exp(jax.random.uniform(splits[11], (P_SIZE,), jnp.float32, math.log(0.2), math.log(2.0))), 0.2, 2.0)
    return dict(displacement=displacement, velocity=velocity, external_force=external_force, node_mass=node_mass, stiffness=stiffness, cloak_list=cloak_list, micro_state=micro_state, localization=localization, modes=modes, point_weight=point_weight, point_modulus=point_modulus, softening=softening)


step_size = 0.25
highest = lax.Precision.HIGHEST

def pair_mean(values_in, dimension):
    upper = lax.slice_in_dim(values_in, 1, values_in.shape[dimension], axis=dimension)
    lower = lax.slice_in_dim(values_in, 0, values_in.shape[dimension] - 1, axis=dimension)
    return 0.5 * (upper + lower)

def pair_diff(values_in, dimension):
    upper = lax.slice_in_dim(values_in, 1, values_in.shape[dimension], axis=dimension)
    lower = lax.slice_in_dim(values_in, 0, values_in.shape[dimension] - 1, axis=dimension)
    return upper - lower

def voigt_strain(node_field):
    first_slope = pair_mean(pair_mean(pair_diff(node_field, 1), 2), 3)
    second_slope = pair_mean(pair_mean(pair_diff(node_field, 2), 1), 3)
    third_slope = pair_mean(pair_mean(pair_diff(node_field, 3), 1), 2)
    return jnp.stack([first_slope[0], second_slope[1], third_slope[2], third_slope[1] + second_slope[2], third_slope[0] + first_slope[2], second_slope[0] + first_slope[1]])

def linear_stress(strain, stiffness):
    volume_strain = strain[0] + strain[1] + strain[2]
    normal = [stiffness * (volume_strain + 2.0 * strain[column]) for column in range(3)]
    shears = [stiffness * strain[column] for column in range(3, 6)]
    return jnp.stack(normal + shears)

def assemble(stress, low_pad, high_pad):
    widths = ((0, 0), (low_pad, high_pad), (low_pad, high_pad), (1, 0))
    first_flux = jnp.pad(jnp.stack([stress[0], stress[5], stress[4]]), widths)
    second_flux = jnp.pad(jnp.stack([stress[5], stress[1], stress[3]]), widths)
    third_flux = jnp.pad(jnp.stack([stress[4], stress[3], stress[2]]), widths)
    return -(pair_diff(pair_mean(pair_mean(first_flux, 2), 3), 1) + pair_diff(pair_mean(pair_mean(second_flux, 1), 3), 2) + pair_diff(pair_mean(pair_mean(third_flux, 1), 2), 3))

def tangent_inverse(modes, point_weight, point_modulus):
    weights = point_weight * point_modulus / modes.shape[0]
    matrix = jnp.dot(modes.T * weights[None, :], modes, precision=highest)
    factor = jnp.linalg.cholesky(matrix)
    identity = jnp.eye(modes.shape[1], dtype=matrix.dtype)
    return jax.scipy.linalg.cho_solve((factor, True), identity)

def respond(point_strain, point_modulus, softening):
    return point_modulus[:, None, None] * point_strain / jnp.sqrt(1.0 + softening[:, None, None] * point_strain * point_strain)

def micro_model(strain_in, modal_state, localization, modes, scaled, point_modulus, softening, inverse):
    imposed = jnp.einsum('pj,jgz->pgz', localization, strain_in, precision=highest)
    for newton_step in range(ITERS):
        point_strain = imposed + jnp.einsum('pm,mgz->pgz', modes, modal_state, precision=highest)
        response = respond(point_strain, point_modulus, softening)
        residual = jnp.einsum('pm,pgz->mgz', modes, scaled[:, None, None] * response, precision=highest)
        modal_state = modal_state - jnp.einsum('mn,ngz->mgz', inverse, residual, precision=highest)
    point_strain = imposed + jnp.einsum('pm,mgz->pgz', modes, modal_state, precision=highest)
    response = respond(point_strain, point_modulus, softening)
    stress = jnp.einsum('pj,pgz->jgz', localization, scaled[:, None, None] * response, precision=highest)
    return (stress, modal_state)

def reference(displacement, velocity, external_force, node_mass, stiffness, cloak_list, micro_state, localization, modes, point_weight, point_modulus, softening):
    padded = jnp.pad(displacement, ((0, 0), (0, 1), (0, 1), (0, 1)))
    strain = voigt_strain(padded)
    stress = linear_stress(strain, stiffness)
    inverse = tangent_inverse(modes, point_weight, point_modulus)
    scaled = point_weight / localization.shape[0]
    strain_flat = strain.reshape(6, NX * NY, LZ)
    tile_count = N_GX * N_GY
    tile_lists = cloak_list.reshape(tile_count, CMAX)
    tile_states = micro_state.reshape(tile_count, M, CMAX, LZ)
    tile_number = jnp.arange(tile_count, dtype=jnp.int32)

    def per_tile(inputs):
        entries, modal_state, number = inputs
        listed = entries >= 0
        in_tile = jnp.maximum(entries, 0)
        global_x = number // N_GY * CX + in_tile // CY
        global_y = number % N_GY * CY + in_tile % CY
        pencil = (global_x * NY + global_y).astype(jnp.int32)
        tile_strain = jnp.take(strain_flat, pencil, axis=1)
        tile_stress, new_state = micro_model(tile_strain, modal_state, localization, modes, scaled, point_modulus, softening, inverse)
        new_state = jnp.where(listed[None, :, None], new_state, 0.0)
        target = jnp.where(listed, pencil, NX * NY).astype(jnp.int32)
        return (tile_stress, new_state, target)
    stresses, states, targets = lax.map(per_tile, (tile_lists, tile_states, tile_number))
    values = jnp.transpose(stresses, (1, 0, 2, 3)).reshape(6, tile_count * CMAX, LZ)
    stress = stress.reshape(6, NX * NY, LZ).at[:, targets.reshape(-1)].set(values, mode='drop')
    stress = stress.reshape(6, NX, NY, LZ)
    internal = assemble(stress, 1, 0)
    acceleration = (external_force - internal) / node_mass[None]
    velocity_next = velocity + step_size * acceleration
    displacement_next = displacement + step_size * velocity_next
    return (displacement_next, velocity_next, states.reshape(N_GX, N_GY, M, CMAX, LZ))
```

```python
import functools

import jax
import jax.numpy as jnp
from jax import lax
from jax.experimental import pallas as pl
from jax.experimental.pallas import tpu as pltpu
from jax.sharding import PartitionSpec as P

ITERS = 3
STEP = 0.25
HIGHEST = lax.Precision.HIGHEST
F32 = jnp.float32
BF16 = jnp.bfloat16
VMEM = pl.BlockSpec(memory_space=pltpu.VMEM)
SMEM = pl.BlockSpec(memory_space=pltpu.SMEM)


def split(x):
    high = x.astype(BF16)
    return high, (x - high.astype(F32)).astype(BF16)


def dot(a, b):
    return jnp.dot(a, b, preferred_element_type=F32)


def exact(a, b):
    return jnp.dot(a, b, precision=HIGHEST, preferred_element_type=F32)


def inverse_rows(matrix):
    size = matrix.shape[0]
    blocks = [matrix[i : i + 8] for i in range(0, size, 8)]
    lane = lax.broadcasted_iota(jnp.int32, (8, size), 1)
    row = lax.broadcasted_iota(jnp.int32, (8, size), 0)
    for b in range(size // 8):
        panel = blocks[b]
        for s in range(8):
            k = b * 8 + s
            column = jnp.broadcast_to(panel[:, k : k + 1], (8, size))
            pivot_row = jnp.broadcast_to(panel[s : s + 1, :], (8, size))
            inverse = 1.0 / jnp.broadcast_to(column[s : s + 1, :], (8, size))
            new_row = jnp.where(lane == k, inverse, pivot_row * inverse)
            rest = jnp.where(lane == k, 0.0, panel) - column * new_row
            panel = jnp.where(row == s, new_row, rest)
        rows = [jnp.broadcast_to(panel[s : s + 1, :], (8, size)) for s in range(8)]
        inside = jnp.logical_and(lane >= b * 8, lane < b * 8 + 8)
        order = list(range(b + 1, size // 8)) + list(range(b))
        for i in order:
            old = blocks[i]
            new = jnp.where(inside, 0.0, old)
            for s in range(8):
                k = b * 8 + s
                new = new - jnp.broadcast_to(old[:, k : k + 1], (8, size)) * rows[s]
            blocks[i] = new
        blocks[b] = panel
    return jnp.concatenate(blocks, axis=0)


def matrices_kernel(
    modes_ref, local_ref, weight_ref, modulus_ref, soft_ref,
    first_ref, newton_ref, back_ref, stress_ref, wide,
):
    points, count = modes_ref.shape
    modes = modes_ref[...]
    modes_t = modes.T
    weight = weight_ref[...] / points
    modulus = modulus_ref[...]
    root = jnp.sqrt(soft_ref[...])
    matrix = exact(modes_t * (weight * modulus), modes)
    inverse = inverse_rows(matrix)
    scale = weight * modulus / root
    wide[...] = jnp.zeros_like(wide)
    wide[:, 0 : local_ref.shape[1]] = local_ref[...]
    local_t = wide[...].T
    stress_ref[...] = (local_t[0:16] * scale).astype(BF16)
    soft_modes = (modes_t * root).T
    soft_local = (local_t * root).T
    back = exact(inverse, modes_t * scale)
    newton = exact(soft_modes, back)
    high, low = split(soft_modes)
    first_ref[:, 0:count] = high
    first_ref[:, count : 2 * count] = high
    first_ref[:, 2 * count : 3 * count] = low
    shape = soft_local.shape
    lane = lax.broadcasted_iota(jnp.int32, shape, 1)
    moved8 = pltpu.roll(soft_local, 8, 1)
    moved16 = pltpu.roll(soft_local, 16, 1)
    high8 = (soft_local + moved8).astype(BF16).astype(F32)
    low16 = moved16 - moved16.astype(BF16).astype(F32)
    first_ref[:, 3 * count :] = jnp.where(lane < 16, high8, low16).astype(BF16)
    high, low = split(newton)
    newton_ref[:, 0:points] = high
    newton_ref[:, points : 2 * points] = low
    high, low = split(back)
    back_ref[:, 0:points] = high
    back_ref[:, points : 2 * points] = low


def respond(u):
    return u * lax.rsqrt(1.0 + u * u)


def cells(states, strains, first_ref, newton_ref, back_ref, stress_ref):
    points = newton_ref.shape[0]
    count = back_ref.shape[0]
    newton_high = newton_ref[:, 0:points]
    newton_low = newton_ref[:, points:]
    back_high = back_ref[:, 0:points]
    back_low = back_ref[:, points:]
    state_high, state_low = split(states)
    strain_high = strains.astype(BF16).astype(F32)
    strain_low = strains - strain_high
    zero = jnp.zeros_like(strains)
    strain_part = jnp.concatenate(
        [strain_high, strain_low, strain_high] + [zero] * (count // 8 - 3), axis=0
    ).astype(BF16)
    u = dot(first_ref[:, 0 : 2 * count], jnp.concatenate([state_high, state_low], axis=0))
    u = u + dot(first_ref[:, 2 * count :], jnp.concatenate([state_high, strain_part], axis=0))
    total = None
    for step in range(ITERS):
        h = respond(u)
        total = h if total is None else total + h
        if step < ITERS - 1:
            high, low = split(h)
            u = u - (dot(newton_high, high) + dot(newton_low, high) + dot(newton_high, low))
        else:
            u = u - dot(newton_high, h.astype(BF16))
    high, low = split(total)
    new_states = states - (dot(back_high, high) + dot(back_low, high) + dot(back_high, low))
    stress = dot(stress_ref[...], respond(u).astype(BF16))
    return new_states, stress[0:8]


def main_kernel(
    lists_ref, disp_ref, xhalo_ref, yhalo_ref, corner_ref, stiff_ref, state_ref,
    first_ref, newton_ref, back_ref, stress_ref,
    force_ref, xface_ref, yface_ref, cface_ref, out_ref,
    strain_s, stress_s,
):
    rows, columns, layers = stiff_ref.shape
    count = back_ref.shape[0]
    most = lists_ref.shape[1]
    tile = (columns, layers)
    lane = lax.broadcasted_iota(jnp.int32, tile, 1)
    sub = lax.broadcasted_iota(jnp.int32, tile, 0)
    last_lane = lane == layers - 1
    first_lane = lane == 0
    last_sub = sub == columns - 1
    first_sub = sub == 0
    member = lax.axis_index("gy")

    def node_row(c, i):
        own = disp_ref[c, i] if i < rows else xhalo_ref[c]
        edge = yhalo_ref[c, i : i + 1] if i < rows else corner_ref[c : c + 1]
        up = jnp.where(last_sub, jnp.broadcast_to(edge, tile), pltpu.roll(own, columns - 1, 0))
        mean, diff = 0.5 * (up + own), up - own
        mean_up = jnp.where(last_lane, 0.0, pltpu.roll(mean, layers - 1, 1))
        diff_up = jnp.where(last_lane, 0.0, pltpu.roll(diff, layers - 1, 1))
        return 0.5 * (mean_up + mean), 0.5 * (diff_up + diff), mean_up - mean

    lower = [node_row(c, 0) for c in range(3)]
    zero_tile = jnp.zeros(tile, F32)
    for i in range(rows):
        upper = [node_row(c, i + 1) for c in range(3)]
        g = [
            (upper[c][0] - lower[c][0], 0.5 * (upper[c][1] + lower[c][1]), 0.5 * (upper[c][2] + lower[c][2]))
            for c in range(3)
        ]
        lower = upper
        strain = [g[0][0], g[1][1], g[2][2], g[1][2] + g[2][1], g[0][2] + g[2][0], g[0][1] + g[1][0]]
        stiffness = stiff_ref[i]
        volume = strain[0] + strain[1] + strain[2]
        for c in range(8):
            place = pl.ds(i * columns * 8 + c, columns, stride=8)
            if c >= 6:
                strain_s[place, :] = zero_tile
                continue
            strain_s[place, :] = strain[c]
            stress_s[place, :] = stiffness * (volume + 2.0 * strain[c] if c < 3 else strain[c])

    group = 4

    def body(q, carry):
        base = q * group
        busy = lists_ref[member, base] >= 0

        @pl.when(busy)
        def _():
            for pair in range(group // 2):
                entries = [lists_ref[member, base + 2 * pair + s] for s in range(2)]
                places = [pl.multiple_of(jnp.maximum(e, 0) * 8, 8) for e in entries]
                slots = [pl.ds(base + 2 * pair + s, count, stride=most) for s in range(2)]
                states = jnp.concatenate([state_ref[slot, :] for slot in slots], axis=1)
                strains = jnp.concatenate([strain_s[pl.ds(p, 8), :] for p in places], axis=1)
                new_states, stress = cells(states, strains, first_ref, newton_ref, back_ref, stress_ref)
                for s in range(2):
                    part = new_states[:, s * layers : (s + 1) * layers]
                    out_ref[slots[s], :] = jnp.where(entries[s] >= 0, part, 0.0)

                    @pl.when(entries[s] >= 0)
                    def _():
                        stress_s[pl.ds(places[s], 8), :] = stress[:, s * layers : (s + 1) * layers]

        @pl.when(jnp.logical_not(busy))
        def _():
            for s in range(group):
                out_ref[pl.ds(base + s, count, stride=most), :] = jnp.zeros((count, layers), F32)

        return carry

    lax.fori_loop(0, most // group, body, 0)

    def fluxes(s, side_mean, side_diff, lane_zero):
        def along(v):
            down = jnp.where(lane_zero, 0.0, pltpu.roll(v, 1, 1))
            return 0.5 * (v + down), v - down

        first = [along(side_mean(s[c]))[0] for c in (0, 5, 4)]
        second = [along(side_diff(s[c]))[0] for c in (5, 1, 3)]
        third = [along(side_mean(s[c]))[1] for c in (4, 3, 2)]
        half = [0.5 * (second[c] + third[c]) for c in range(3)]
        return [(first[c] + half[c], half[c] - first[c]) for c in range(3)]

    def shift(v):
        return jnp.where(first_sub, 0.0, pltpu.roll(v, 1, 0))

    below = None
    for i in range(rows):
        s = [stress_s[pl.ds(i * columns * 8 + c, columns, stride=8), :] for c in range(6)]
        here = fluxes(s, lambda v: 0.5 * (v + shift(v)), lambda v: v - shift(v), first_lane)
        for c in range(3):
            force_ref[c, i] = -here[c][0] if below is None else -(here[c][0] + below[c][1])
        below = here
    for c in range(3):
        xface_ref[c] = -below[c][1]
    s = [stress_s[pl.ds((columns - 1) * 8 + c, rows, stride=columns * 8), :] for c in range(6)]
    wide_zero = lax.broadcasted_iota(jnp.int32, (rows, layers), 1) == 0
    side = fluxes(s, lambda v: 0.5 * v, lambda v: -v, wide_zero)
    for c in range(3):
        yface_ref[c] = -side[c][0]
        yface_ref[c, 1:rows] = yface_ref[c, 1:rows] - side[c][1][0 : rows - 1]
        cface_ref[c : c + 1] = -side[c][1][rows - 1 : rows]


def update_kernel(
    disp_ref, velocity_ref, external_ref, mass_ref, force_ref, xface_ref, yface_ref, cface_ref,
    disp_out, velocity_out,
):
    rows, columns, layers = mass_ref.shape
    first_sub = lax.broadcasted_iota(jnp.int32, (columns, layers), 0) == 0
    for i in range(rows):
        factor = STEP / mass_ref[i]
        for c in range(3):
            edge = yface_ref[c, i : i + 1]
            if i == 0:
                edge = edge + cface_ref[c : c + 1]
            internal = force_ref[c, i] + jnp.where(
                first_sub, jnp.broadcast_to(edge, (columns, layers)), 0.0
            )
            if i == 0:
                internal = internal + xface_ref[c]
            velocity = velocity_ref[c, i] + factor * (external_ref[c, i] - internal)
            velocity_out[c, i] = velocity
            disp_out[c, i] = disp_ref[c, i] + STEP * velocity


def shape(*dims, dtype=F32):
    return jax.ShapeDtypeStruct(dims, dtype)


def on_device(
    displacement, velocity, external_force, node_mass, stiffness, cloak_list, micro_state,
    localization, modes, point_weight, point_modulus, softening,
):
    rows, columns, layers = stiffness.shape
    points, count = modes.shape
    most = cloak_list.shape[2]
    gx, gy = lax.axis_size("gx"), lax.axis_size("gy")
    along_x = [(i + 1, i) for i in range(gx - 1)]
    along_y = [(i + 1, i) for i in range(gy - 1)]
    both = [((i + 1) * gy + j + 1, i * gy + j) for i in range(gx - 1) for j in range(gy - 1)]
    back = lambda pairs: [(b, a) for a, b in pairs]
    xhalo = lax.ppermute(displacement[:, 0], "gx", along_x)
    yhalo = lax.ppermute(displacement[:, :, 0], "gy", along_y)
    corner = lax.ppermute(displacement[:, 0, 0], ("gx", "gy"), both)

    first, newton, back_m, stress_m = pl.pallas_call(
        matrices_kernel,
        out_shape=(
            shape(points, 4 * count, dtype=BF16), shape(points, 2 * points, dtype=BF16),
            shape(count, 2 * points, dtype=BF16), shape(16, points, dtype=BF16),
        ),
        in_specs=[VMEM] * 5,
        out_specs=(VMEM,) * 4,
        scratch_shapes=[pltpu.VMEM((points, 128), F32)],
        compiler_params=pltpu.CompilerParams(vmem_limit_bytes=16 * 2**20),
        cost_estimate=pl.CostEstimate(flops=10**8, bytes_accessed=10**6, transcendentals=0),
    )(
        modes, localization, point_weight.reshape(1, points), point_modulus.reshape(1, points),
        softening.reshape(1, points),
    )

    force, xface, yface, cface, new_state = pl.pallas_call(
        main_kernel,
        out_shape=(
            shape(3, rows, columns, layers), shape(3, columns, layers), shape(3, rows, layers),
            shape(3, layers), shape(count * most, layers),
        ),
        in_specs=[SMEM] + [VMEM] * 10,
        out_specs=(VMEM,) * 5,
        scratch_shapes=[pltpu.VMEM((rows * columns * 8, layers), F32)] * 2,
        compiler_params=pltpu.CompilerParams(vmem_limit_bytes=40 * 2**20),
        cost_estimate=pl.CostEstimate(flops=10**10, bytes_accessed=10**7, transcendentals=0),
    )(
        cloak_list[0], displacement, xhalo, yhalo, corner, stiffness,
        micro_state.reshape(count * most, layers), first, newton, back_m, stress_m,
    )

    xface = lax.ppermute(xface, "gx", back(along_x))
    yface = lax.ppermute(yface, "gy", back(along_y))
    cface = lax.ppermute(cface, ("gx", "gy"), back(both))

    displacement_next, velocity_next = pl.pallas_call(
        update_kernel,
        out_shape=(shape(3, rows, columns, layers),) * 2,
        in_specs=[VMEM] * 8,
        out_specs=(VMEM,) * 2,
        compiler_params=pltpu.CompilerParams(vmem_limit_bytes=16 * 2**20),
    )(displacement, velocity, external_force, node_mass, force, xface, yface, cface)
    return displacement_next, velocity_next, new_state.reshape(micro_state.shape)


def solution(mesh):
    field = P(None, "gx", "gy", None)
    grid = P("gx", "gy", None)
    state = P("gx", "gy", None, None, None)
    in_specs = (field, field, field, grid, grid, P("gx", None, None), state, P(), P(), P(), P(), P())
    return jax.shard_map(
        on_device, mesh=mesh, in_specs=in_specs, out_specs=(field, field, state), check_vma=False
    )
```

```python
import functools

import jax
import jax.numpy as jnp
from jax import lax
from jax.experimental import pallas as pl
from jax.experimental.pallas import tpu as pltpu
from jax.sharding import PartitionSpec as P

ITERS = 3
STEP = 0.25
HIGHEST = lax.Precision.HIGHEST
F32 = jnp.float32
BF16 = jnp.bfloat16
VMEM = pl.BlockSpec(memory_space=pltpu.VMEM)
HBM = pl.BlockSpec(memory_space=pltpu.HBM)
SMEM = pl.BlockSpec(memory_space=pltpu.SMEM)


def split(x):
    high = x.astype(BF16)
    return high, (x - high.astype(F32)).astype(BF16)


def dot(a, b):
    return jnp.dot(a, b, preferred_element_type=F32)


def exact(a, b):
    return jnp.dot(a, b, precision=HIGHEST, preferred_element_type=F32)


def transposed_product(a, b):
    terms = []
    for x in (a, b):
        one = x.astype(BF16).astype(F32)
        two = (x - one).astype(BF16).astype(F32)
        terms.append((one, two, x - one - two))
    (a1, a2, a3), (b1, b2, b3) = terms
    left = jnp.concatenate([a1, a1, a2, a2, a1, a3], axis=0).astype(BF16)
    right = jnp.concatenate([b1, b2, b1, b2, b3, b1], axis=0).astype(BF16)
    return lax.dot_general(left, right, (((0,), (0,)), ((), ())), preferred_element_type=F32)


def inverse(matrix):
    size = matrix.shape[0]
    tile = (8, size)
    count = size // 8
    blocks = [matrix[i : i + 8] for i in range(0, size, 8)]
    lane = lax.broadcasted_iota(jnp.int32, tile, 1)
    row = lax.broadcasted_iota(jnp.int32, tile, 0)
    for b in range(count):
        before = panel = blocks[b]
        for s in range(0, 8, 2):
            k = b * 8 + s
            c0 = jnp.broadcast_to(panel[:, k : k + 1], tile)
            c1 = jnp.broadcast_to(panel[:, k + 1 : k + 2], tile)
            r0 = jnp.broadcast_to(panel[s : s + 1, :], tile)
            r1 = jnp.broadcast_to(panel[s + 1 : s + 2, :], tile)
            p00 = jnp.broadcast_to(c0[s : s + 1, :], tile)
            p10 = jnp.broadcast_to(c0[s + 1 : s + 2, :], tile)
            p11 = jnp.broadcast_to(c1[s + 1 : s + 2, :], tile)
            scale = 1.0 / (p00 * p11 - p10 * p10)
            q00, q10, q11 = p11 * scale, p10 * scale, p00 * scale
            r0, r1 = q00 * r0 - q10 * r1, q11 * r1 - q10 * r0
            n0 = jnp.where(lane == k, q00, jnp.where(lane == k + 1, -q10, r0))
            n1 = jnp.where(lane == k, -q10, jnp.where(lane == k + 1, q11, r1))
            both = jnp.logical_or(lane == k, lane == k + 1)
            rest = jnp.where(both, 0.0, panel) - c0 * n0 - c1 * n1
            panel = jnp.where(row == s, n0, jnp.where(row == s + 1, n1, rest))
        inside = jnp.logical_and(lane >= b * 8, lane < b * 8 + 8)
        panel = jnp.where(inside, -panel, panel)
        change = transposed_product(before, panel)
        for i in range(count):
            old = blocks[i]
            kept = jnp.where(inside, 0.0, old)
            if i == b:
                blocks[i] = panel
            elif i == b + 1:
                for s in range(8):
                    k = b * 8 + s
                    column = jnp.broadcast_to(old[:, k : k + 1], tile)
                    kept = kept - column * jnp.broadcast_to(panel[s : s + 1, :], tile)
                blocks[i] = kept
            else:
                blocks[i] = kept - change[i * 8 : i * 8 + 8]
    return -jnp.concatenate(blocks, axis=0)


def near(a, b):
    (ah, al), (bh, bl) = split(a), split(b)
    return dot(ah, bh) + dot(al, bh) + dot(ah, bl)


def fetch(sources, targets, sems):
    copies = [
        pltpu.make_async_copy(a, b, sems.at[i]) for i, (a, b) in enumerate(zip(sources, targets))
    ]
    for copy in copies:
        copy.start()
    for copy in copies:
        copy.wait()


def matrices_kernel(
    modes_hbm, local_hbm, weight_hbm, modulus_hbm, soft_hbm,
    start0_ref, start1_ref, high_ref, low_ref, back_ref, stress_ref,
    wide, modes_ref, local_ref, weight_ref, modulus_ref, soft_ref, sems,
):
    fetch(
        (modes_hbm, local_hbm, weight_hbm, modulus_hbm, soft_hbm),
        (modes_ref, local_ref, weight_ref, modulus_ref, soft_ref),
        sems,
    )
    points, count = modes_ref.shape
    modes = modes_ref[...]
    modes_t = modes.T
    weight = weight_ref[...] / points
    modulus = modulus_ref[...]
    root = jnp.sqrt(soft_ref[...])
    scale = weight * modulus / root
    inverted = inverse(exact(modes_t * (weight * modulus), modes))
    wide[...] = jnp.zeros_like(wide)
    wide[0 : local_ref.shape[0], :] = local_ref[...]
    local = wide[...]
    stress_ref[...] = (local * scale).astype(BF16)
    high, low = split(modes_t * root)
    start0_ref[0:count] = high
    start0_ref[count:] = high
    start1_ref[0:count] = low
    soft_local = local[0:8] * root
    local_high = soft_local.astype(BF16).astype(F32)
    part = [local_high, local_high, soft_local - local_high, jnp.zeros_like(local_high)]
    start1_ref[count:] = jnp.concatenate(part * (count // 32), axis=0).astype(BF16)
    back = near((modes_t * scale).T, inverted)
    high, low = split(back)
    back_ref[:, 0:count] = high
    back_ref[:, count:] = low
    newton = near(back, modes_t * root)
    high, low = split(newton)
    high_ref[...] = high
    low_ref[...] = low


def respond(u):
    return u * lax.rsqrt(1.0 + u * u)


def cells(states, strains, start0, start1, newton_high, newton_low, back, stress_m):
    layers = states[0].shape[1]
    count = states[0].shape[0]
    number = len(states)
    part = min(2, number)
    turned = [state.T for state in states]
    place = lax.broadcasted_iota(jnp.int32, (layers, count), 1) // 32
    strain_parts = []
    each = count // 32
    for q in range(0, number, each):
        rows = []
        for strain in strains[q : q + each]:
            high = strain.astype(BF16).astype(F32)
            rows += [high, strain - high, high, jnp.zeros_like(high)]
        rows = jnp.concatenate(rows, axis=0).T
        strain_parts += [jnp.where(place == g, rows, 0.0).astype(BF16) for g in range(each)]
    start = []
    for c in range(0, number, part):
        high, low = split(jnp.concatenate(turned[c : c + part], axis=0))
        strain = jnp.concatenate(strain_parts[c : c + part], axis=0)
        start.append(
            dot(jnp.concatenate([high, low], axis=1), start0)
            + dot(jnp.concatenate([high, strain], axis=1), start1)
        )
    now = start
    for step in range(ITERS - 1):
        later = []
        for u in now:
            high, low = split(respond(u))
            later.append(u - (dot(high, newton_high) + dot(low, newton_high) + dot(high, newton_low)))
        now = later
    last, moved = [], []
    for first, u in zip(start, now):
        h = respond(u)
        last.append(u - dot(h.astype(BF16), newton_high))
        moved.append(split(first - u + h))
    new_states, stresses = [], []
    for c, (high, low) in enumerate(moved):
        both = dot(high, back)
        change = both[:, 0:count] + both[:, count:] + dot(low, back[:, 0:count])
        for g in range(part):
            new_states.append(states[c * part + g] - change[g * layers : (g + 1) * layers].T)
    for u in last:
        stress = lax.dot_general(
            stress_m, respond(u).astype(BF16), (((1,), (1,)), ((), ())), preferred_element_type=F32
        )
        stresses += [stress[0:8, g * layers : (g + 1) * layers] for g in range(part)]
    return new_states, stresses


def pencil_rows(ref, q, g):
    groups, count, group, layers = ref.shape
    place = pl.ds(q * (count * group) + g, count, stride=group)
    return ref.reshape(groups * count * group, layers), place


def get_pencil(ref, q, g):
    flat, place = pencil_rows(ref, q, g)
    return flat[place, :]


def set_pencil(ref, q, g, value):
    flat, place = pencil_rows(ref, q, g)
    flat[place, :] = value


def edges_kernel(disp_hbm, xface_ref, yface_ref, corner_ref, disp_ref, sems):
    fetch((disp_hbm,), (disp_ref,), sems)
    for c in range(3):
        xface_ref[c] = disp_ref[c, 0]
        yface_ref[c] = disp_ref[c, :, 0, :]
        corner_ref[c : c + 1] = disp_ref[c, 0, 0:1]


def main_kernel(
    lists_ref, disp_ref, xhalo_ref, yhalo_ref, corner_ref, stiff_ref, state_hbm,
    start0_ref, start1_ref, high_ref, low_ref, back_ref, stress_ref,
    force_ref, xface_ref, yface_ref, cface_ref, out_hbm,
    strain_s, stress_s, state_s, out_s, in_sems, out_sems,
):
    rows, columns, layers = stiff_ref.shape
    groups, count, group, _ = state_s.shape
    pencils = rows * columns

    def load(q):
        return pltpu.make_async_copy(
            state_hbm.at[:, pl.ds(q * group, group), :], state_s.at[q], in_sems.at[q]
        )

    def store(q):
        return pltpu.make_async_copy(
            out_s.at[q], out_hbm.at[:, pl.ds(q * group, group), :], out_sems.at[q]
        )

    for q in range(groups):
        load(q).start()
    tile = (columns, layers)
    lane = lax.broadcasted_iota(jnp.int32, tile, 1)
    sub = lax.broadcasted_iota(jnp.int32, tile, 0)
    last_lane = lane == layers - 1
    first_lane = lane == 0
    last_sub = sub == columns - 1
    first_sub = sub == 0
    member = lax.axis_index("gy")

    def node_row(c, i):
        own = disp_ref[c, i] if i < rows else xhalo_ref[c]
        edge = yhalo_ref[c, i : i + 1] if i < rows else corner_ref[c : c + 1]
        up = jnp.where(last_sub, jnp.broadcast_to(edge, tile), pltpu.roll(own, columns - 1, 0))
        mean, diff = 0.5 * (up + own), up - own
        mean_up = jnp.where(last_lane, 0.0, pltpu.roll(mean, layers - 1, 1))
        diff_up = jnp.where(last_lane, 0.0, pltpu.roll(diff, layers - 1, 1))
        return 0.5 * (mean_up + mean), 0.5 * (diff_up + diff), mean_up - mean

    lower = [node_row(c, 0) for c in range(3)]
    zero_tile = jnp.zeros(tile, F32)
    for i in range(rows):
        upper = [node_row(c, i + 1) for c in range(3)]
        g = [
            (upper[c][0] - lower[c][0], 0.5 * (upper[c][1] + lower[c][1]), 0.5 * (upper[c][2] + lower[c][2]))
            for c in range(3)
        ]
        lower = upper
        strain = [g[0][0], g[1][1], g[2][2], g[1][2] + g[2][1], g[0][2] + g[2][0], g[0][1] + g[1][0]]
        stiffness = stiff_ref[i]
        volume = strain[0] + strain[1] + strain[2]
        for c in range(8):
            place = pl.ds(i * columns * 8 + c, columns, stride=8)
            if c >= 6:
                strain_s[place, :] = zero_tile
                continue
            strain_s[place, :] = strain[c]
            stress_s[place, :] = stiffness * (volume + 2.0 * strain[c] if c < 3 else strain[c])

    def body(q, carry):
        base = q * group
        load(q).wait()
        busy = lists_ref[member, base] >= 0

        @pl.when(busy)
        def _():
            entries = [lists_ref[member, base + g] for g in range(group)]
            states = [get_pencil(state_s, q, g) for g in range(group)]
            strains = [
                strain_s[pl.ds(pl.multiple_of(jnp.maximum(e, 0) * 8, 8), 8), :] for e in entries
            ]
            new_states, stresses = cells(
                states, strains, start0_ref[...], start1_ref[...], high_ref[...], low_ref[...],
                back_ref[...], stress_ref[...],
            )
            for g in range(group):
                set_pencil(out_s, q, g, jnp.where(entries[g] >= 0, new_states[g], 0.0))
                spot = jnp.where(entries[g] >= 0, entries[g], pencils)
                stress_s[pl.ds(pl.multiple_of(spot * 8, 8), 8), :] = stresses[g]

        @pl.when(jnp.logical_not(busy))
        def _():
            out_s[q] = jnp.zeros((count, group, layers), F32)

        store(q).start()
        return carry

    lax.fori_loop(0, groups, body, 0)

    def fluxes(s, side_mean, side_diff, lane_zero):
        def along(v):
            down = jnp.where(lane_zero, 0.0, pltpu.roll(v, 1, 1))
            return 0.5 * (v + down), v - down

        first = [along(side_mean(s[c]))[0] for c in (0, 5, 4)]
        second = [along(side_diff(s[c]))[0] for c in (5, 1, 3)]
        third = [along(side_mean(s[c]))[1] for c in (4, 3, 2)]
        half = [0.5 * (second[c] + third[c]) for c in range(3)]
        return [(first[c] + half[c], half[c] - first[c]) for c in range(3)]

    def shift(v):
        return jnp.where(first_sub, 0.0, pltpu.roll(v, 1, 0))

    below = None
    for i in range(rows):
        s = [stress_s[pl.ds(i * columns * 8 + c, columns, stride=8), :] for c in range(6)]
        here = fluxes(s, lambda v: 0.5 * (v + shift(v)), lambda v: v - shift(v), first_lane)
        for c in range(3):
            force_ref[c, i] = -here[c][0] if below is None else -(here[c][0] + below[c][1])
        below = here
    for c in range(3):
        xface_ref[c] = -below[c][1]
    s = [stress_s[pl.ds((columns - 1) * 8 + c, rows, stride=columns * 8), :] for c in range(6)]
    wide_zero = lax.broadcasted_iota(jnp.int32, (rows, layers), 1) == 0
    side = fluxes(s, lambda v: 0.5 * v, lambda v: -v, wide_zero)
    for c in range(3):
        yface_ref[c] = -side[c][0]
        yface_ref[c, 1:rows] = yface_ref[c, 1:rows] - side[c][1][0 : rows - 1]
        cface_ref[c : c + 1] = -side[c][1][rows - 1 : rows]
    for q in range(groups):
        store(q).wait()


def update_kernel(
    disp_ref, velocity_ref, external_ref, mass_ref, force_ref, xface_ref, yface_ref, cface_ref,
    disp_out, velocity_out,
):
    rows, columns, layers = mass_ref.shape
    first_sub = lax.broadcasted_iota(jnp.int32, (columns, layers), 0) == 0
    for i in range(rows):
        factor = STEP / mass_ref[i]
        for c in range(3):
            edge = yface_ref[c, i : i + 1]
            if i == 0:
                edge = edge + cface_ref[c : c + 1]
            internal = force_ref[c, i] + jnp.where(
                first_sub, jnp.broadcast_to(edge, (columns, layers)), 0.0
            )
            if i == 0:
                internal = internal + xface_ref[c]
            velocity = velocity_ref[c, i] + factor * (external_ref[c, i] - internal)
            velocity_out[c, i] = velocity
            disp_out[c, i] = disp_ref[c, i] + STEP * velocity


def shape(*dims, dtype=F32):
    return jax.ShapeDtypeStruct(dims, dtype)


def on_device(
    displacement, velocity, external_force, node_mass, stiffness, cloak_list, micro_state,
    localization, modes, point_weight, point_modulus, softening,
):
    rows, columns, layers = stiffness.shape
    points, count = modes.shape
    most = cloak_list.shape[2]
    gx, gy = lax.axis_size("gx"), lax.axis_size("gy")
    along_x = [(i + 1, i) for i in range(gx - 1)]
    along_y = [(i + 1, i) for i in range(gy - 1)]
    both = [((i + 1) * gy + j + 1, i * gy + j) for i in range(gx - 1) for j in range(gy - 1)]
    back = lambda pairs: [(b, a) for a, b in pairs]
    group = 8
    xhalo, yhalo, corner = pl.pallas_call(
        edges_kernel,
        out_shape=(shape(3, columns, layers), shape(3, rows, layers), shape(3, layers)),
        in_specs=[HBM],
        out_specs=(VMEM,) * 3,
        scratch_shapes=[pltpu.VMEM(displacement.shape, F32), pltpu.SemaphoreType.DMA((1,))],
        compiler_params=pltpu.CompilerParams(vmem_limit_bytes=4 * 2**20),
    )(displacement)
    xhalo = lax.ppermute(xhalo, "gx", along_x)
    yhalo = lax.ppermute(yhalo, "gy", along_y)
    corner = lax.ppermute(corner, ("gx", "gy"), both)

    matrices = pl.pallas_call(
        matrices_kernel,
        out_shape=tuple(shape(n, points, dtype=BF16) for n in (2 * count, 2 * count, points, points))
        + (shape(points, 2 * count, dtype=BF16), shape(16, points, dtype=BF16)),
        in_specs=[HBM] * 5,
        out_specs=(VMEM,) * 6,
        scratch_shapes=[
            pltpu.VMEM((16, points), F32), pltpu.VMEM((points, count), F32),
            pltpu.VMEM((localization.shape[1], points), F32),
        ]
        + [pltpu.VMEM((1, points), F32)] * 3
        + [pltpu.SemaphoreType.DMA((5,))],
        compiler_params=pltpu.CompilerParams(vmem_limit_bytes=16 * 2**20),
        cost_estimate=pl.CostEstimate(flops=10**10, bytes_accessed=10**6, transcendentals=0),
    )(
        modes, localization.T, point_weight.reshape(1, points), point_modulus.reshape(1, points),
        softening.reshape(1, points),
    )

    groups = most // group
    force, xface, yface, cface, new_state = pl.pallas_call(
        main_kernel,
        out_shape=(
            shape(3, rows, columns, layers), shape(3, columns, layers), shape(3, rows, layers),
            shape(3, layers), shape(count, most, layers),
        ),
        in_specs=[SMEM] + [VMEM] * 5 + [HBM] + [VMEM] * 6,
        out_specs=(VMEM,) * 4 + (HBM,),
        scratch_shapes=[
            pltpu.VMEM((rows * columns * 8, layers), F32),
            pltpu.VMEM((rows * columns * 8 + 8, layers), F32),
            pltpu.VMEM((groups, count, group, layers), F32),
            pltpu.VMEM((groups, count, group, layers), F32),
            pltpu.SemaphoreType.DMA((groups,)),
            pltpu.SemaphoreType.DMA((groups,)),
        ],
        compiler_params=pltpu.CompilerParams(vmem_limit_bytes=40 * 2**20),
        cost_estimate=pl.CostEstimate(flops=10**10, bytes_accessed=10**7, transcendentals=0),
    )(
        cloak_list[0], displacement, xhalo, yhalo, corner, stiffness,
        micro_state.reshape(count, most, layers), *matrices,
    )

    xface = lax.ppermute(xface, "gx", back(along_x))
    yface = lax.ppermute(yface, "gy", back(along_y))
    cface = lax.ppermute(cface, ("gx", "gy"), back(both))

    displacement_next, velocity_next = pl.pallas_call(
        update_kernel,
        out_shape=(shape(3, rows, columns, layers),) * 2,
        in_specs=[VMEM] * 8,
        out_specs=(VMEM,) * 2,
        compiler_params=pltpu.CompilerParams(vmem_limit_bytes=16 * 2**20),
    )(displacement, velocity, external_force, node_mass, force, xface, yface, cface)
    return displacement_next, velocity_next, new_state.reshape(micro_state.shape)


def solution(mesh):
    field = P(None, "gx", "gy", None)
    grid = P("gx", "gy", None)
    state = P("gx", "gy", None, None, None)
    in_specs = (field, field, field, grid, grid, P("gx", None, None), state, P(), P(), P(), P(), P())
    return jax.shard_map(
        on_device, mesh=mesh, in_specs=in_specs, out_specs=(field, field, state), check_vma=False
    )
```

```python
import functools

import jax
import jax.numpy as jnp
from jax import lax
from jax.experimental import pallas as pl
from jax.experimental.pallas import tpu as pltpu
from jax.sharding import PartitionSpec as P

ITERS = 3
STEP = 0.25
HIGHEST = lax.Precision.HIGHEST
F32 = jnp.float32
BF16 = jnp.bfloat16
GRANT = 60 * 2**20
VMEM = pl.BlockSpec(memory_space=pltpu.VMEM)
HBM = pl.BlockSpec(memory_space=pltpu.HBM)
SMEM = pl.BlockSpec(memory_space=pltpu.SMEM)


def split(x):
    high = x.astype(BF16)
    return high, (x - high.astype(F32)).astype(BF16)


def dot(a, b):
    return jnp.dot(a, b, preferred_element_type=F32)


def exact(a, b):
    return jnp.dot(a, b, precision=HIGHEST, preferred_element_type=F32)


def transposed_product(a, b):
    terms = []
    for x in (a, b):
        one = x.astype(BF16).astype(F32)
        two = (x - one).astype(BF16).astype(F32)
        terms.append((one, two, x - one - two))
    (a1, a2, a3), (b1, b2, b3) = terms
    left = jnp.concatenate([a1, a1, a2, a2, a1, a3], axis=0).astype(BF16)
    right = jnp.concatenate([b1, b2, b1, b2, b3, b1], axis=0).astype(BF16)
    return lax.dot_general(left, right, (((0,), (0,)), ((), ())), preferred_element_type=F32)


def lane_of(x, k):
    return jnp.take_along_axis(x, jnp.full(x.shape, k, jnp.int32), axis=1, mode="promise_in_bounds")


def row_of(x, s):
    return jnp.take_along_axis(x, jnp.full(x.shape, s, jnp.int32), axis=0, mode="promise_in_bounds")


def invert_two(a, b, c):
    scale = 1.0 / (a * c - b * b)
    return c * scale, -(b * scale), a * scale


def inverse(matrix):
    size = matrix.shape[0]
    tile = (8, size)
    count = size // 8
    blocks = [matrix[i : i + 8] for i in range(0, size, 8)]
    lane = lax.broadcasted_iota(jnp.int32, tile, 1)
    row = lax.broadcasted_iota(jnp.int32, tile, 0)

    def spread(x, s):
        return jnp.broadcast_to(x[s : s + 1, :], tile)

    for b in range(count):
        before = panel = blocks[b]
        for s in range(0, 8, 4):
            k = b * 8 + s
            lanes4 = jnp.logical_and(lane >= k, lane < k + 4)
            rows4 = jnp.logical_and(row >= s, row < s + 4)
            c = [lane_of(panel, k + i) for i in range(4)]
            r = [
                jnp.where(lane == k + i, 1.0, jnp.where(lanes4, 0.0, spread(panel, s + i)))
                for i in range(4)
            ]
            p = [[row_of(c[j], s + i) for j in range(i + 1)] for i in range(4)]
            (b00, b01), (b10, b11) = p[2][:2], p[3][:2]
            i00, i10, i11 = invert_two(p[0][0], p[1][0], p[1][1])
            w00, w01 = b00 * i00 + b01 * i10, b00 * i10 + b01 * i11
            w10, w11 = b10 * i00 + b11 * i10, b10 * i10 + b11 * i11
            j00, j10, j11 = invert_two(
                p[2][2] - (w00 * b00 + w01 * b01),
                p[3][2] - (w10 * b00 + w11 * b01),
                p[3][3] - (w10 * b10 + w11 * b11),
            )
            y2 = r[2] - (w00 * r[0] + w01 * r[1])
            y3 = r[3] - (w10 * r[0] + w11 * r[1])
            n2, n3 = j00 * y2 + j10 * y3, j10 * y2 + j11 * y3
            n0 = (i00 * r[0] + i10 * r[1]) - (w00 * n2 + w10 * n3)
            n1 = (i10 * r[0] + i11 * r[1]) - (w01 * n2 + w11 * n3)
            f = [jnp.where(row == s + i, -1.0, jnp.where(rows4, 0.0, c[i])) for i in range(4)]
            rest = jnp.where(jnp.logical_or(lanes4, rows4), 0.0, panel)
            panel = rest - ((f[0] * n0 + f[1] * n1) + (f[2] * n2 + f[3] * n3))
        inside = jnp.logical_and(lane >= b * 8, lane < b * 8 + 8)
        panel = jnp.where(inside, -panel, panel)
        change = transposed_product(before, panel)
        for i in range(count):
            old = blocks[i]
            kept = jnp.where(inside, 0.0, old)
            if i == b:
                blocks[i] = panel
            elif i == b + 1:
                t = [lane_of(old, b * 8 + s) * spread(panel, s) for s in range(8)]
                blocks[i] = kept - (((t[0] + t[1]) + (t[2] + t[3])) + ((t[4] + t[5]) + (t[6] + t[7])))
            else:
                blocks[i] = kept - change[i * 8 : i * 8 + 8]
    return -jnp.concatenate(blocks, axis=0)


def near(a, b):
    (ah, al), (bh, bl) = split(a), split(b)
    return dot(ah, bh) + dot(al, bh) + dot(ah, bl)


def fetch(sources, targets, sems):
    copies = [
        pltpu.make_async_copy(a, b, sems.at[i]) for i, (a, b) in enumerate(zip(sources, targets))
    ]
    for copy in copies:
        copy.start()
    for copy in copies:
        copy.wait()


def matrices_kernel(
    modes_hbm, local_hbm, weight_hbm, modulus_hbm, soft_hbm,
    start0_ref, start1_ref, high_ref, low_ref, back_ref, stress_ref,
    wide, modes_ref, local_ref, weight_ref, modulus_ref, soft_ref, sems,
):
    fetch(
        (modes_hbm, local_hbm, weight_hbm, modulus_hbm, soft_hbm),
        (modes_ref, local_ref, weight_ref, modulus_ref, soft_ref),
        sems,
    )
    points, count = modes_ref.shape
    modes = modes_ref[...]
    modes_t = modes.T
    weight = weight_ref[...] / points
    modulus = modulus_ref[...]
    root = jnp.sqrt(soft_ref[...])
    scale = weight * modulus / root
    inverted = inverse(exact(modes_t * (weight * modulus), modes))
    wide[...] = jnp.zeros_like(wide)
    wide[0 : local_ref.shape[0], :] = local_ref[...]
    local = wide[...]
    stress_ref[...] = (local * scale).astype(BF16)
    high, low = split(modes_t * root)
    start0_ref[0:count] = high
    start0_ref[count:] = high
    start1_ref[0:count] = low
    soft_local = local[0:8] * root
    local_high = soft_local.astype(BF16).astype(F32)
    part = [local_high, local_high, soft_local - local_high, jnp.zeros_like(local_high)]
    start1_ref[count:] = jnp.concatenate(part * (count // 32), axis=0).astype(BF16)
    back = near((modes_t * scale).T, inverted)
    high, low = split(back)
    back_ref[:, 0:count] = high
    back_ref[:, count:] = low
    newton = near(back, modes_t * root)
    high, low = split(newton)
    high_ref[...] = high
    low_ref[...] = low


def respond(u):
    return u * lax.rsqrt(1.0 + u * u)


def cells(states, strains, start0, start1, newton_high, newton_low, back, stress_m):
    layers = states[0].shape[1]
    count = states[0].shape[0]
    number = len(states)
    part = min(2, number)
    turned = [state.T for state in states]
    place = lax.broadcasted_iota(jnp.int32, (layers, count), 1) // 32
    strain_parts = []
    each = count // 32
    for q in range(0, number, each):
        rows = []
        for strain in strains[q : q + each]:
            high = strain.astype(BF16).astype(F32)
            rows += [high, strain - high, high, jnp.zeros_like(high)]
        rows = jnp.concatenate(rows, axis=0).T
        strain_parts += [jnp.where(place == g, rows, 0.0).astype(BF16) for g in range(each)]
    start = []
    for c in range(0, number, part):
        high, low = split(jnp.concatenate(turned[c : c + part], axis=0))
        strain = jnp.concatenate(strain_parts[c : c + part], axis=0)
        start.append(
            dot(jnp.concatenate([high, low], axis=1), start0)
            + dot(jnp.concatenate([high, strain], axis=1), start1)
        )
    now = start
    for step in range(ITERS - 1):
        later = []
        for u in now:
            high, low = split(respond(u))
            later.append(u - (dot(high, newton_high) + dot(low, newton_high) + dot(high, newton_low)))
        now = later
    last, moved = [], []
    for first, u in zip(start, now):
        h = respond(u)
        last.append(u - dot(h.astype(BF16), newton_high))
        moved.append(split(first - u + h))
    new_states, stresses = [], []
    for c, (high, low) in enumerate(moved):
        both = dot(high, back)
        change = both[:, 0:count] + both[:, count:] + dot(low, back[:, 0:count])
        for g in range(part):
            new_states.append(states[c * part + g] - change[g * layers : (g + 1) * layers].T)
    for u in last:
        stress = lax.dot_general(
            stress_m, respond(u).astype(BF16), (((1,), (1,)), ((), ())), preferred_element_type=F32
        )
        stresses += [stress[0:8, g * layers : (g + 1) * layers] for g in range(part)]
    return new_states, stresses


def pencil_rows(ref, q, g):
    groups, count, group, layers = ref.shape
    place = pl.ds(q * (count * group) + g, count, stride=group)
    return ref.reshape(groups * count * group, layers), place


def get_pencil(ref, q, g):
    flat, place = pencil_rows(ref, q, g)
    return flat[place, :]


def set_pencil(ref, q, g, value):
    flat, place = pencil_rows(ref, q, g)
    flat[place, :] = value


def edges_kernel(disp_hbm, xface_ref, yface_ref, corner_ref, disp_ref, sems):
    fetch((disp_hbm,), (disp_ref,), sems)
    for c in range(3):
        xface_ref[c] = disp_ref[c, 0]
        yface_ref[c] = disp_ref[c, :, 0, :]
        corner_ref[c : c + 1] = disp_ref[c, 0, 0:1]


def main_kernel(
    lists_ref, disp_ref, xhalo_ref, yhalo_ref, corner_ref, stiff_ref, state_hbm,
    start0_ref, start1_ref, high_ref, low_ref, back_ref, stress_ref,
    force_ref, xface_ref, yface_ref, cface_ref, out_hbm,
    strain_s, stress_s, state_s, out_s, in_sems, out_sems,
):
    rows, columns, layers = stiff_ref.shape
    groups, count, group, _ = state_s.shape
    pencils = rows * columns

    def load(q):
        return pltpu.make_async_copy(
            state_hbm.at[:, pl.ds(q * group, group), :], state_s.at[q], in_sems.at[q]
        )

    def store(q):
        return pltpu.make_async_copy(
            out_s.at[q], out_hbm.at[:, pl.ds(q * group, group), :], out_sems.at[q]
        )

    for q in range(groups):
        load(q).start()
    tile = (columns, layers)
    lane = lax.broadcasted_iota(jnp.int32, tile, 1)
    sub = lax.broadcasted_iota(jnp.int32, tile, 0)
    last_lane = lane == layers - 1
    first_lane = lane == 0
    last_sub = sub == columns - 1
    first_sub = sub == 0
    member = lax.axis_index("gy")

    def node_row(c, i):
        own = disp_ref[c, i] if i < rows else xhalo_ref[c]
        edge = yhalo_ref[c, i : i + 1] if i < rows else corner_ref[c : c + 1]
        up = jnp.where(last_sub, jnp.broadcast_to(edge, tile), pltpu.roll(own, columns - 1, 0))
        mean, diff = 0.5 * (up + own), up - own
        mean_up = jnp.where(last_lane, 0.0, pltpu.roll(mean, layers - 1, 1))
        diff_up = jnp.where(last_lane, 0.0, pltpu.roll(diff, layers - 1, 1))
        return 0.5 * (mean_up + mean), 0.5 * (diff_up + diff), mean_up - mean

    lower = [node_row(c, 0) for c in range(3)]
    zero_tile = jnp.zeros(tile, F32)
    for i in range(rows):
        upper = [node_row(c, i + 1) for c in range(3)]
        g = [
            (upper[c][0] - lower[c][0], 0.5 * (upper[c][1] + lower[c][1]), 0.5 * (upper[c][2] + lower[c][2]))
            for c in range(3)
        ]
        lower = upper
        strain = [g[0][0], g[1][1], g[2][2], g[1][2] + g[2][1], g[0][2] + g[2][0], g[0][1] + g[1][0]]
        stiffness = stiff_ref[i]
        volume = strain[0] + strain[1] + strain[2]
        for c in range(8):
            place = pl.ds(i * columns * 8 + c, columns, stride=8)
            if c >= 6:
                strain_s[place, :] = zero_tile
                continue
            strain_s[place, :] = strain[c]
            stress_s[place, :] = stiffness * (volume + 2.0 * strain[c] if c < 3 else strain[c])

    def body(q, carry):
        base = q * group
        load(q).wait()
        busy = lists_ref[member, base] >= 0

        @pl.when(busy)
        def _():
            entries = [lists_ref[member, base + g] for g in range(group)]
            states = [get_pencil(state_s, q, g) for g in range(group)]
            strains = [
                strain_s[pl.ds(pl.multiple_of(jnp.maximum(e, 0) * 8, 8), 8), :] for e in entries
            ]
            new_states, stresses = cells(
                states, strains, start0_ref[...], start1_ref[...], high_ref[...], low_ref[...],
                back_ref[...], stress_ref[...],
            )
            for g in range(group):
                set_pencil(out_s, q, g, jnp.where(entries[g] >= 0, new_states[g], 0.0))
                spot = jnp.where(entries[g] >= 0, entries[g], pencils)
                stress_s[pl.ds(pl.multiple_of(spot * 8, 8), 8), :] = stresses[g]

        @pl.when(jnp.logical_not(busy))
        def _():
            out_s[q] = jnp.zeros((count, group, layers), F32)

        store(q).start()
        return carry

    lax.fori_loop(0, groups, body, 0)

    def fluxes(s, side_mean, side_diff, lane_zero):
        def along(v):
            down = jnp.where(lane_zero, 0.0, pltpu.roll(v, 1, 1))
            return 0.5 * (v + down), v - down

        first = [along(side_mean(s[c]))[0] for c in (0, 5, 4)]
        second = [along(side_diff(s[c]))[0] for c in (5, 1, 3)]
        third = [along(side_mean(s[c]))[1] for c in (4, 3, 2)]
        half = [0.5 * (second[c] + third[c]) for c in range(3)]
        return [(first[c] + half[c], half[c] - first[c]) for c in range(3)]

    def shift(v):
        return jnp.where(first_sub, 0.0, pltpu.roll(v, 1, 0))

    below = None
    for i in range(rows):
        s = [stress_s[pl.ds(i * columns * 8 + c, columns, stride=8), :] for c in range(6)]
        here = fluxes(s, lambda v: 0.5 * (v + shift(v)), lambda v: v - shift(v), first_lane)
        for c in range(3):
            force_ref[c, i] = -here[c][0] if below is None else -(here[c][0] + below[c][1])
        below = here
    for c in range(3):
        xface_ref[c] = -below[c][1]
    s = [stress_s[pl.ds((columns - 1) * 8 + c, rows, stride=columns * 8), :] for c in range(6)]
    wide_zero = lax.broadcasted_iota(jnp.int32, (rows, layers), 1) == 0
    side = fluxes(s, lambda v: 0.5 * v, lambda v: -v, wide_zero)
    for c in range(3):
        yface_ref[c] = -side[c][0]
        yface_ref[c, 1:rows] = yface_ref[c, 1:rows] - side[c][1][0 : rows - 1]
        cface_ref[c : c + 1] = -side[c][1][rows - 1 : rows]
    for q in range(groups):
        store(q).wait()


def update_kernel(
    disp_ref, velocity_ref, external_ref, mass_ref, force_ref, xface_ref, yface_ref, cface_ref,
    disp_out, velocity_out,
):
    rows, columns, layers = mass_ref.shape
    first_sub = lax.broadcasted_iota(jnp.int32, (columns, layers), 0) == 0
    for i in range(rows):
        factor = STEP / mass_ref[i]
        for c in range(3):
            edge = yface_ref[c, i : i + 1]
            if i == 0:
                edge = edge + cface_ref[c : c + 1]
            internal = force_ref[c, i] + jnp.where(
                first_sub, jnp.broadcast_to(edge, (columns, layers)), 0.0
            )
            if i == 0:
                internal = internal + xface_ref[c]
            velocity = velocity_ref[c, i] + factor * (external_ref[c, i] - internal)
            velocity_out[c, i] = velocity
            disp_out[c, i] = disp_ref[c, i] + STEP * velocity


def shape(*dims, dtype=F32):
    return jax.ShapeDtypeStruct(dims, dtype)


def on_device(
    displacement, velocity, external_force, node_mass, stiffness, cloak_list, micro_state,
    localization, modes, point_weight, point_modulus, softening,
):
    rows, columns, layers = stiffness.shape
    points, count = modes.shape
    most = cloak_list.shape[2]
    gx, gy = lax.axis_size("gx"), lax.axis_size("gy")
    along_x = [(i + 1, i) for i in range(gx - 1)]
    along_y = [(i + 1, i) for i in range(gy - 1)]
    both = [((i + 1) * gy + j + 1, i * gy + j) for i in range(gx - 1) for j in range(gy - 1)]
    back = lambda pairs: [(b, a) for a, b in pairs]
    group = 8
    xhalo, yhalo, corner = pl.pallas_call(
        edges_kernel,
        out_shape=(shape(3, columns, layers), shape(3, rows, layers), shape(3, layers)),
        in_specs=[HBM],
        out_specs=(VMEM,) * 3,
        scratch_shapes=[pltpu.VMEM(displacement.shape, F32), pltpu.SemaphoreType.DMA((1,))],
        compiler_params=pltpu.CompilerParams(vmem_limit_bytes=GRANT),
        cost_estimate=pl.CostEstimate(flops=10**10, bytes_accessed=10**6, transcendentals=0),
    )(displacement)
    xhalo = lax.ppermute(xhalo, "gx", along_x)
    yhalo = lax.ppermute(yhalo, "gy", along_y)
    corner = lax.ppermute(corner, ("gx", "gy"), both)

    matrices = pl.pallas_call(
        matrices_kernel,
        out_shape=tuple(shape(n, points, dtype=BF16) for n in (2 * count, 2 * count, points, points))
        + (shape(points, 2 * count, dtype=BF16), shape(16, points, dtype=BF16)),
        in_specs=[HBM] * 5,
        out_specs=(VMEM,) * 6,
        scratch_shapes=[
            pltpu.VMEM((16, points), F32), pltpu.VMEM((points, count), F32),
            pltpu.VMEM((localization.shape[1], points), F32),
        ]
        + [pltpu.VMEM((1, points), F32)] * 3
        + [pltpu.SemaphoreType.DMA((5,))],
        compiler_params=pltpu.CompilerParams(vmem_limit_bytes=16 * 2**20),
        cost_estimate=pl.CostEstimate(flops=10**10, bytes_accessed=10**6, transcendentals=0),
    )(
        modes, localization.T, point_weight.reshape(1, points), point_modulus.reshape(1, points),
        softening.reshape(1, points),
    )

    groups = most // group
    force, xface, yface, cface, new_state = pl.pallas_call(
        main_kernel,
        out_shape=(
            shape(3, rows, columns, layers), shape(3, columns, layers), shape(3, rows, layers),
            shape(3, layers), shape(count, most, layers),
        ),
        in_specs=[SMEM] + [VMEM] * 5 + [HBM] + [VMEM] * 6,
        out_specs=(VMEM,) * 4 + (HBM,),
        scratch_shapes=[
            pltpu.VMEM((rows * columns * 8, layers), F32),
            pltpu.VMEM((rows * columns * 8 + 8, layers), F32),
            pltpu.VMEM((groups, count, group, layers), F32),
            pltpu.VMEM((groups, count, group, layers), F32),
            pltpu.SemaphoreType.DMA((groups,)),
            pltpu.SemaphoreType.DMA((groups,)),
        ],
        compiler_params=pltpu.CompilerParams(vmem_limit_bytes=40 * 2**20),
        cost_estimate=pl.CostEstimate(flops=10**10, bytes_accessed=10**7, transcendentals=0),
    )(
        cloak_list[0], displacement, xhalo, yhalo, corner, stiffness,
        micro_state.reshape(count, most, layers), *matrices,
    )

    xface = lax.ppermute(xface, "gx", back(along_x))
    yface = lax.ppermute(yface, "gy", back(along_y))
    cface = lax.ppermute(cface, ("gx", "gy"), back(both))

    displacement_next, velocity_next = pl.pallas_call(
        update_kernel,
        out_shape=(shape(3, rows, columns, layers),) * 2,
        in_specs=[VMEM] * 8,
        out_specs=(VMEM,) * 2,
        compiler_params=pltpu.CompilerParams(vmem_limit_bytes=16 * 2**20),
    )(displacement, velocity, external_force, node_mass, force, xface, yface, cface)
    return displacement_next, velocity_next, new_state.reshape(micro_state.shape)


def solution(mesh):
    field = P(None, "gx", "gy", None)
    grid = P("gx", "gy", None)
    state = P("gx", "gy", None, None, None)
    in_specs = (field, field, field, grid, grid, P("gx", None, None), state, P(), P(), P(), P(), P())
    return jax.shard_map(
        on_device, mesh=mesh, in_specs=in_specs, out_specs=(field, field, state), check_vma=False
    )
```

```python
import functools

import jax
import jax.numpy as jnp
from jax import lax
from jax.experimental import pallas as pl
from jax.experimental.pallas import tpu as pltpu
from jax.sharding import PartitionSpec as P

ITERS = 3
STEP = 0.25
HIGHEST = lax.Precision.HIGHEST
F32 = jnp.float32
BF16 = jnp.bfloat16
GRANT = 60 * 2**20
VMEM = pl.BlockSpec(memory_space=pltpu.VMEM)
HBM = pl.BlockSpec(memory_space=pltpu.HBM)
SMEM = pl.BlockSpec(memory_space=pltpu.SMEM)


def split(x):
    high = x.astype(BF16)
    return high, (x - high.astype(F32)).astype(BF16)


def dot(a, b):
    return jnp.dot(a, b, preferred_element_type=F32)


def exact(a, b):
    return jnp.dot(a, b, precision=HIGHEST, preferred_element_type=F32)


def transposed_product(a, b):
    terms = []
    for x in (a, b):
        one = x.astype(BF16).astype(F32)
        two = (x - one).astype(BF16).astype(F32)
        terms.append((one, two, x - one - two))
    (a1, a2, a3), (b1, b2, b3) = terms
    left = jnp.concatenate([a1, a1, a2, a2, a1, a3], axis=0).astype(BF16)
    right = jnp.concatenate([b1, b2, b1, b2, b3, b1], axis=0).astype(BF16)
    return lax.dot_general(left, right, (((0,), (0,)), ((), ())), preferred_element_type=F32)


def lane_of(x, k):
    return jnp.take_along_axis(x, jnp.full(x.shape, k, jnp.int32), axis=1, mode="promise_in_bounds")


def row_of(x, s):
    return jnp.take_along_axis(x, jnp.full(x.shape, s, jnp.int32), axis=0, mode="promise_in_bounds")


def invert_two(a, b, c):
    scale = 1.0 / (a * c - b * b)
    return c * scale, -(b * scale), a * scale


def inverse(matrix):
    size = matrix.shape[0]
    tile = (8, size)
    count = size // 8
    blocks = [matrix[i : i + 8] for i in range(0, size, 8)]
    lane = lax.broadcasted_iota(jnp.int32, tile, 1)
    row = lax.broadcasted_iota(jnp.int32, tile, 0)

    def spread(x, s):
        return jnp.broadcast_to(x[s : s + 1, :], tile)

    for b in range(count):
        before = panel = blocks[b]
        for s in range(0, 8, 4):
            k = b * 8 + s
            lanes4 = jnp.logical_and(lane >= k, lane < k + 4)
            rows4 = jnp.logical_and(row >= s, row < s + 4)
            c = [lane_of(panel, k + i) for i in range(4)]
            r = [
                jnp.where(lane == k + i, 1.0, jnp.where(lanes4, 0.0, spread(panel, s + i)))
                for i in range(4)
            ]
            p = [[row_of(c[j], s + i) for j in range(i + 1)] for i in range(4)]
            (b00, b01), (b10, b11) = p[2][:2], p[3][:2]
            i00, i10, i11 = invert_two(p[0][0], p[1][0], p[1][1])
            w00, w01 = b00 * i00 + b01 * i10, b00 * i10 + b01 * i11
            w10, w11 = b10 * i00 + b11 * i10, b10 * i10 + b11 * i11
            j00, j10, j11 = invert_two(
                p[2][2] - (w00 * b00 + w01 * b01),
                p[3][2] - (w10 * b00 + w11 * b01),
                p[3][3] - (w10 * b10 + w11 * b11),
            )
            y2 = r[2] - (w00 * r[0] + w01 * r[1])
            y3 = r[3] - (w10 * r[0] + w11 * r[1])
            n2, n3 = j00 * y2 + j10 * y3, j10 * y2 + j11 * y3
            n0 = (i00 * r[0] + i10 * r[1]) - (w00 * n2 + w10 * n3)
            n1 = (i10 * r[0] + i11 * r[1]) - (w01 * n2 + w11 * n3)
            f = [jnp.where(row == s + i, -1.0, jnp.where(rows4, 0.0, c[i])) for i in range(4)]
            rest = jnp.where(jnp.logical_or(lanes4, rows4), 0.0, panel)
            panel = rest - ((f[0] * n0 + f[1] * n1) + (f[2] * n2 + f[3] * n3))
        inside = jnp.logical_and(lane >= b * 8, lane < b * 8 + 8)
        panel = jnp.where(inside, -panel, panel)
        change = transposed_product(before, panel)
        for i in range(count):
            old = blocks[i]
            kept = jnp.where(inside, 0.0, old)
            if i == b:
                blocks[i] = panel
            elif i == b + 1:
                t = [lane_of(old, b * 8 + s) * spread(panel, s) for s in range(8)]
                blocks[i] = kept - (((t[0] + t[1]) + (t[2] + t[3])) + ((t[4] + t[5]) + (t[6] + t[7])))
            else:
                blocks[i] = kept - change[i * 8 : i * 8 + 8]
    return -jnp.concatenate(blocks, axis=0)


def near(a, b):
    (ah, al), (bh, bl) = split(a), split(b)
    return dot(ah, bh) + dot(al, bh) + dot(ah, bl)


def fetch(sources, targets, sems):
    copies = [
        pltpu.make_async_copy(a, b, sems.at[i]) for i, (a, b) in enumerate(zip(sources, targets))
    ]
    for copy in copies:
        copy.start()
    for copy in copies:
        copy.wait()


def order_entries(rows, columns, lists_ref, order_ref):
    member = lax.axis_index("gy")
    most = lists_ref.shape[1]
    pencils = [lists_ref[member, e] for e in range(most)]
    listed = [(p >= 0).astype(jnp.int32) for p in pencils]
    edge = [
        jnp.logical_or(p >= (rows - 1) * columns, lax.rem(p, columns) == columns - 1).astype(jnp.int32)
        for p in pencils
    ]
    edges, number = sum(edge), sum(listed)
    next_edge, next_inner, next_rest = 0, edges, number
    for e in range(most):
        inner = listed[e] - edge[e]
        place = jnp.where(edge[e] > 0, next_edge, jnp.where(inner > 0, next_inner, next_rest))
        order_ref[0, place] = e
        order_ref[1, place] = pencils[e]
        next_edge = next_edge + edge[e]
        next_inner = next_inner + inner
        next_rest = next_rest + (1 - listed[e])
    order_ref[0, most] = edges
    order_ref[0, most + 1] = number


def matrices_kernel(
    rows, columns,
    modes_hbm, local_hbm, weight_hbm, modulus_hbm, soft_hbm, lists_ref,
    start0_ref, start1_ref, high_ref, low_ref, back_ref, stress_ref, order_ref,
    wide, modes_ref, local_ref, weight_ref, modulus_ref, soft_ref, sems,
):
    fetch(
        (modes_hbm, local_hbm, weight_hbm, modulus_hbm, soft_hbm),
        (modes_ref, local_ref, weight_ref, modulus_ref, soft_ref),
        sems,
    )
    points, count = modes_ref.shape
    order_entries(rows, columns, lists_ref, order_ref)
    modes = modes_ref[...]
    modes_t = modes.T
    weight = weight_ref[...] / points
    modulus = modulus_ref[...]
    root = jnp.sqrt(soft_ref[...])
    scale = weight * modulus / root
    inverted = inverse(exact(modes_t * (weight * modulus), modes))
    wide[...] = jnp.zeros_like(wide)
    wide[0 : local_ref.shape[0], :] = local_ref[...]
    local = wide[...]
    stress_ref[...] = (local * scale).astype(BF16)
    high, low = split(modes_t * root)
    start0_ref[0:count] = high
    start0_ref[count:] = high
    start1_ref[0:count] = low
    soft_local = local[0:8] * root
    local_high = soft_local.astype(BF16).astype(F32)
    part = [local_high, local_high, soft_local - local_high, jnp.zeros_like(local_high)]
    start1_ref[count:] = jnp.concatenate(part * (count // 32), axis=0).astype(BF16)
    back = near((modes_t * scale).T, inverted)
    high, low = split(back)
    back_ref[:, 0:count] = high
    back_ref[:, count:] = low
    newton = near(back, modes_t * root)
    high, low = split(newton)
    high_ref[...] = high
    low_ref[...] = low


def respond(u):
    return u * lax.rsqrt(1.0 + u * u)


def cells(states, strains, start0, start1, newton_high, newton_low, back, stress_m):
    layers = states[0].shape[1]
    count = states[0].shape[0]
    number = len(states)
    part = min(2, number)
    turned = [state.T for state in states]
    place = lax.broadcasted_iota(jnp.int32, (layers, count), 1) // 32
    strain_parts = []
    each = count // 32
    for q in range(0, number, each):
        rows = []
        for strain in strains[q : q + each]:
            high = strain.astype(BF16).astype(F32)
            rows += [high, strain - high, high, jnp.zeros_like(high)]
        rows = jnp.concatenate(rows, axis=0).T
        strain_parts += [jnp.where(place == g, rows, 0.0).astype(BF16) for g in range(each)]
    start = []
    for c in range(0, number, part):
        high, low = split(jnp.concatenate(turned[c : c + part], axis=0))
        strain = jnp.concatenate(strain_parts[c : c + part], axis=0)
        start.append(
            dot(jnp.concatenate([high, low], axis=1), start0)
            + dot(jnp.concatenate([high, strain], axis=1), start1)
        )
    now = start
    for step in range(ITERS - 1):
        later = []
        for u in now:
            high, low = split(respond(u))
            later.append(u - (dot(high, newton_high) + dot(low, newton_high) + dot(high, newton_low)))
        now = later
    last, moved = [], []
    for first, u in zip(start, now):
        h = respond(u)
        last.append(u - dot(h.astype(BF16), newton_high))
        moved.append(split(first - u + h))
    new_states, stresses = [], []
    for c, (high, low) in enumerate(moved):
        both = dot(high, back)
        change = both[:, 0:count] + both[:, count:] + dot(low, back[:, 0:count])
        for g in range(part):
            new_states.append(states[c * part + g] - change[g * layers : (g + 1) * layers].T)
    for u in last:
        stress = lax.dot_general(
            stress_m, respond(u).astype(BF16), (((1,), (1,)), ((), ())), preferred_element_type=F32
        )
        stresses += [stress[0:8, g * layers : (g + 1) * layers] for g in range(part)]
    return new_states, stresses


def set_pencil(ref, entry, value):
    groups, count, group, layers = ref.shape
    place = lax.div(entry, group) * (count * group) + lax.rem(entry, group)
    ref.reshape(groups * count * group, layers)[pl.ds(place, count, stride=group), :] = value


def run_group(base, group, order_ref, state_ref, strain_ref, weights, stress_s, spare):
    count = weights[4].shape[1] // 2
    most = state_ref.shape[0] // count
    entries = [order_ref[0, base + g] for g in range(group)]
    pencils = [order_ref[1, base + g] for g in range(group)]
    states = [state_ref[pl.ds(e, count, stride=most), :] for e in entries]
    strains = [
        strain_ref[pl.ds(pl.multiple_of(jnp.maximum(p, 0) * 8, 8), 8), :] for p in pencils
    ]
    new_states, stresses = cells(states, strains, *(w[...] for w in weights))
    for g in range(group):
        spot = jnp.where(pencils[g] >= 0, pencils[g], spare)
        stress_s[pl.ds(pl.multiple_of(spot * 8, 8), 8), :] = stresses[g]
    return entries, [jnp.where(p >= 0, a, 0.0) for p, a in zip(pencils, new_states)]


def fluxes(s, side_mean, side_diff):
    lane_zero = lax.broadcasted_iota(jnp.int32, s[0].shape, 1) == 0

    def along(v):
        down = jnp.where(lane_zero, 0.0, pltpu.roll(v, 1, 1))
        return 0.5 * (v + down), v - down

    first = [along(side_mean(s[c]))[0] for c in (0, 5, 4)]
    second = [along(side_diff(s[c]))[0] for c in (5, 1, 3)]
    third = [along(side_mean(s[c]))[1] for c in (4, 3, 2)]
    half = [0.5 * (second[c] + third[c]) for c in range(3)]
    return [(first[c] + half[c], half[c] - first[c]) for c in range(3)]


def row_fluxes(stress_ref, i, columns):
    s = [stress_ref[pl.ds(i * columns * 8 + c, columns, stride=8), :] for c in range(6)]
    first_sub = lax.broadcasted_iota(jnp.int32, s[0].shape, 0) == 0

    def shift(v):
        return jnp.where(first_sub, 0.0, pltpu.roll(v, 1, 0))

    return fluxes(s, lambda v: 0.5 * (v + shift(v)), lambda v: v - shift(v))


def first_groups(order_ref, most, group):
    return lax.div(order_ref[0, most] + (group - 1), group)


def edges_kernel(disp_hbm, xface_ref, yface_ref, corner_ref, disp_ref, sems):
    fetch((disp_hbm,), (disp_ref,), sems)
    for c in range(3):
        xface_ref[c] = disp_ref[c, 0]
        yface_ref[c] = disp_ref[c, :, 0, :]
        corner_ref[c : c + 1] = disp_ref[c, 0, 0:1]


def edge_kernel(
    group, order_ref, disp_ref, xhalo_ref, yhalo_ref, corner_ref, stiff_ref, state_ref,
    start0_ref, start1_ref, high_ref, low_ref, back_ref, stress_ref,
    xface_ref, yface_ref, cface_ref, strain_ref, stress_out, done_ref,
):
    rows, columns, layers = stiff_ref.shape
    most = order_ref.shape[1] - 2
    count = state_ref.shape[0] // most
    weights = (start0_ref, start1_ref, high_ref, low_ref, back_ref, stress_ref)
    tile = (columns, layers)
    lane = lax.broadcasted_iota(jnp.int32, tile, 1)
    sub = lax.broadcasted_iota(jnp.int32, tile, 0)
    last_lane = lane == layers - 1
    last_sub = sub == columns - 1

    def node_row(c, i):
        own = disp_ref[c, i] if i < rows else xhalo_ref[c]
        edge = yhalo_ref[c, i : i + 1] if i < rows else corner_ref[c : c + 1]
        up = jnp.where(last_sub, jnp.broadcast_to(edge, tile), pltpu.roll(own, columns - 1, 0))
        mean, diff = 0.5 * (up + own), up - own
        mean_up = jnp.where(last_lane, 0.0, pltpu.roll(mean, layers - 1, 1))
        diff_up = jnp.where(last_lane, 0.0, pltpu.roll(diff, layers - 1, 1))
        return 0.5 * (mean_up + mean), 0.5 * (diff_up + diff), mean_up - mean

    lower = [node_row(c, 0) for c in range(3)]
    zero_tile = jnp.zeros(tile, F32)
    for i in range(rows):
        upper = [node_row(c, i + 1) for c in range(3)]
        g = [
            (upper[c][0] - lower[c][0], 0.5 * (upper[c][1] + lower[c][1]), 0.5 * (upper[c][2] + lower[c][2]))
            for c in range(3)
        ]
        lower = upper
        strain = [g[0][0], g[1][1], g[2][2], g[1][2] + g[2][1], g[0][2] + g[2][0], g[0][1] + g[1][0]]
        stiffness = stiff_ref[i]
        volume = strain[0] + strain[1] + strain[2]
        for c in range(8):
            place = pl.ds(i * columns * 8 + c, columns, stride=8)
            if c >= 6:
                strain_ref[place, :] = zero_tile
                continue
            strain_ref[place, :] = strain[c]
            stress_out[place, :] = stiffness * (volume + 2.0 * strain[c] if c < 3 else strain[c])

    def body(q, carry):
        _, states = run_group(
            q * group, group, order_ref, state_ref, strain_ref, weights, stress_out, rows * columns
        )
        for g in range(group):
            done_ref[pl.ds(pl.multiple_of((q * group + g) * count, count), count), :] = states[g]
        return carry

    lax.fori_loop(0, first_groups(order_ref, most, group), body, 0)

    last = row_fluxes(stress_out, rows - 1, columns)
    for c in range(3):
        xface_ref[c] = -last[c][1]
    s = [stress_out[pl.ds((columns - 1) * 8 + c, rows, stride=columns * 8), :] for c in range(6)]
    side = fluxes(s, lambda v: 0.5 * v, lambda v: -v)
    for c in range(3):
        yface_ref[c] = -side[c][0]
        yface_ref[c, 1:rows] = yface_ref[c, 1:rows] - side[c][1][0 : rows - 1]
        cface_ref[c : c + 1] = -side[c][1][rows - 1 : rows]


def inner_kernel(
    rows, columns, order_ref, state_ref, strain_ref, stress_in, done_ref,
    start0_ref, start1_ref, high_ref, low_ref, back_ref, stress_ref,
    force_ref, out_hbm,
    stress_s, out_s, sems,
):
    groups, count, group, layers = out_s.shape
    most = groups * group
    weights = (start0_ref, start1_ref, high_ref, low_ref, back_ref, stress_ref)
    before = first_groups(order_ref, most, group)
    after = lax.div(order_ref[0, most + 1] + (group - 1), group)
    stress_s[...] = stress_in[...]

    def store(q):
        return pltpu.make_async_copy(
            out_s.at[q], out_hbm.at[:, pl.ds(q * group, group), :], sems.at[q]
        )

    def copy(q, carry):
        for g in range(group):
            place = q * group + g
            set_pencil(
                out_s, order_ref[0, place],
                done_ref[pl.ds(pl.multiple_of(place * count, count), count), :],
            )
        return carry

    def clear(q, carry):
        for g in range(group):
            set_pencil(out_s, order_ref[0, q * group + g], jnp.zeros((count, layers), F32))
        return carry

    lax.fori_loop(0, before, copy, 0)
    lax.fori_loop(jnp.maximum(before, after), groups, clear, 0)

    def body(q, sent):
        entries, states = run_group(
            q * group, group, order_ref, state_ref, strain_ref, weights, stress_s, rows * columns
        )
        for g in range(group):
            set_pencil(out_s, entries[g], states[g])
        whole = jnp.maximum(sent, lax.div(entries[group - 1] + 1, group))

        def send(chunk, carry):
            store(chunk).start()
            return carry

        lax.fori_loop(sent, whole, send, 0)
        return whole

    sent = lax.fori_loop(before, after, body, 0)

    def send(chunk, carry):
        store(chunk).start()
        return carry

    lax.fori_loop(sent, groups, send, 0)

    below = None
    for i in range(rows):
        here = row_fluxes(stress_s, i, columns)
        for c in range(3):
            force_ref[c, i] = -here[c][0] if below is None else -(here[c][0] + below[c][1])
        below = here
    for q in range(groups):
        store(q).wait()


def update_kernel(
    disp_ref, velocity_ref, external_ref, mass_ref, force_ref, xface_ref, yface_ref, cface_ref,
    disp_out, velocity_out,
):
    rows, columns, layers = mass_ref.shape
    first_sub = lax.broadcasted_iota(jnp.int32, (columns, layers), 0) == 0
    for i in range(rows):
        factor = STEP / mass_ref[i]
        for c in range(3):
            edge = yface_ref[c, i : i + 1]
            if i == 0:
                edge = edge + cface_ref[c : c + 1]
            internal = force_ref[c, i] + jnp.where(
                first_sub, jnp.broadcast_to(edge, (columns, layers)), 0.0
            )
            if i == 0:
                internal = internal + xface_ref[c]
            velocity = velocity_ref[c, i] + factor * (external_ref[c, i] - internal)
            velocity_out[c, i] = velocity
            disp_out[c, i] = disp_ref[c, i] + STEP * velocity


def shape(*dims, dtype=F32):
    return jax.ShapeDtypeStruct(dims, dtype)


def on_device(
    displacement, velocity, external_force, node_mass, stiffness, cloak_list, micro_state,
    localization, modes, point_weight, point_modulus, softening,
):
    rows, columns, layers = stiffness.shape
    points, count = modes.shape
    most = cloak_list.shape[2]
    gx, gy = lax.axis_size("gx"), lax.axis_size("gy")
    along_x = [(i + 1, i) for i in range(gx - 1)]
    along_y = [(i + 1, i) for i in range(gy - 1)]
    both = [((i + 1) * gy + j + 1, i * gy + j) for i in range(gx - 1) for j in range(gy - 1)]
    back = lambda pairs: [(b, a) for a, b in pairs]
    group = 8
    xhalo, yhalo, corner = pl.pallas_call(
        edges_kernel,
        out_shape=(shape(3, columns, layers), shape(3, rows, layers), shape(3, layers)),
        in_specs=[HBM],
        out_specs=(VMEM,) * 3,
        scratch_shapes=[pltpu.VMEM(displacement.shape, F32), pltpu.SemaphoreType.DMA((1,))],
        compiler_params=pltpu.CompilerParams(vmem_limit_bytes=GRANT),
        cost_estimate=pl.CostEstimate(flops=10**10, bytes_accessed=10**6, transcendentals=0),
    )(displacement)
    xhalo = lax.ppermute(xhalo, "gx", along_x)
    yhalo = lax.ppermute(yhalo, "gy", along_y)
    corner = lax.ppermute(corner, ("gx", "gy"), both)

    *matrices, order = pl.pallas_call(
        functools.partial(matrices_kernel, rows, columns),
        out_shape=tuple(shape(n, points, dtype=BF16) for n in (2 * count, 2 * count, points, points))
        + (
            shape(points, 2 * count, dtype=BF16), shape(16, points, dtype=BF16),
            shape(2, most + 2, dtype=jnp.int32),
        ),
        in_specs=[HBM] * 5 + [SMEM],
        out_specs=(VMEM,) * 6 + (SMEM,),
        scratch_shapes=[
            pltpu.VMEM((16, points), F32), pltpu.VMEM((points, count), F32),
            pltpu.VMEM((localization.shape[1], points), F32),
        ]
        + [pltpu.VMEM((1, points), F32)] * 3
        + [pltpu.SemaphoreType.DMA((5,))],
        compiler_params=pltpu.CompilerParams(vmem_limit_bytes=16 * 2**20),
        cost_estimate=pl.CostEstimate(flops=10**10, bytes_accessed=10**6, transcendentals=0),
    )(
        modes, localization.T, point_weight.reshape(1, points), point_modulus.reshape(1, points),
        softening.reshape(1, points), cloak_list[0],
    )

    groups = most // group
    states = micro_state.reshape(count * most, layers)
    strain_shape = shape(rows * columns * 8, layers)
    stress_shape = shape(rows * columns * 8 + 8, layers)
    xface, yface, cface, strain, stress, done = pl.pallas_call(
        functools.partial(edge_kernel, group),
        out_shape=(
            shape(3, columns, layers), shape(3, rows, layers), shape(3, layers),
            strain_shape, stress_shape, shape(most * count, layers),
        ),
        in_specs=[SMEM] + [VMEM] * 12,
        out_specs=(VMEM,) * 6,
        compiler_params=pltpu.CompilerParams(vmem_limit_bytes=30 * 2**20),
        cost_estimate=pl.CostEstimate(flops=10**10, bytes_accessed=10**7, transcendentals=0),
    )(order, displacement, xhalo, yhalo, corner, stiffness, states, *matrices)

    xface = lax.ppermute(xface, "gx", back(along_x))
    yface = lax.ppermute(yface, "gy", back(along_y))
    cface = lax.ppermute(cface, ("gx", "gy"), back(both))

    force, new_state = pl.pallas_call(
        functools.partial(inner_kernel, rows, columns),
        out_shape=(shape(3, rows, columns, layers), shape(count, most, layers)),
        in_specs=[SMEM] + [VMEM] * 10,
        out_specs=(VMEM, HBM),
        scratch_shapes=[
            pltpu.VMEM(stress_shape.shape, F32), pltpu.VMEM((groups, count, group, layers), F32),
            pltpu.SemaphoreType.DMA((groups,)),
        ],
        compiler_params=pltpu.CompilerParams(vmem_limit_bytes=30 * 2**20),
        cost_estimate=pl.CostEstimate(flops=2 * 10**10, bytes_accessed=10**7, transcendentals=0),
    )(order, states, strain, stress, done, *matrices)

    displacement_next, velocity_next = pl.pallas_call(
        update_kernel,
        out_shape=(shape(3, rows, columns, layers),) * 2,
        in_specs=[VMEM] * 8,
        out_specs=(VMEM,) * 2,
        compiler_params=pltpu.CompilerParams(vmem_limit_bytes=16 * 2**20),
    )(displacement, velocity, external_force, node_mass, force, xface, yface, cface)
    return displacement_next, velocity_next, new_state.reshape(micro_state.shape)


def solution(mesh):
    field = P(None, "gx", "gy", None)
    grid = P("gx", "gy", None)
    state = P("gx", "gy", None, None, None)
    in_specs = (field, field, field, grid, grid, P("gx", None, None), state, P(), P(), P(), P(), P())
    return jax.shard_map(
        on_device, mesh=mesh, in_specs=in_specs, out_specs=(field, field, state), check_vma=False
    )
```

```python
import functools

import jax
import jax.numpy as jnp
from jax import lax
from jax.experimental import pallas as pl
from jax.experimental.pallas import tpu as pltpu
from jax.sharding import PartitionSpec as P

ITERS = 3
STEP = 0.25
HIGHEST = lax.Precision.HIGHEST
F32 = jnp.float32
BF16 = jnp.bfloat16
GRANT = 60 * 2**20
VMEM = pl.BlockSpec(memory_space=pltpu.VMEM)
HBM = pl.BlockSpec(memory_space=pltpu.HBM)
SMEM = pl.BlockSpec(memory_space=pltpu.SMEM)


def split(x):
    high = x.astype(BF16)
    return high, (x - high.astype(F32)).astype(BF16)


def dot(a, b):
    return jnp.dot(a, b, preferred_element_type=F32)


def exact(a, b):
    return jnp.dot(a, b, precision=HIGHEST, preferred_element_type=F32)


def transposed_product(a, b):
    terms = []
    for x in (a, b):
        one = x.astype(BF16).astype(F32)
        two = (x - one).astype(BF16).astype(F32)
        terms.append((one, two, x - one - two))
    (a1, a2, a3), (b1, b2, b3) = terms
    left = jnp.concatenate([a1, a1, a2, a2, a1, a3], axis=0).astype(BF16)
    right = jnp.concatenate([b1, b2, b1, b2, b3, b1], axis=0).astype(BF16)
    return lax.dot_general(left, right, (((0,), (0,)), ((), ())), preferred_element_type=F32)


def lane_of(x, k):
    return jnp.take_along_axis(x, jnp.full(x.shape, k, jnp.int32), axis=1, mode="promise_in_bounds")


def row_of(x, s):
    return jnp.take_along_axis(x, jnp.full(x.shape, s, jnp.int32), axis=0, mode="promise_in_bounds")


def invert_two(a, b, c):
    scale = 1.0 / (a * c - b * b)
    return c * scale, -(b * scale), a * scale


def inverse(matrix):
    size = matrix.shape[0]
    tile = (8, size)
    count = size // 8
    blocks = [matrix[i : i + 8] for i in range(0, size, 8)]
    lane = lax.broadcasted_iota(jnp.int32, tile, 1)
    row = lax.broadcasted_iota(jnp.int32, tile, 0)

    def spread(x, s):
        return jnp.broadcast_to(x[s : s + 1, :], tile)

    for b in range(count):
        before = panel = blocks[b]
        for s in range(0, 8, 4):
            k = b * 8 + s
            lanes4 = jnp.logical_and(lane >= k, lane < k + 4)
            rows4 = jnp.logical_and(row >= s, row < s + 4)
            c = [lane_of(panel, k + i) for i in range(4)]
            r = [
                jnp.where(lane == k + i, 1.0, jnp.where(lanes4, 0.0, spread(panel, s + i)))
                for i in range(4)
            ]
            p = [[row_of(c[j], s + i) for j in range(i + 1)] for i in range(4)]
            (b00, b01), (b10, b11) = p[2][:2], p[3][:2]
            i00, i10, i11 = invert_two(p[0][0], p[1][0], p[1][1])
            w00, w01 = b00 * i00 + b01 * i10, b00 * i10 + b01 * i11
            w10, w11 = b10 * i00 + b11 * i10, b10 * i10 + b11 * i11
            j00, j10, j11 = invert_two(
                p[2][2] - (w00 * b00 + w01 * b01),
                p[3][2] - (w10 * b00 + w11 * b01),
                p[3][3] - (w10 * b10 + w11 * b11),
            )
            y2 = r[2] - (w00 * r[0] + w01 * r[1])
            y3 = r[3] - (w10 * r[0] + w11 * r[1])
            n2, n3 = j00 * y2 + j10 * y3, j10 * y2 + j11 * y3
            n0 = (i00 * r[0] + i10 * r[1]) - (w00 * n2 + w10 * n3)
            n1 = (i10 * r[0] + i11 * r[1]) - (w01 * n2 + w11 * n3)
            f = [jnp.where(row == s + i, -1.0, jnp.where(rows4, 0.0, c[i])) for i in range(4)]
            rest = jnp.where(jnp.logical_or(lanes4, rows4), 0.0, panel)
            panel = rest - ((f[0] * n0 + f[1] * n1) + (f[2] * n2 + f[3] * n3))
        inside = jnp.logical_and(lane >= b * 8, lane < b * 8 + 8)
        panel = jnp.where(inside, -panel, panel)
        change = transposed_product(before, panel)
        for i in range(count):
            old = blocks[i]
            kept = jnp.where(inside, 0.0, old)
            if i == b:
                blocks[i] = panel
            elif i == b + 1:
                t = [lane_of(old, b * 8 + s) * spread(panel, s) for s in range(8)]
                blocks[i] = kept - (((t[0] + t[1]) + (t[2] + t[3])) + ((t[4] + t[5]) + (t[6] + t[7])))
            else:
                blocks[i] = kept - change[i * 8 : i * 8 + 8]
    return -jnp.concatenate(blocks, axis=0)


def near(a, b):
    (ah, al), (bh, bl) = split(a), split(b)
    return dot(ah, bh) + dot(al, bh) + dot(ah, bl)


def fetch(sources, targets, sems):
    copies = [
        pltpu.make_async_copy(a, b, sems.at[i]) for i, (a, b) in enumerate(zip(sources, targets))
    ]
    for copy in copies:
        copy.start()
    for copy in copies:
        copy.wait()


def order_entries(rows, columns, lists_ref, order_ref):
    member = lax.axis_index("gy")
    most = lists_ref.shape[1]
    pencils = [lists_ref[member, e] for e in range(most)]
    listed = [(p >= 0).astype(jnp.int32) for p in pencils]
    edge = [
        jnp.logical_or(p >= (rows - 1) * columns, lax.rem(p, columns) == columns - 1).astype(jnp.int32)
        for p in pencils
    ]
    edges, number = sum(edge), sum(listed)
    next_edge, next_inner, next_rest = 0, edges, number
    for e in range(most):
        inner = listed[e] - edge[e]
        place = jnp.where(edge[e] > 0, next_edge, jnp.where(inner > 0, next_inner, next_rest))
        order_ref[0, place] = e
        order_ref[1, place] = pencils[e]
        next_edge = next_edge + edge[e]
        next_inner = next_inner + inner
        next_rest = next_rest + (1 - listed[e])
    order_ref[0, most] = edges
    order_ref[0, most + 1] = number


def matrices_kernel(
    modes_hbm, local_hbm, weight_hbm, modulus_hbm, soft_hbm,
    start0_ref, start1_ref, high_ref, low_ref, back_ref, stress_ref,
    wide, modes_ref, local_ref, weight_ref, modulus_ref, soft_ref, sems,
):
    fetch(
        (modes_hbm, local_hbm, weight_hbm, modulus_hbm, soft_hbm),
        (modes_ref, local_ref, weight_ref, modulus_ref, soft_ref),
        sems,
    )
    points, count = modes_ref.shape
    modes = modes_ref[...]
    modes_t = modes.T
    weight = weight_ref[...] / points
    modulus = modulus_ref[...]
    root = jnp.sqrt(soft_ref[...])
    scale = weight * modulus / root
    inverted = inverse(exact(modes_t * (weight * modulus), modes))
    wide[...] = jnp.zeros_like(wide)
    wide[0 : local_ref.shape[0], :] = local_ref[...]
    local = wide[...]
    stress_ref[...] = (local * scale).astype(BF16)
    high, low = split(modes_t * root)
    start0_ref[0:count] = high
    start0_ref[count:] = high
    start1_ref[0:count] = low
    soft_local = local[0:8] * root
    local_high = soft_local.astype(BF16).astype(F32)
    part = [local_high, local_high, soft_local - local_high, jnp.zeros_like(local_high)]
    start1_ref[count:] = jnp.concatenate(part * (count // 32), axis=0).astype(BF16)
    back = near((modes_t * scale).T, inverted)
    high, low = split(back)
    back_ref[:, 0:count] = high
    back_ref[:, count:] = low
    newton = near(back, modes_t * root)
    high, low = split(newton)
    high_ref[...] = high
    low_ref[...] = low


def respond(u):
    return u * lax.rsqrt(1.0 + u * u)


def cells(states, strains, start0, start1, newton_high, newton_low, back, stress_m):
    layers = states[0].shape[1]
    count = states[0].shape[0]
    number = len(states)
    part = min(2, number)
    turned = [state.T for state in states]
    place = lax.broadcasted_iota(jnp.int32, (layers, count), 1) // 32
    strain_parts = []
    each = count // 32
    for q in range(0, number, each):
        rows = []
        for strain in strains[q : q + each]:
            high = strain.astype(BF16).astype(F32)
            rows += [high, strain - high, high, jnp.zeros_like(high)]
        rows = jnp.concatenate(rows, axis=0).T
        strain_parts += [jnp.where(place == g, rows, 0.0).astype(BF16) for g in range(each)]
    start = []
    for c in range(0, number, part):
        high, low = split(jnp.concatenate(turned[c : c + part], axis=0))
        strain = jnp.concatenate(strain_parts[c : c + part], axis=0)
        start.append(
            dot(jnp.concatenate([high, low], axis=1), start0)
            + dot(jnp.concatenate([high, strain], axis=1), start1)
        )
    now = start
    for step in range(ITERS - 1):
        later = []
        for u in now:
            high, low = split(respond(u))
            later.append(u - (dot(high, newton_high) + dot(low, newton_high) + dot(high, newton_low)))
        now = later
    last, moved = [], []
    for first, u in zip(start, now):
        h = respond(u)
        last.append(u - dot(h.astype(BF16), newton_high))
        moved.append(split(first - u + h))
    new_states, stresses = [], []
    for c, (high, low) in enumerate(moved):
        both = dot(high, back)
        change = both[:, 0:count] + both[:, count:] + dot(low, back[:, 0:count])
        for g in range(part):
            new_states.append(states[c * part + g] - change[g * layers : (g + 1) * layers].T)
    for u in last:
        stress = lax.dot_general(
            stress_m, respond(u).astype(BF16), (((1,), (1,)), ((), ())), preferred_element_type=F32
        )
        stresses += [stress[0:8, g * layers : (g + 1) * layers] for g in range(part)]
    return new_states, stresses


def set_pencil(ref, entry, value):
    groups, count, group, layers = ref.shape
    place = lax.div(entry, group) * (count * group) + lax.rem(entry, group)
    ref.reshape(groups * count * group, layers)[pl.ds(place, count, stride=group), :] = value


def run_group(base, group, order_ref, state_ref, strain_ref, weights, stress_s, spare):
    count = weights[4].shape[1] // 2
    most = state_ref.shape[0] // count
    entries = [order_ref[0, base + g] for g in range(group)]
    pencils = [order_ref[1, base + g] for g in range(group)]
    states = [state_ref[pl.ds(e, count, stride=most), :] for e in entries]
    strains = [
        strain_ref[pl.ds(pl.multiple_of(jnp.maximum(p, 0) * 8, 8), 8), :] for p in pencils
    ]
    new_states, stresses = cells(states, strains, *(w[...] for w in weights))
    for g in range(group):
        spot = jnp.where(pencils[g] >= 0, pencils[g], spare)
        stress_s[pl.ds(pl.multiple_of(spot * 8, 8), 8), :] = stresses[g]
    return entries, [jnp.where(p >= 0, a, 0.0) for p, a in zip(pencils, new_states)]


def fluxes(s, side_mean, side_diff):
    lane_zero = lax.broadcasted_iota(jnp.int32, s[0].shape, 1) == 0

    def along(v):
        down = jnp.where(lane_zero, 0.0, pltpu.roll(v, 1, 1))
        return 0.5 * (v + down), v - down

    first = [along(side_mean(s[c]))[0] for c in (0, 5, 4)]
    second = [along(side_diff(s[c]))[0] for c in (5, 1, 3)]
    third = [along(side_mean(s[c]))[1] for c in (4, 3, 2)]
    half = [0.5 * (second[c] + third[c]) for c in range(3)]
    return [(first[c] + half[c], half[c] - first[c]) for c in range(3)]


def row_fluxes(stress_ref, i, columns):
    s = [stress_ref[pl.ds(i * columns * 8 + c, columns, stride=8), :] for c in range(6)]
    first_sub = lax.broadcasted_iota(jnp.int32, s[0].shape, 0) == 0

    def shift(v):
        return jnp.where(first_sub, 0.0, pltpu.roll(v, 1, 0))

    return fluxes(s, lambda v: 0.5 * (v + shift(v)), lambda v: v - shift(v))


def first_groups(order_ref, most, group):
    return lax.div(order_ref[0, most] + (group - 1), group)


def edges_kernel(disp_hbm, lists_ref, xface_ref, yface_ref, corner_ref, order_ref, disp_ref, sem):
    copy = pltpu.make_async_copy(disp_hbm, disp_ref, sem)
    copy.start()
    order_entries(disp_ref.shape[1], disp_ref.shape[2], lists_ref, order_ref)
    copy.wait()
    for c in range(3):
        xface_ref[c] = disp_ref[c, 0]
        yface_ref[c] = disp_ref[c, :, 0, :]
        corner_ref[c : c + 1] = disp_ref[c, 0, 0:1]


def edge_kernel(
    group, order_ref, disp_ref, xhalo_ref, yhalo_ref, corner_ref, stiff_ref, state_ref,
    start0_ref, start1_ref, high_ref, low_ref, back_ref, stress_ref,
    xface_ref, yface_ref, cface_ref, strain_ref, stress_out, done_ref,
):
    rows, columns, layers = stiff_ref.shape
    most = order_ref.shape[1] - 2
    count = state_ref.shape[0] // most
    weights = (start0_ref, start1_ref, high_ref, low_ref, back_ref, stress_ref)
    tile = (columns, layers)
    lane = lax.broadcasted_iota(jnp.int32, tile, 1)
    sub = lax.broadcasted_iota(jnp.int32, tile, 0)
    last_lane = lane == layers - 1
    last_sub = sub == columns - 1

    more_x = lax.axis_index("gx") < lax.axis_size("gx") - 1
    more_y = lax.axis_index("gy") < lax.axis_size("gy") - 1

    def node_row(c, i):
        own = disp_ref[c, i] if i < rows else jnp.where(more_x, xhalo_ref[c], 0.0)
        edge = yhalo_ref[c, i : i + 1] if i < rows else jnp.where(more_x, corner_ref[c : c + 1], 0.0)
        edge = jnp.where(more_y, edge, 0.0)
        up = jnp.where(last_sub, jnp.broadcast_to(edge, tile), pltpu.roll(own, columns - 1, 0))
        mean, diff = 0.5 * (up + own), up - own
        mean_up = jnp.where(last_lane, 0.0, pltpu.roll(mean, layers - 1, 1))
        diff_up = jnp.where(last_lane, 0.0, pltpu.roll(diff, layers - 1, 1))
        return 0.5 * (mean_up + mean), 0.5 * (diff_up + diff), mean_up - mean

    lower = [node_row(c, 0) for c in range(3)]
    zero_tile = jnp.zeros(tile, F32)
    for i in range(rows):
        upper = [node_row(c, i + 1) for c in range(3)]
        g = [
            (upper[c][0] - lower[c][0], 0.5 * (upper[c][1] + lower[c][1]), 0.5 * (upper[c][2] + lower[c][2]))
            for c in range(3)
        ]
        lower = upper
        strain = [g[0][0], g[1][1], g[2][2], g[1][2] + g[2][1], g[0][2] + g[2][0], g[0][1] + g[1][0]]
        stiffness = stiff_ref[i]
        volume = strain[0] + strain[1] + strain[2]
        for c in range(8):
            place = pl.ds(i * columns * 8 + c, columns, stride=8)
            if c >= 6:
                strain_ref[place, :] = zero_tile
                continue
            strain_ref[place, :] = strain[c]
            stress_out[place, :] = stiffness * (volume + 2.0 * strain[c] if c < 3 else strain[c])

    def body(q, carry):
        _, states = run_group(
            q * group, group, order_ref, state_ref, strain_ref, weights, stress_out, rows * columns
        )
        for g in range(group):
            done_ref[pl.ds(pl.multiple_of((q * group + g) * count, count), count), :] = states[g]
        return carry

    lax.fori_loop(0, first_groups(order_ref, most, group), body, 0)

    last = row_fluxes(stress_out, rows - 1, columns)
    for c in range(3):
        xface_ref[c] = -last[c][1]
    s = [stress_out[pl.ds((columns - 1) * 8 + c, rows, stride=columns * 8), :] for c in range(6)]
    side = fluxes(s, lambda v: 0.5 * v, lambda v: -v)
    for c in range(3):
        yface_ref[c] = -side[c][0]
        yface_ref[c, 1:rows] = yface_ref[c, 1:rows] - side[c][1][0 : rows - 1]
        cface_ref[c : c + 1] = -side[c][1][rows - 1 : rows]


def inner_kernel(
    rows, columns, order_ref, state_ref, strain_ref, stress_in, done_ref,
    start0_ref, start1_ref, high_ref, low_ref, back_ref, stress_ref,
    force_ref, out_hbm,
    stress_s, out_s, sems,
):
    groups, count, group, layers = out_s.shape
    most = groups * group
    weights = (start0_ref, start1_ref, high_ref, low_ref, back_ref, stress_ref)
    before = first_groups(order_ref, most, group)
    after = lax.div(order_ref[0, most + 1] + (group - 1), group)
    stress_s[...] = stress_in[...]

    def store(q):
        return pltpu.make_async_copy(
            out_s.at[q], out_hbm.at[:, pl.ds(q * group, group), :], sems.at[q]
        )

    def copy(q, carry):
        for g in range(group):
            place = q * group + g
            set_pencil(
                out_s, order_ref[0, place],
                done_ref[pl.ds(pl.multiple_of(place * count, count), count), :],
            )
        return carry

    def clear(q, carry):
        for g in range(group):
            set_pencil(out_s, order_ref[0, q * group + g], jnp.zeros((count, layers), F32))
        return carry

    lax.fori_loop(0, before, copy, 0)
    lax.fori_loop(jnp.maximum(before, after), groups, clear, 0)

    def body(q, sent):
        entries, states = run_group(
            q * group, group, order_ref, state_ref, strain_ref, weights, stress_s, rows * columns
        )
        for g in range(group):
            set_pencil(out_s, entries[g], states[g])
        whole = jnp.maximum(sent, lax.div(entries[group - 1] + 1, group))

        def send(chunk, carry):
            store(chunk).start()
            return carry

        lax.fori_loop(sent, whole, send, 0)
        return whole

    sent = lax.fori_loop(before, after, body, 0)

    def send(chunk, carry):
        store(chunk).start()
        return carry

    lax.fori_loop(sent, groups, send, 0)

    below = None
    for i in range(rows):
        here = row_fluxes(stress_s, i, columns)
        for c in range(3):
            force_ref[c, i] = -here[c][0] if below is None else -(here[c][0] + below[c][1])
        below = here
    for q in range(groups):
        store(q).wait()


def update_kernel(
    disp_ref, velocity_ref, external_ref, mass_ref, force_ref, xface_ref, yface_ref, cface_ref,
    disp_out, velocity_out,
):
    rows, columns, layers = mass_ref.shape
    less_x = lax.axis_index("gx") > 0
    first_sub = lax.broadcasted_iota(jnp.int32, (columns, layers), 0) == 0
    first_sub = jnp.logical_and(first_sub, lax.axis_index("gy") > 0)
    for i in range(rows):
        factor = STEP / mass_ref[i]
        for c in range(3):
            edge = yface_ref[c, i : i + 1]
            if i == 0:
                edge = edge + jnp.where(less_x, cface_ref[c : c + 1], 0.0)
            internal = force_ref[c, i] + jnp.where(
                first_sub, jnp.broadcast_to(edge, (columns, layers)), 0.0
            )
            if i == 0:
                internal = internal + jnp.where(less_x, xface_ref[c], 0.0)
            velocity = velocity_ref[c, i] + factor * (external_ref[c, i] - internal)
            velocity_out[c, i] = velocity
            disp_out[c, i] = disp_ref[c, i] + STEP * velocity


def shape(*dims, dtype=F32):
    return jax.ShapeDtypeStruct(dims, dtype)


def on_device(
    displacement, velocity, external_force, node_mass, stiffness, cloak_list, micro_state,
    localization, modes, point_weight, point_modulus, softening,
):
    rows, columns, layers = stiffness.shape
    points, count = modes.shape
    most = cloak_list.shape[2]
    gx, gy = lax.axis_size("gx"), lax.axis_size("gy")
    along_x = [((i + 1) % gx, i) for i in range(gx)]
    along_y = [((j + 1) % gy, j) for j in range(gy)]
    both = [((i + 1) % gx * gy + (j + 1) % gy, i * gy + j) for i in range(gx) for j in range(gy)]
    back = lambda pairs: [(b, a) for a, b in pairs]
    group = 8
    xhalo, yhalo, corner, order = pl.pallas_call(
        edges_kernel,
        out_shape=(
            shape(3, columns, layers), shape(3, rows, layers), shape(3, layers),
            shape(2, most + 2, dtype=jnp.int32),
        ),
        in_specs=[HBM, SMEM],
        out_specs=(VMEM,) * 3 + (SMEM,),
        scratch_shapes=[pltpu.VMEM(displacement.shape, F32), pltpu.SemaphoreType.DMA],
        compiler_params=pltpu.CompilerParams(vmem_limit_bytes=GRANT),
        cost_estimate=pl.CostEstimate(flops=10**10, bytes_accessed=10**6, transcendentals=0),
    )(displacement, cloak_list[0])
    xhalo = lax.ppermute(xhalo, "gx", along_x)
    yhalo = lax.ppermute(yhalo, "gy", along_y)
    corner = lax.ppermute(corner, ("gx", "gy"), both)

    matrices = pl.pallas_call(
        matrices_kernel,
        out_shape=tuple(shape(n, points, dtype=BF16) for n in (2 * count, 2 * count, points, points))
        + (shape(points, 2 * count, dtype=BF16), shape(16, points, dtype=BF16)),
        in_specs=[HBM] * 5,
        out_specs=(VMEM,) * 6,
        scratch_shapes=[
            pltpu.VMEM((16, points), F32), pltpu.VMEM((points, count), F32),
            pltpu.VMEM((localization.shape[1], points), F32),
        ]
        + [pltpu.VMEM((1, points), F32)] * 3
        + [pltpu.SemaphoreType.DMA((5,))],
        compiler_params=pltpu.CompilerParams(vmem_limit_bytes=16 * 2**20),
        cost_estimate=pl.CostEstimate(flops=10**10, bytes_accessed=10**6, transcendentals=0),
    )(
        modes, localization.T, point_weight.reshape(1, points), point_modulus.reshape(1, points),
        softening.reshape(1, points),
    )

    groups = most // group
    states = micro_state.reshape(count * most, layers)
    strain_shape = shape(rows * columns * 8, layers)
    stress_shape = shape(rows * columns * 8 + 8, layers)
    xface, yface, cface, strain, stress, done = pl.pallas_call(
        functools.partial(edge_kernel, group),
        out_shape=(
            shape(3, columns, layers), shape(3, rows, layers), shape(3, layers),
            strain_shape, stress_shape, shape(most * count, layers),
        ),
        in_specs=[SMEM] + [VMEM] * 12,
        out_specs=(VMEM,) * 6,
        compiler_params=pltpu.CompilerParams(vmem_limit_bytes=30 * 2**20),
        cost_estimate=pl.CostEstimate(flops=10**10, bytes_accessed=10**7, transcendentals=0),
    )(order, displacement, xhalo, yhalo, corner, stiffness, states, *matrices)

    xface = lax.ppermute(xface, "gx", back(along_x))
    yface = lax.ppermute(yface, "gy", back(along_y))
    cface = lax.ppermute(cface, ("gx", "gy"), back(both))

    force, new_state = pl.pallas_call(
        functools.partial(inner_kernel, rows, columns),
        out_shape=(shape(3, rows, columns, layers), shape(count, most, layers)),
        in_specs=[SMEM] + [VMEM] * 10,
        out_specs=(VMEM, HBM),
        scratch_shapes=[
            pltpu.VMEM(stress_shape.shape, F32), pltpu.VMEM((groups, count, group, layers), F32),
            pltpu.SemaphoreType.DMA((groups,)),
        ],
        compiler_params=pltpu.CompilerParams(vmem_limit_bytes=30 * 2**20),
        cost_estimate=pl.CostEstimate(flops=2 * 10**10, bytes_accessed=10**7, transcendentals=0),
    )(order, states, strain, stress, done, *matrices)

    displacement_next, velocity_next = pl.pallas_call(
        update_kernel,
        out_shape=(shape(3, rows, columns, layers),) * 2,
        in_specs=[VMEM] * 8,
        out_specs=(VMEM,) * 2,
        compiler_params=pltpu.CompilerParams(vmem_limit_bytes=16 * 2**20),
    )(displacement, velocity, external_force, node_mass, force, xface, yface, cface)
    return displacement_next, velocity_next, new_state.reshape(micro_state.shape)


def solution(mesh):
    field = P(None, "gx", "gy", None)
    grid = P("gx", "gy", None)
    state = P("gx", "gy", None, None, None)
    in_specs = (field, field, field, grid, grid, P("gx", None, None), state, P(), P(), P(), P(), P())
    return jax.shard_map(
        on_device, mesh=mesh, in_specs=in_specs, out_specs=(field, field, state), check_vma=False
    )
```

```python
import functools

import jax
import jax.numpy as jnp
from jax import lax
from jax.experimental import pallas as pl
from jax.experimental.pallas import tpu as pltpu
from jax.sharding import PartitionSpec as P

ITERS = 3
STEP = 0.25
HIGHEST = lax.Precision.HIGHEST
F32 = jnp.float32
BF16 = jnp.bfloat16
VMEM = pl.BlockSpec(memory_space=pltpu.VMEM)
HBM = pl.BlockSpec(memory_space=pltpu.HBM)


def split(x):
    high = x.astype(BF16)
    return high, (x - high.astype(F32)).astype(BF16)


def dot(a, b):
    return jnp.dot(a, b, preferred_element_type=F32)


def exact(a, b):
    return jnp.dot(a, b, precision=HIGHEST, preferred_element_type=F32)


def transposed_product(a, b):
    terms = []
    for x in (a, b):
        one = x.astype(BF16).astype(F32)
        two = (x - one).astype(BF16).astype(F32)
        terms.append((one, two, x - one - two))
    (a1, a2, a3), (b1, b2, b3) = terms
    left = jnp.concatenate([a1, a1, a2, a2, a1, a3], axis=0).astype(BF16)
    right = jnp.concatenate([b1, b2, b1, b2, b3, b1], axis=0).astype(BF16)
    return lax.dot_general(left, right, (((0,), (0,)), ((), ())), preferred_element_type=F32)


def lane_of(x, k):
    return jnp.take_along_axis(x, jnp.full(x.shape, k, jnp.int32), axis=1, mode="promise_in_bounds")


def row_of(x, s):
    return jnp.take_along_axis(x, jnp.full(x.shape, s, jnp.int32), axis=0, mode="promise_in_bounds")


def invert_two(a, b, c):
    scale = 1.0 / (a * c - b * b)
    return c * scale, -(b * scale), a * scale


def inverse(matrix):
    size = matrix.shape[0]
    tile = (8, size)
    count = size // 8
    blocks = [matrix[i : i + 8] for i in range(0, size, 8)]
    lane = lax.broadcasted_iota(jnp.int32, tile, 1)
    row = lax.broadcasted_iota(jnp.int32, tile, 0)

    def spread(x, s):
        return jnp.broadcast_to(x[s : s + 1, :], tile)

    for b in range(count):
        before = panel = blocks[b]
        for s in range(0, 8, 4):
            k = b * 8 + s
            lanes4 = jnp.logical_and(lane >= k, lane < k + 4)
            rows4 = jnp.logical_and(row >= s, row < s + 4)
            c = [lane_of(panel, k + i) for i in range(4)]
            r = [
                jnp.where(lane == k + i, 1.0, jnp.where(lanes4, 0.0, spread(panel, s + i)))
                for i in range(4)
            ]
            p = [[row_of(c[j], s + i) for j in range(i + 1)] for i in range(4)]
            (b00, b01), (b10, b11) = p[2][:2], p[3][:2]
            i00, i10, i11 = invert_two(p[0][0], p[1][0], p[1][1])
            w00, w01 = b00 * i00 + b01 * i10, b00 * i10 + b01 * i11
            w10, w11 = b10 * i00 + b11 * i10, b10 * i10 + b11 * i11
            j00, j10, j11 = invert_two(
                p[2][2] - (w00 * b00 + w01 * b01),
                p[3][2] - (w10 * b00 + w11 * b01),
                p[3][3] - (w10 * b10 + w11 * b11),
            )
            y2 = r[2] - (w00 * r[0] + w01 * r[1])
            y3 = r[3] - (w10 * r[0] + w11 * r[1])
            n2, n3 = j00 * y2 + j10 * y3, j10 * y2 + j11 * y3
            n0 = (i00 * r[0] + i10 * r[1]) - (w00 * n2 + w10 * n3)
            n1 = (i10 * r[0] + i11 * r[1]) - (w01 * n2 + w11 * n3)
            f = [jnp.where(row == s + i, -1.0, jnp.where(rows4, 0.0, c[i])) for i in range(4)]
            rest = jnp.where(jnp.logical_or(lanes4, rows4), 0.0, panel)
            panel = rest - ((f[0] * n0 + f[1] * n1) + (f[2] * n2 + f[3] * n3))
        inside = jnp.logical_and(lane >= b * 8, lane < b * 8 + 8)
        panel = jnp.where(inside, -panel, panel)
        change = transposed_product(before, panel)
        for i in range(count):
            old = blocks[i]
            kept = jnp.where(inside, 0.0, old)
            if i == b:
                blocks[i] = panel
            elif i == b + 1:
                t = [lane_of(old, b * 8 + s) * spread(panel, s) for s in range(8)]
                blocks[i] = kept - (((t[0] + t[1]) + (t[2] + t[3])) + ((t[4] + t[5]) + (t[6] + t[7])))
            else:
                blocks[i] = kept - change[i * 8 : i * 8 + 8]
    return -jnp.concatenate(blocks, axis=0)


def near(a, b):
    (ah, al), (bh, bl) = split(a), split(b)
    return dot(ah, bh) + dot(al, bh) + dot(ah, bl)


def order_entries(rows, columns, lists_ref, order_ref, line):
    most = lists_ref.shape[1]
    width = order_ref.shape[1]
    tile = order_ref.shape
    line[...] = jnp.full(line.shape, -1, jnp.int32)
    line[0:1, 0:most] = lists_ref[pl.ds(lax.axis_index("gy"), 1), :]
    pencil = jnp.broadcast_to(line[0:1, :].astype(F32), tile)
    lane = lax.broadcasted_iota(jnp.int32, tile, 1)
    row = lax.broadcasted_iota(jnp.int32, tile, 0)
    column = pencil - columns * jnp.floor((pencil + 0.5) / columns)
    listed = pencil >= 0.0
    face = jnp.logical_or(pencil >= (rows - 1) * columns, column == columns - 1)
    kind = jnp.where(listed, jnp.where(face, 0, 1), jnp.where(lane < most, 2, 3))
    flags = jnp.where(kind == row, 1.0, 0.0).astype(BF16)
    square = (width, width)
    first = lax.broadcasted_iota(jnp.int32, square, 0)
    second = lax.broadcasted_iota(jnp.int32, square, 1)
    before = dot(flags, (first < second).astype(F32).astype(BF16))
    totals = dot(flags, jnp.ones(square, BF16))
    faces, number = totals[0:1], totals[0:1] + totals[1:2]
    kind = kind[0:1]
    place = jnp.where(
        kind == 0, before[0:1],
        jnp.where(kind == 1, faces + before[1:2], jnp.where(kind == 2, number + before[2:3], -1.0)),
    )
    moves = (jnp.broadcast_to(place, square) == first.astype(F32)).astype(F32)
    values = jnp.where(row == 0, lane.astype(F32), pencil)
    ordered = lax.dot_general(
        values, moves, (((1,), (1,)), ((), ())), precision=HIGHEST, preferred_element_type=F32
    )
    counts = jnp.where(lane == most, jnp.broadcast_to(faces, tile), jnp.broadcast_to(number, tile))
    tail = jnp.logical_and(row == 0, lane >= most)
    order_ref[...] = jnp.where(tail, counts, ordered).astype(jnp.int32)


def matrices_kernel(
    rows, columns, modes_ref, local_ref, weight_ref, modulus_ref, soft_ref, lists_ref,
    start0_ref, start1_ref, high_ref, low_ref, back_ref, stress_ref, order_ref, wide, line,
):
    order_entries(rows, columns, lists_ref, order_ref, line)
    points, count = modes_ref.shape
    modes = modes_ref[...]
    modes_t = modes.T
    weight = weight_ref[...] / points
    modulus = modulus_ref[...]
    root = jnp.sqrt(soft_ref[...])
    scale = weight * modulus / root
    inverted = inverse(exact(modes_t * (weight * modulus), modes))
    wide[...] = jnp.zeros_like(wide)
    wide[0 : local_ref.shape[0], :] = local_ref[...]
    local = wide[...]
    stress_ref[...] = (local * scale).astype(BF16)
    high, low = split(modes_t * root)
    start0_ref[0:count] = high
    start0_ref[count:] = high
    start1_ref[0:count] = low
    soft_local = local[0:8] * root
    local_high = soft_local.astype(BF16).astype(F32)
    part = [local_high, local_high, soft_local - local_high, jnp.zeros_like(local_high)]
    start1_ref[count:] = jnp.concatenate(part * (count // 32), axis=0).astype(BF16)
    back = near((modes_t * scale).T, inverted)
    high, low = split(back)
    back_ref[:, 0:count] = high
    back_ref[:, count:] = low
    newton = near(back, modes_t * root)
    high, low = split(newton)
    high_ref[...] = high
    low_ref[...] = low


def respond(u):
    return u * lax.rsqrt(1.0 + u * u)


def cells(states, strains, start0, start1, newton_high, newton_low, back, stress_m):
    layers = states[0].shape[1]
    count = states[0].shape[0]
    number = len(states)
    part = min(2, number)
    turned = [state.T for state in states]
    place = lax.broadcasted_iota(jnp.int32, (layers, count), 1) // 32
    strain_parts = []
    each = count // 32
    for q in range(0, number, each):
        rows = []
        for strain in strains[q : q + each]:
            high = strain.astype(BF16).astype(F32)
            rows += [high, strain - high, high, jnp.zeros_like(high)]
        rows = jnp.concatenate(rows, axis=0).T
        strain_parts += [jnp.where(place == g, rows, 0.0).astype(BF16) for g in range(each)]
    start = []
    for c in range(0, number, part):
        high, low = split(jnp.concatenate(turned[c : c + part], axis=0))
        strain = jnp.concatenate(strain_parts[c : c + part], axis=0)
        start.append(
            dot(jnp.concatenate([high, low], axis=1), start0)
            + dot(jnp.concatenate([high, strain], axis=1), start1)
        )
    now = start
    for step in range(ITERS - 1):
        later = []
        for u in now:
            high, low = split(respond(u))
            later.append(u - (dot(high, newton_high) + dot(low, newton_high) + dot(high, newton_low)))
        now = later
    last, moved = [], []
    for first, u in zip(start, now):
        h = respond(u)
        last.append(u - dot(h.astype(BF16), newton_high))
        moved.append(split(first - u + h))
    new_states, stresses = [], []
    for c, (high, low) in enumerate(moved):
        both = dot(high, back)
        change = both[:, 0:count] + both[:, count:] + dot(low, back[:, 0:count])
        for g in range(part):
            new_states.append(states[c * part + g] - change[g * layers : (g + 1) * layers].T)
    for u in last:
        stress = lax.dot_general(
            stress_m, respond(u).astype(BF16), (((1,), (1,)), ((), ())), preferred_element_type=F32
        )
        stresses += [stress[0:8, g * layers : (g + 1) * layers] for g in range(part)]
    return new_states, stresses


def set_pencil(ref, entry, value):
    groups, count, group, layers = ref.shape
    place = lax.div(entry, group) * (count * group) + lax.rem(entry, group)
    ref.reshape(groups * count * group, layers)[pl.ds(place, count, stride=group), :] = value


def run_group(base, group, order_ref, state_ref, strain_ref, weights, stress_s, spare):
    count = weights[4].shape[1] // 2
    most = state_ref.shape[0] // count
    entries = [order_ref[0, base + g] for g in range(group)]
    pencils = [order_ref[1, base + g] for g in range(group)]
    states = [state_ref[pl.ds(e, count, stride=most), :] for e in entries]
    strains = [
        strain_ref[pl.ds(pl.multiple_of(jnp.maximum(p, 0) * 8, 8), 8), :] for p in pencils
    ]
    new_states, stresses = cells(states, strains, *(w[...] for w in weights))
    for g in range(group):
        spot = jnp.where(pencils[g] >= 0, pencils[g], spare)
        stress_s[pl.ds(pl.multiple_of(spot * 8, 8), 8), :] = stresses[g]
    return entries, [jnp.where(p >= 0, a, 0.0) for p, a in zip(pencils, new_states)]


def fluxes(s, side_mean, side_diff):
    lane_zero = lax.broadcasted_iota(jnp.int32, s[0].shape, 1) == 0

    def along(v):
        down = jnp.where(lane_zero, 0.0, pltpu.roll(v, 1, 1))
        return 0.5 * (v + down), v - down

    first = [along(side_mean(s[c]))[0] for c in (0, 5, 4)]
    second = [along(side_diff(s[c]))[0] for c in (5, 1, 3)]
    third = [along(side_mean(s[c]))[1] for c in (4, 3, 2)]
    half = [0.5 * (second[c] + third[c]) for c in range(3)]
    return [(first[c] + half[c], half[c] - first[c]) for c in range(3)]


def row_fluxes(stress_ref, i, columns):
    s = [stress_ref[pl.ds(i * columns * 8 + c, columns, stride=8), :] for c in range(6)]
    first_sub = lax.broadcasted_iota(jnp.int32, s[0].shape, 0) == 0

    def shift(v):
        return jnp.where(first_sub, 0.0, pltpu.roll(v, 1, 0))

    return fluxes(s, lambda v: 0.5 * (v + shift(v)), lambda v: v - shift(v))


def first_groups(order_ref, most, group):
    return lax.div(order_ref[0, most] + (group - 1), group)


def edges_kernel(disp_ref, xface_ref, yface_ref, corner_ref):
    for c in range(3):
        xface_ref[c] = disp_ref[c, 0]
        yface_ref[c] = disp_ref[c, :, 0, :]
        corner_ref[c : c + 1] = disp_ref[c, 0, 0:1]


def edge_kernel(
    group, most, order_vmem, disp_ref, xhalo_ref, yhalo_ref, corner_ref, stiff_ref, state_ref,
    start0_ref, start1_ref, high_ref, low_ref, back_ref, stress_ref,
    xface_ref, yface_ref, cface_ref, strain_ref, stress_out, done_ref,
    order_ref, order_sem,
):
    order_copy = pltpu.make_async_copy(order_vmem, order_ref, order_sem)
    order_copy.start()
    rows, columns, layers = stiff_ref.shape
    count = state_ref.shape[0] // most
    weights = (start0_ref, start1_ref, high_ref, low_ref, back_ref, stress_ref)
    tile = (columns, layers)
    lane = lax.broadcasted_iota(jnp.int32, tile, 1)
    sub = lax.broadcasted_iota(jnp.int32, tile, 0)
    last_lane = lane == layers - 1
    last_sub = sub == columns - 1

    more_x = lax.axis_index("gx") < lax.axis_size("gx") - 1
    more_y = lax.axis_index("gy") < lax.axis_size("gy") - 1

    def node_row(c, i):
        own = disp_ref[c, i] if i < rows else jnp.where(more_x, xhalo_ref[c], 0.0)
        edge = yhalo_ref[c, i : i + 1] if i < rows else jnp.where(more_x, corner_ref[c : c + 1], 0.0)
        edge = jnp.where(more_y, edge, 0.0)
        up = jnp.where(last_sub, jnp.broadcast_to(edge, tile), pltpu.roll(own, columns - 1, 0))
        mean, diff = 0.5 * (up + own), up - own
        mean_up = jnp.where(last_lane, 0.0, pltpu.roll(mean, layers - 1, 1))
        diff_up = jnp.where(last_lane, 0.0, pltpu.roll(diff, layers - 1, 1))
        return 0.5 * (mean_up + mean), 0.5 * (diff_up + diff), mean_up - mean

    lower = [node_row(c, 0) for c in range(3)]
    zero_tile = jnp.zeros(tile, F32)
    for i in range(rows):
        upper = [node_row(c, i + 1) for c in range(3)]
        g = [
            (upper[c][0] - lower[c][0], 0.5 * (upper[c][1] + lower[c][1]), 0.5 * (upper[c][2] + lower[c][2]))
            for c in range(3)
        ]
        lower = upper
        strain = [g[0][0], g[1][1], g[2][2], g[1][2] + g[2][1], g[0][2] + g[2][0], g[0][1] + g[1][0]]
        stiffness = stiff_ref[i]
        volume = strain[0] + strain[1] + strain[2]
        for c in range(8):
            place = pl.ds(i * columns * 8 + c, columns, stride=8)
            if c >= 6:
                strain_ref[place, :] = zero_tile
                continue
            strain_ref[place, :] = strain[c]
            stress_out[place, :] = stiffness * (volume + 2.0 * strain[c] if c < 3 else strain[c])

    order_copy.wait()

    def body(q, carry):
        _, states = run_group(
            q * group, group, order_ref, state_ref, strain_ref, weights, stress_out, rows * columns
        )
        for g in range(group):
            done_ref[pl.ds(pl.multiple_of((q * group + g) * count, count), count), :] = states[g]
        return carry

    lax.fori_loop(0, first_groups(order_ref, most, group), body, 0)

    last = row_fluxes(stress_out, rows - 1, columns)
    for c in range(3):
        xface_ref[c] = -last[c][1]
    s = [stress_out[pl.ds((columns - 1) * 8 + c, rows, stride=columns * 8), :] for c in range(6)]
    side = fluxes(s, lambda v: 0.5 * v, lambda v: -v)
    for c in range(3):
        yface_ref[c] = -side[c][0]
        yface_ref[c, 1:rows] = yface_ref[c, 1:rows] - side[c][1][0 : rows - 1]
        cface_ref[c : c + 1] = -side[c][1][rows - 1 : rows]


def inner_kernel(
    rows, columns, order_vmem, state_ref, strain_ref, stress_in, done_ref,
    start0_ref, start1_ref, high_ref, low_ref, back_ref, stress_ref,
    force_ref, out_hbm,
    stress_s, out_s, sems, order_ref, order_sem,
):
    order_copy = pltpu.make_async_copy(order_vmem, order_ref, order_sem)
    order_copy.start()
    groups, count, group, layers = out_s.shape
    most = groups * group
    weights = (start0_ref, start1_ref, high_ref, low_ref, back_ref, stress_ref)
    stress_s[...] = stress_in[...]
    order_copy.wait()
    before = first_groups(order_ref, most, group)
    after = lax.div(order_ref[0, most + 1] + (group - 1), group)

    def store(q):
        return pltpu.make_async_copy(
            out_s.at[q], out_hbm.at[:, pl.ds(q * group, group), :], sems.at[q]
        )

    def copy(q, carry):
        for g in range(group):
            place = q * group + g
            set_pencil(
                out_s, order_ref[0, place],
                done_ref[pl.ds(pl.multiple_of(place * count, count), count), :],
            )
        return carry

    def clear(q, carry):
        for g in range(group):
            set_pencil(out_s, order_ref[0, q * group + g], jnp.zeros((count, layers), F32))
        return carry

    lax.fori_loop(0, before, copy, 0)
    lax.fori_loop(jnp.maximum(before, after), groups, clear, 0)

    def body(q, sent):
        entries, states = run_group(
            q * group, group, order_ref, state_ref, strain_ref, weights, stress_s, rows * columns
        )
        for g in range(group):
            set_pencil(out_s, entries[g], states[g])
        whole = jnp.maximum(sent, lax.div(entries[group - 1] + 1, group))

        def send(chunk, carry):
            store(chunk).start()
            return carry

        lax.fori_loop(sent, whole, send, 0)
        return whole

    sent = lax.fori_loop(before, after, body, 0)

    def send(chunk, carry):
        store(chunk).start()
        return carry

    lax.fori_loop(sent, groups, send, 0)

    below = None
    for i in range(rows):
        here = row_fluxes(stress_s, i, columns)
        for c in range(3):
            force_ref[c, i] = -here[c][0] if below is None else -(here[c][0] + below[c][1])
        below = here
    for q in range(groups):
        store(q).wait()


def update_kernel(
    disp_ref, velocity_ref, external_ref, mass_ref, force_ref, xface_ref, yface_ref, cface_ref,
    disp_out, velocity_out,
):
    rows, columns, layers = mass_ref.shape
    less_x = lax.axis_index("gx") > 0
    first_sub = lax.broadcasted_iota(jnp.int32, (columns, layers), 0) == 0
    first_sub = jnp.logical_and(first_sub, lax.axis_index("gy") > 0)
    for i in range(rows):
        factor = STEP / mass_ref[i]
        for c in range(3):
            edge = yface_ref[c, i : i + 1]
            if i == 0:
                edge = edge + jnp.where(less_x, cface_ref[c : c + 1], 0.0)
            internal = force_ref[c, i] + jnp.where(
                first_sub, jnp.broadcast_to(edge, (columns, layers)), 0.0
            )
            if i == 0:
                internal = internal + jnp.where(less_x, xface_ref[c], 0.0)
            velocity = velocity_ref[c, i] + factor * (external_ref[c, i] - internal)
            velocity_out[c, i] = velocity
            disp_out[c, i] = disp_ref[c, i] + STEP * velocity


def shape(*dims, dtype=F32):
    return jax.ShapeDtypeStruct(dims, dtype)


def on_device(
    displacement, velocity, external_force, node_mass, stiffness, cloak_list, micro_state,
    localization, modes, point_weight, point_modulus, softening,
):
    rows, columns, layers = stiffness.shape
    points, count = modes.shape
    most = cloak_list.shape[2]
    gx, gy = lax.axis_size("gx"), lax.axis_size("gy")
    along_x = [((i + 1) % gx, i) for i in range(gx)]
    along_y = [((j + 1) % gy, j) for j in range(gy)]
    both = [((i + 1) % gx * gy + (j + 1) % gy, i * gy + j) for i in range(gx) for j in range(gy)]
    back = lambda pairs: [(b, a) for a, b in pairs]
    group = 8
    xhalo, yhalo, corner = pl.pallas_call(
        edges_kernel,
        out_shape=(shape(3, columns, layers), shape(3, rows, layers), shape(3, layers)),
        in_specs=[VMEM],
        out_specs=(VMEM,) * 3,
        compiler_params=pltpu.CompilerParams(vmem_limit_bytes=4 * 2**20),
        cost_estimate=pl.CostEstimate(flops=10**10, bytes_accessed=10**6, transcendentals=0),
    )(displacement)
    xhalo = lax.ppermute(xhalo, "gx", along_x)
    yhalo = lax.ppermute(yhalo, "gy", along_y)
    corner = lax.ppermute(corner, ("gx", "gy"), both)

    order_shape = shape(8, (most + 2 + 127) // 128 * 128, dtype=jnp.int32)
    *matrices, order = pl.pallas_call(
        functools.partial(matrices_kernel, rows, columns),
        out_shape=tuple(shape(n, points, dtype=BF16) for n in (2 * count, 2 * count, points, points))
        + (shape(points, 2 * count, dtype=BF16), shape(16, points, dtype=BF16), order_shape),
        in_specs=[VMEM] * 6,
        out_specs=(VMEM,) * 7,
        scratch_shapes=[pltpu.VMEM((16, points), F32), pltpu.VMEM(order_shape.shape, jnp.int32)],
        compiler_params=pltpu.CompilerParams(vmem_limit_bytes=16 * 2**20),
        cost_estimate=pl.CostEstimate(flops=10**10, bytes_accessed=10**6, transcendentals=0),
    )(
        modes, localization.T, point_weight.reshape(1, points), point_modulus.reshape(1, points),
        softening.reshape(1, points), cloak_list[0],
    )

    groups = most // group
    states = micro_state.reshape(count * most, layers)
    strain_shape = shape(rows * columns * 8, layers)
    stress_shape = shape(rows * columns * 8 + 8, layers)
    xface, yface, cface, strain, stress, done = pl.pallas_call(
        functools.partial(edge_kernel, group, most),
        out_shape=(
            shape(3, columns, layers), shape(3, rows, layers), shape(3, layers),
            strain_shape, stress_shape, shape(most * count, layers),
        ),
        in_specs=[VMEM] * 13,
        out_specs=(VMEM,) * 6,
        scratch_shapes=[pltpu.SMEM(order_shape.shape, jnp.int32), pltpu.SemaphoreType.DMA],
        compiler_params=pltpu.CompilerParams(vmem_limit_bytes=30 * 2**20),
        cost_estimate=pl.CostEstimate(flops=10**10, bytes_accessed=10**7, transcendentals=0),
    )(order, displacement, xhalo, yhalo, corner, stiffness, states, *matrices)

    xface = lax.ppermute(xface, "gx", back(along_x))
    yface = lax.ppermute(yface, "gy", back(along_y))
    cface = lax.ppermute(cface, ("gx", "gy"), back(both))

    force, new_state = pl.pallas_call(
        functools.partial(inner_kernel, rows, columns),
        out_shape=(shape(3, rows, columns, layers), shape(count, most, layers)),
        in_specs=[VMEM] * 11,
        out_specs=(VMEM, HBM),
        scratch_shapes=[
            pltpu.VMEM(stress_shape.shape, F32), pltpu.VMEM((groups, count, group, layers), F32),
            pltpu.SemaphoreType.DMA((groups,)),
            pltpu.SMEM(order_shape.shape, jnp.int32), pltpu.SemaphoreType.DMA,
        ],
        compiler_params=pltpu.CompilerParams(vmem_limit_bytes=30 * 2**20),
        cost_estimate=pl.CostEstimate(flops=2 * 10**10, bytes_accessed=10**7, transcendentals=0),
    )(order, states, strain, stress, done, *matrices)

    displacement_next, velocity_next = pl.pallas_call(
        update_kernel,
        out_shape=(shape(3, rows, columns, layers),) * 2,
        in_specs=[VMEM] * 8,
        out_specs=(VMEM,) * 2,
        compiler_params=pltpu.CompilerParams(vmem_limit_bytes=16 * 2**20),
    )(displacement, velocity, external_force, node_mass, force, xface, yface, cface)
    return displacement_next, velocity_next, new_state.reshape(micro_state.shape)


def solution(mesh):
    field = P(None, "gx", "gy", None)
    grid = P("gx", "gy", None)
    state = P("gx", "gy", None, None, None)
    in_specs = (field, field, field, grid, grid, P("gx", None, None), state, P(), P(), P(), P(), P())
    return jax.shard_map(
        on_device, mesh=mesh, in_specs=in_specs, out_specs=(field, field, state), check_vma=False
    )
```

```python
import functools

import jax
import jax.numpy as jnp
from jax import lax
from jax.experimental import pallas as pl
from jax.experimental.pallas import tpu as pltpu
from jax.sharding import PartitionSpec as P

ITERS = 3
STEP = 0.25
HIGHEST = lax.Precision.HIGHEST
F32 = jnp.float32
BF16 = jnp.bfloat16
VMEM = pl.BlockSpec(memory_space=pltpu.VMEM)
HBM = pl.BlockSpec(memory_space=pltpu.HBM)


def split(x):
    high = x.astype(BF16)
    return high, (x - high.astype(F32)).astype(BF16)


def dot(a, b):
    return jnp.dot(a, b, preferred_element_type=F32)


def exact(a, b):
    return jnp.dot(a, b, precision=HIGHEST, preferred_element_type=F32)


def transposed_product(a, b):
    terms = []
    for x in (a, b):
        one = x.astype(BF16).astype(F32)
        two = (x - one).astype(BF16).astype(F32)
        terms.append((one, two, x - one - two))
    (a1, a2, a3), (b1, b2, b3) = terms
    left = jnp.concatenate([a1, a1, a2, a2, a1, a3], axis=0).astype(BF16)
    right = jnp.concatenate([b1, b2, b1, b2, b3, b1], axis=0).astype(BF16)
    return lax.dot_general(left, right, (((0,), (0,)), ((), ())), preferred_element_type=F32)


def lane_of(x, k):
    return jnp.take_along_axis(x, jnp.full(x.shape, k, jnp.int32), axis=1, mode="promise_in_bounds")


def row_of(x, s):
    return jnp.take_along_axis(x, jnp.full(x.shape, s, jnp.int32), axis=0, mode="promise_in_bounds")


def invert_two(a, b, c):
    scale = 1.0 / (a * c - b * b)
    return c * scale, -(b * scale), a * scale


def inverse(matrix):
    size = matrix.shape[0]
    tile = (8, size)
    count = size // 8
    blocks = [matrix[i : i + 8] for i in range(0, size, 8)]
    lane = lax.broadcasted_iota(jnp.int32, tile, 1)
    row = lax.broadcasted_iota(jnp.int32, tile, 0)

    def spread(x, s):
        return jnp.broadcast_to(x[s : s + 1, :], tile)

    for b in range(count):
        before = panel = blocks[b]
        for s in range(0, 8, 4):
            k = b * 8 + s
            lanes4 = jnp.logical_and(lane >= k, lane < k + 4)
            rows4 = jnp.logical_and(row >= s, row < s + 4)
            c = [lane_of(panel, k + i) for i in range(4)]
            r = [
                jnp.where(lane == k + i, 1.0, jnp.where(lanes4, 0.0, spread(panel, s + i)))
                for i in range(4)
            ]
            p = [[row_of(c[j], s + i) for j in range(i + 1)] for i in range(4)]
            (b00, b01), (b10, b11) = p[2][:2], p[3][:2]
            i00, i10, i11 = invert_two(p[0][0], p[1][0], p[1][1])
            w00, w01 = b00 * i00 + b01 * i10, b00 * i10 + b01 * i11
            w10, w11 = b10 * i00 + b11 * i10, b10 * i10 + b11 * i11
            j00, j10, j11 = invert_two(
                p[2][2] - (w00 * b00 + w01 * b01),
                p[3][2] - (w10 * b00 + w11 * b01),
                p[3][3] - (w10 * b10 + w11 * b11),
            )
            y2 = r[2] - (w00 * r[0] + w01 * r[1])
            y3 = r[3] - (w10 * r[0] + w11 * r[1])
            n2, n3 = j00 * y2 + j10 * y3, j10 * y2 + j11 * y3
            n0 = (i00 * r[0] + i10 * r[1]) - (w00 * n2 + w10 * n3)
            n1 = (i10 * r[0] + i11 * r[1]) - (w01 * n2 + w11 * n3)
            f = [jnp.where(row == s + i, -1.0, jnp.where(rows4, 0.0, c[i])) for i in range(4)]
            rest = jnp.where(jnp.logical_or(lanes4, rows4), 0.0, panel)
            panel = rest - ((f[0] * n0 + f[1] * n1) + (f[2] * n2 + f[3] * n3))
        inside = jnp.logical_and(lane >= b * 8, lane < b * 8 + 8)
        panel = jnp.where(inside, -panel, panel)
        change = transposed_product(before, panel)
        for i in range(count):
            old = blocks[i]
            kept = jnp.where(inside, 0.0, old)
            if i == b:
                blocks[i] = panel
            elif i == b + 1:
                t = [lane_of(old, b * 8 + s) * spread(panel, s) for s in range(8)]
                blocks[i] = kept - (((t[0] + t[1]) + (t[2] + t[3])) + ((t[4] + t[5]) + (t[6] + t[7])))
            else:
                blocks[i] = kept - change[i * 8 : i * 8 + 8]
    return -jnp.concatenate(blocks, axis=0)


def near(a, b):
    (ah, al), (bh, bl) = split(a), split(b)
    return dot(ah, bh) + dot(al, bh) + dot(ah, bl)


def order_entries(rows, columns, lists_ref, order_ref, line):
    most = lists_ref.shape[1]
    width = order_ref.shape[1]
    tile = order_ref.shape
    line[...] = jnp.full(line.shape, -1, jnp.int32)
    line[0:1, 0:most] = lists_ref[pl.ds(lax.axis_index("gy"), 1), :]
    pencil = jnp.broadcast_to(line[0:1, :].astype(F32), tile)
    lane = lax.broadcasted_iota(jnp.int32, tile, 1)
    row = lax.broadcasted_iota(jnp.int32, tile, 0)
    column = pencil - columns * jnp.floor((pencil + 0.5) / columns)
    listed = pencil >= 0.0
    face = jnp.logical_or(pencil >= (rows - 1) * columns, column == columns - 1)
    kind = jnp.where(listed, jnp.where(face, 0, 1), jnp.where(lane < most, 2, 3))
    flags = jnp.where(kind == row, 1.0, 0.0).astype(BF16)
    square = (width, width)
    first = lax.broadcasted_iota(jnp.int32, square, 0)
    second = lax.broadcasted_iota(jnp.int32, square, 1)
    before = dot(flags, (first < second).astype(F32).astype(BF16))
    totals = dot(flags, jnp.ones(square, BF16))
    faces, number = totals[0:1], totals[0:1] + totals[1:2]
    kind = kind[0:1]
    place = jnp.where(
        kind == 0, before[0:1],
        jnp.where(kind == 1, faces + before[1:2], jnp.where(kind == 2, number + before[2:3], -1.0)),
    )
    moves = (jnp.broadcast_to(place, square) == first.astype(F32)).astype(F32)
    values = jnp.where(row == 0, lane.astype(F32), pencil)
    ordered = lax.dot_general(
        values, moves, (((1,), (1,)), ((), ())), precision=HIGHEST, preferred_element_type=F32
    )
    counts = jnp.where(lane == most, jnp.broadcast_to(faces, tile), jnp.broadcast_to(number, tile))
    tail = jnp.logical_and(row == 0, lane >= most)
    order_ref[...] = jnp.where(tail, counts, ordered).astype(jnp.int32)


def matrices_kernel(
    rows, columns, modes_ref, local_ref, weight_ref, modulus_ref, soft_ref, lists_ref,
    start0_ref, start1_ref, high_ref, low_ref, back_ref, stress_ref, order_ref, wide, line,
):
    order_entries(rows, columns, lists_ref, order_ref, line)
    points, count = modes_ref.shape
    modes = modes_ref[...]
    modes_t = modes.T
    weight = weight_ref[...] / points
    modulus = modulus_ref[...]
    root = jnp.sqrt(soft_ref[...])
    scale = weight * modulus / root
    inverted = inverse(exact(modes_t * (weight * modulus), modes))
    wide[...] = jnp.zeros_like(wide)
    wide[0 : local_ref.shape[0], :] = local_ref[...]
    local = wide[...]
    stress_ref[...] = (local * scale).astype(BF16)
    high, low = split(modes_t * root)
    start0_ref[0:count] = high
    start0_ref[count:] = high
    start1_ref[0:count] = low
    soft_local = local[0:8] * root
    local_high = soft_local.astype(BF16).astype(F32)
    part = [local_high, local_high, soft_local - local_high, jnp.zeros_like(local_high)]
    start1_ref[count:] = jnp.concatenate(part * (count // 32), axis=0).astype(BF16)
    back = near((modes_t * scale).T, inverted)
    high, low = split(back)
    back_ref[:, 0:count] = high
    back_ref[:, count:] = low
    newton = near(back, modes_t * root)
    high, low = split(newton)
    high_ref[...] = high
    low_ref[...] = low


def respond(u):
    return u * lax.rsqrt(1.0 + u * u)


def cells(states, strains, start0, start1, newton_high, newton_low, back, stress_m):
    layers = states[0].shape[1]
    count = states[0].shape[0]
    number = len(states)
    part = min(2, number)
    turned = [state.T for state in states]
    place = lax.broadcasted_iota(jnp.int32, (layers, count), 1) // 32
    strain_parts = []
    each = count // 32
    for q in range(0, number, each):
        rows = []
        for strain in strains[q : q + each]:
            high = strain.astype(BF16).astype(F32)
            rows += [high, strain - high, high, jnp.zeros_like(high)]
        rows = jnp.concatenate(rows, axis=0).T
        strain_parts += [jnp.where(place == g, rows, 0.0).astype(BF16) for g in range(each)]
    new_states, stresses = [None] * number, [None] * number

    def chunk(c):
        high, low = split(jnp.concatenate(turned[c : c + part], axis=0))
        strain = jnp.concatenate(strain_parts[c : c + part], axis=0)
        start = dot(jnp.concatenate([high, low], axis=1), start0)
        start = start + dot(jnp.concatenate([high, strain], axis=1), start1)
        u = start
        yield
        for step in range(ITERS - 1):
            high, low = split(respond(u))
            u = u - (dot(high, newton_high) + dot(low, newton_high) + dot(high, newton_low))
            yield
        h = respond(u)
        last = u - dot(h.astype(BF16), newton_high)
        high, low = split(start - u + h)
        both = dot(high, back)
        change = both[:, 0:count] + both[:, count:] + dot(low, back[:, 0:count])
        yield
        stress = lax.dot_general(
            stress_m, respond(last).astype(BF16), (((1,), (1,)), ((), ())), preferred_element_type=F32
        )
        for g in range(part):
            rows = slice(g * layers, (g + 1) * layers)
            new_states[c + g] = states[c + g] - change[rows].T
            stresses[c + g] = stress[0:8, rows]
        yield

    chunks = [chunk(c) for c in range(0, number, part)]
    for stage in range(ITERS + 2):
        for c in chunks:
            next(c)
    return new_states, stresses


def set_pencil(ref, entry, value):
    groups, count, group, layers = ref.shape
    place = lax.div(entry, group) * (count * group) + lax.rem(entry, group)
    ref.reshape(groups * count * group, layers)[pl.ds(place, count, stride=group), :] = value


def run_group(base, group, order_ref, state_ref, strain_ref, weights, stress_s, spare):
    count = weights[4].shape[1] // 2
    most = state_ref.shape[0] // count
    entries = [order_ref[0, base + g] for g in range(group)]
    pencils = [order_ref[1, base + g] for g in range(group)]
    states = [state_ref[pl.ds(e, count, stride=most), :] for e in entries]
    strains = [
        strain_ref[pl.ds(pl.multiple_of(jnp.maximum(p, 0) * 8, 8), 8), :] for p in pencils
    ]
    new_states, stresses = cells(states, strains, *(w[...] for w in weights))
    for g in range(group):
        spot = jnp.where(pencils[g] >= 0, pencils[g], spare)
        stress_s[pl.ds(pl.multiple_of(spot * 8, 8), 8), :] = stresses[g]
    return entries, [jnp.where(p >= 0, a, 0.0) for p, a in zip(pencils, new_states)]


def fluxes(s, side_mean, side_diff):
    lane_zero = lax.broadcasted_iota(jnp.int32, s[0].shape, 1) == 0

    def along(v):
        down = jnp.where(lane_zero, 0.0, pltpu.roll(v, 1, 1))
        return 0.5 * (v + down), v - down

    first = [along(side_mean(s[c]))[0] for c in (0, 5, 4)]
    second = [along(side_diff(s[c]))[0] for c in (5, 1, 3)]
    third = [along(side_mean(s[c]))[1] for c in (4, 3, 2)]
    half = [0.5 * (second[c] + third[c]) for c in range(3)]
    return [(first[c] + half[c], half[c] - first[c]) for c in range(3)]


def row_fluxes(stress_ref, i, columns):
    s = [stress_ref[pl.ds(i * columns * 8 + c, columns, stride=8), :] for c in range(6)]
    first_sub = lax.broadcasted_iota(jnp.int32, s[0].shape, 0) == 0

    def shift(v):
        return jnp.where(first_sub, 0.0, pltpu.roll(v, 1, 0))

    return fluxes(s, lambda v: 0.5 * (v + shift(v)), lambda v: v - shift(v))


def first_groups(order_ref, most, group):
    return lax.div(order_ref[0, most] + (group - 1), group)


def edges_kernel(disp_ref, xface_ref, yface_ref, corner_ref):
    for c in range(3):
        xface_ref[c] = disp_ref[c, 0]
        yface_ref[c] = disp_ref[c, :, 0, :]
        corner_ref[c : c + 1] = disp_ref[c, 0, 0:1]


def edge_kernel(
    group, most, order_vmem, disp_ref, xhalo_ref, yhalo_ref, corner_ref, stiff_ref, state_ref,
    start0_ref, start1_ref, high_ref, low_ref, back_ref, stress_ref,
    xface_ref, yface_ref, cface_ref, strain_ref, stress_out, done_ref,
    order_ref, order_sem,
):
    order_copy = pltpu.make_async_copy(order_vmem, order_ref, order_sem)
    order_copy.start()
    rows, columns, layers = stiff_ref.shape
    count = state_ref.shape[0] // most
    weights = (start0_ref, start1_ref, high_ref, low_ref, back_ref, stress_ref)
    tile = (columns, layers)
    lane = lax.broadcasted_iota(jnp.int32, tile, 1)
    sub = lax.broadcasted_iota(jnp.int32, tile, 0)
    last_lane = lane == layers - 1
    last_sub = sub == columns - 1

    more_x = lax.axis_index("gx") < lax.axis_size("gx") - 1
    more_y = lax.axis_index("gy") < lax.axis_size("gy") - 1

    def node_row(c, i):
        own = disp_ref[c, i] if i < rows else jnp.where(more_x, xhalo_ref[c], 0.0)
        edge = yhalo_ref[c, i : i + 1] if i < rows else jnp.where(more_x, corner_ref[c : c + 1], 0.0)
        edge = jnp.where(more_y, edge, 0.0)
        up = jnp.where(last_sub, jnp.broadcast_to(edge, tile), pltpu.roll(own, columns - 1, 0))
        mean, diff = 0.5 * (up + own), up - own
        mean_up = jnp.where(last_lane, 0.0, pltpu.roll(mean, layers - 1, 1))
        diff_up = jnp.where(last_lane, 0.0, pltpu.roll(diff, layers - 1, 1))
        return 0.5 * (mean_up + mean), 0.5 * (diff_up + diff), mean_up - mean

    lower = [node_row(c, 0) for c in range(3)]
    zero_tile = jnp.zeros(tile, F32)
    for i in range(rows):
        upper = [node_row(c, i + 1) for c in range(3)]
        g = [
            (upper[c][0] - lower[c][0], 0.5 * (upper[c][1] + lower[c][1]), 0.5 * (upper[c][2] + lower[c][2]))
            for c in range(3)
        ]
        lower = upper
        strain = [g[0][0], g[1][1], g[2][2], g[1][2] + g[2][1], g[0][2] + g[2][0], g[0][1] + g[1][0]]
        stiffness = stiff_ref[i]
        volume = strain[0] + strain[1] + strain[2]
        for c in range(8):
            place = pl.ds(i * columns * 8 + c, columns, stride=8)
            if c >= 6:
                strain_ref[place, :] = zero_tile
                continue
            strain_ref[place, :] = strain[c]
            stress_out[place, :] = stiffness * (volume + 2.0 * strain[c] if c < 3 else strain[c])

    order_copy.wait()

    def body(q, carry):
        _, states = run_group(
            q * group, group, order_ref, state_ref, strain_ref, weights, stress_out, rows * columns
        )
        for g in range(group):
            done_ref[pl.ds(pl.multiple_of((q * group + g) * count, count), count), :] = states[g]
        return carry

    lax.fori_loop(0, first_groups(order_ref, most, group), body, 0)

    last = row_fluxes(stress_out, rows - 1, columns)
    for c in range(3):
        xface_ref[c] = -last[c][1]
    s = [stress_out[pl.ds((columns - 1) * 8 + c, rows, stride=columns * 8), :] for c in range(6)]
    side = fluxes(s, lambda v: 0.5 * v, lambda v: -v)
    for c in range(3):
        yface_ref[c] = -side[c][0]
        yface_ref[c, 1:rows] = yface_ref[c, 1:rows] - side[c][1][0 : rows - 1]
        cface_ref[c : c + 1] = -side[c][1][rows - 1 : rows]


def inner_kernel(
    rows, columns, order_vmem, state_ref, strain_ref, stress_in, done_ref,
    start0_ref, start1_ref, high_ref, low_ref, back_ref, stress_ref,
    force_ref, out_hbm,
    stress_s, out_s, sems, order_ref, order_sem,
):
    order_copy = pltpu.make_async_copy(order_vmem, order_ref, order_sem)
    order_copy.start()
    groups, count, group, layers = out_s.shape
    most = groups * group
    weights = (start0_ref, start1_ref, high_ref, low_ref, back_ref, stress_ref)
    stress_s[...] = stress_in[...]
    order_copy.wait()
    before = first_groups(order_ref, most, group)
    after = lax.div(order_ref[0, most + 1] + (group - 1), group)

    def store(q):
        return pltpu.make_async_copy(
            out_s.at[q], out_hbm.at[:, pl.ds(q * group, group), :], sems.at[q]
        )

    def copy(q, carry):
        for g in range(group):
            place = q * group + g
            set_pencil(
                out_s, order_ref[0, place],
                done_ref[pl.ds(pl.multiple_of(place * count, count), count), :],
            )
        return carry

    def clear(q, carry):
        for g in range(group):
            set_pencil(out_s, order_ref[0, q * group + g], jnp.zeros((count, layers), F32))
        return carry

    lax.fori_loop(0, before, copy, 0)
    lax.fori_loop(jnp.maximum(before, after), groups, clear, 0)

    def body(q, sent):
        entries, states = run_group(
            q * group, group, order_ref, state_ref, strain_ref, weights, stress_s, rows * columns
        )
        for g in range(group):
            set_pencil(out_s, entries[g], states[g])
        whole = jnp.maximum(sent, lax.div(entries[group - 1] + 1, group))

        def send(chunk, carry):
            store(chunk).start()
            return carry

        lax.fori_loop(sent, whole, send, 0)
        return whole

    sent = lax.fori_loop(before, after, body, 0)

    def send(chunk, carry):
        store(chunk).start()
        return carry

    lax.fori_loop(sent, groups, send, 0)

    below = None
    for i in range(rows):
        here = row_fluxes(stress_s, i, columns)
        for c in range(3):
            force_ref[c, i] = -here[c][0] if below is None else -(here[c][0] + below[c][1])
        below = here
    for q in range(groups):
        store(q).wait()


def update_kernel(
    disp_ref, velocity_ref, external_ref, mass_ref, force_ref, xface_ref, yface_ref, cface_ref,
    disp_hbm, velocity_hbm, disp_out, velocity_out, sems,
):
    rows, columns, layers = mass_ref.shape
    tile = (columns, layers)
    less_x = lax.axis_index("gx") > 0
    first_sub = lax.broadcasted_iota(jnp.int32, tile, 0) == 0
    first_sub = jnp.logical_and(first_sub, lax.axis_index("gy") > 0)
    factors = [STEP / mass_ref[i] for i in range(rows)]
    copies = []
    for c in range(3):
        for i in range(rows):
            edge = yface_ref[c, i : i + 1]
            if i == 0:
                edge = edge + jnp.where(less_x, cface_ref[c : c + 1], 0.0)
            internal = force_ref[c, i] + jnp.where(first_sub, jnp.broadcast_to(edge, tile), 0.0)
            if i == 0:
                internal = internal + jnp.where(less_x, xface_ref[c], 0.0)
            velocity = velocity_ref[c, i] + factors[i] * (external_ref[c, i] - internal)
            velocity_out[c, i] = velocity
            disp_out[c, i] = disp_ref[c, i] + STEP * velocity
        for n, (ours, whole) in enumerate(((velocity_out, velocity_hbm), (disp_out, disp_hbm))):
            copies.append(pltpu.make_async_copy(ours.at[c], whole.at[c], sems.at[n, c]))
            copies[-1].start()
    for copy in copies:
        copy.wait()


def shape(*dims, dtype=F32):
    return jax.ShapeDtypeStruct(dims, dtype)


def on_device(
    displacement, velocity, external_force, node_mass, stiffness, cloak_list, micro_state,
    localization, modes, point_weight, point_modulus, softening,
):
    rows, columns, layers = stiffness.shape
    points, count = modes.shape
    most = cloak_list.shape[2]
    gx, gy = lax.axis_size("gx"), lax.axis_size("gy")
    along_x = [((i + 1) % gx, i) for i in range(gx)]
    along_y = [((j + 1) % gy, j) for j in range(gy)]
    both = [((i + 1) % gx * gy + (j + 1) % gy, i * gy + j) for i in range(gx) for j in range(gy)]
    back = lambda pairs: [(b, a) for a, b in pairs]
    group = 8
    xhalo, yhalo, corner = pl.pallas_call(
        edges_kernel,
        out_shape=(shape(3, columns, layers), shape(3, rows, layers), shape(3, layers)),
        in_specs=[VMEM],
        out_specs=(VMEM,) * 3,
        compiler_params=pltpu.CompilerParams(vmem_limit_bytes=4 * 2**20),
        cost_estimate=pl.CostEstimate(flops=10**10, bytes_accessed=10**6, transcendentals=0),
    )(displacement)
    xhalo = lax.ppermute(xhalo, "gx", along_x)
    yhalo = lax.ppermute(yhalo, "gy", along_y)
    corner = lax.ppermute(corner, ("gx", "gy"), both)

    order_shape = shape(8, (most + 2 + 127) // 128 * 128, dtype=jnp.int32)
    *matrices, order = pl.pallas_call(
        functools.partial(matrices_kernel, rows, columns),
        out_shape=tuple(shape(n, points, dtype=BF16) for n in (2 * count, 2 * count, points, points))
        + (shape(points, 2 * count, dtype=BF16), shape(16, points, dtype=BF16), order_shape),
        in_specs=[VMEM] * 6,
        out_specs=(VMEM,) * 7,
        scratch_shapes=[pltpu.VMEM((16, points), F32), pltpu.VMEM(order_shape.shape, jnp.int32)],
        compiler_params=pltpu.CompilerParams(vmem_limit_bytes=16 * 2**20),
        cost_estimate=pl.CostEstimate(flops=10**10, bytes_accessed=10**6, transcendentals=0),
    )(
        modes, localization.T, point_weight.reshape(1, points), point_modulus.reshape(1, points),
        softening.reshape(1, points), cloak_list[0],
    )

    groups = most // group
    states = micro_state.reshape(count * most, layers)
    strain_shape = shape(rows * columns * 8, layers)
    stress_shape = shape(rows * columns * 8 + 8, layers)
    xface, yface, cface, strain, stress, done = pl.pallas_call(
        functools.partial(edge_kernel, group, most),
        out_shape=(
            shape(3, columns, layers), shape(3, rows, layers), shape(3, layers),
            strain_shape, stress_shape, shape(most * count, layers),
        ),
        in_specs=[VMEM] * 13,
        out_specs=(VMEM,) * 6,
        scratch_shapes=[pltpu.SMEM(order_shape.shape, jnp.int32), pltpu.SemaphoreType.DMA],
        compiler_params=pltpu.CompilerParams(vmem_limit_bytes=30 * 2**20),
        cost_estimate=pl.CostEstimate(flops=10**10, bytes_accessed=10**7, transcendentals=0),
    )(order, displacement, xhalo, yhalo, corner, stiffness, states, *matrices)

    xface = lax.ppermute(xface, "gx", back(along_x))
    yface = lax.ppermute(yface, "gy", back(along_y))
    cface = lax.ppermute(cface, ("gx", "gy"), back(both))

    force, new_state = pl.pallas_call(
        functools.partial(inner_kernel, rows, columns),
        out_shape=(shape(3, rows, columns, layers), shape(count, most, layers)),
        in_specs=[VMEM] * 11,
        out_specs=(VMEM, HBM),
        scratch_shapes=[
            pltpu.VMEM(stress_shape.shape, F32), pltpu.VMEM((groups, count, group, layers), F32),
            pltpu.SemaphoreType.DMA((groups,)),
            pltpu.SMEM(order_shape.shape, jnp.int32), pltpu.SemaphoreType.DMA,
        ],
        compiler_params=pltpu.CompilerParams(vmem_limit_bytes=30 * 2**20),
        cost_estimate=pl.CostEstimate(flops=2 * 10**10, bytes_accessed=10**7, transcendentals=0),
    )(order, states, strain, stress, done, *matrices)

    displacement_next, velocity_next = pl.pallas_call(
        update_kernel,
        out_shape=(shape(3, rows, columns, layers),) * 2,
        in_specs=[VMEM] * 8,
        out_specs=(HBM,) * 2,
        scratch_shapes=[pltpu.VMEM(displacement.shape, F32)] * 2 + [pltpu.SemaphoreType.DMA((2, 3))],
        compiler_params=pltpu.CompilerParams(vmem_limit_bytes=16 * 2**20),
    )(displacement, velocity, external_force, node_mass, force, xface, yface, cface)
    return displacement_next, velocity_next, new_state.reshape(micro_state.shape)


def solution(mesh):
    field = P(None, "gx", "gy", None)
    grid = P("gx", "gy", None)
    state = P("gx", "gy", None, None, None)
    in_specs = (field, field, field, grid, grid, P("gx", None, None), state, P(), P(), P(), P(), P())
    return jax.shard_map(
        on_device, mesh=mesh, in_specs=in_specs, out_specs=(field, field, state), check_vma=False
    )
```

```python
import functools

import jax
import jax.numpy as jnp
from jax import lax
from jax.experimental import pallas as pl
from jax.experimental.pallas import tpu as pltpu
from jax.sharding import PartitionSpec as P

ITERS = 3
STEP = 0.25
HIGHEST = lax.Precision.HIGHEST
F32 = jnp.float32
BF16 = jnp.bfloat16
VMEM = pl.BlockSpec(memory_space=pltpu.VMEM)
HBM = pl.BlockSpec(memory_space=pltpu.HBM)


def split(x):
    high = x.astype(BF16)
    return high, (x - high.astype(F32)).astype(BF16)


def dot(a, b):
    return jnp.dot(a, b, preferred_element_type=F32)


def exact(a, b):
    return jnp.dot(a, b, precision=HIGHEST, preferred_element_type=F32)


def transposed_product(a, b):
    terms = []
    for x in (a, b):
        one = x.astype(BF16).astype(F32)
        two = (x - one).astype(BF16).astype(F32)
        terms.append((one, two, x - one - two))
    (a1, a2, a3), (b1, b2, b3) = terms
    left = jnp.concatenate([a1, a1, a2, a2, a1, a3], axis=0).astype(BF16)
    right = jnp.concatenate([b1, b2, b1, b2, b3, b1], axis=0).astype(BF16)
    return lax.dot_general(left, right, (((0,), (0,)), ((), ())), preferred_element_type=F32)


def lane_of(x, k):
    return jnp.take_along_axis(x, jnp.full(x.shape, k, jnp.int32), axis=1, mode="promise_in_bounds")


def row_of(x, s):
    return jnp.take_along_axis(x, jnp.full(x.shape, s, jnp.int32), axis=0, mode="promise_in_bounds")


def invert_two(a, b, c):
    scale = 1.0 / (a * c - b * b)
    return c * scale, -(b * scale), a * scale


def sweep(blocks, first, last):
    tile = blocks[0].shape
    size = tile[1]
    count = len(blocks)
    lane = lax.broadcasted_iota(jnp.int32, tile, 1)
    row = lax.broadcasted_iota(jnp.int32, tile, 0)

    def spread(x, s):
        return jnp.broadcast_to(x[s : s + 1, :], tile)

    for b in range(first, last):
        before = panel = blocks[b]
        for s in range(0, 8, 4):
            k = b * 8 + s
            lanes4 = jnp.logical_and(lane >= k, lane < k + 4)
            rows4 = jnp.logical_and(row >= s, row < s + 4)
            c = [lane_of(panel, k + i) for i in range(4)]
            r = [
                jnp.where(lane == k + i, 1.0, jnp.where(lanes4, 0.0, spread(panel, s + i)))
                for i in range(4)
            ]
            p = [[row_of(c[j], s + i) for j in range(i + 1)] for i in range(4)]
            (b00, b01), (b10, b11) = p[2][:2], p[3][:2]
            i00, i10, i11 = invert_two(p[0][0], p[1][0], p[1][1])
            w00, w01 = b00 * i00 + b01 * i10, b00 * i10 + b01 * i11
            w10, w11 = b10 * i00 + b11 * i10, b10 * i10 + b11 * i11
            j00, j10, j11 = invert_two(
                p[2][2] - (w00 * b00 + w01 * b01),
                p[3][2] - (w10 * b00 + w11 * b01),
                p[3][3] - (w10 * b10 + w11 * b11),
            )
            y2 = r[2] - (w00 * r[0] + w01 * r[1])
            y3 = r[3] - (w10 * r[0] + w11 * r[1])
            n2, n3 = j00 * y2 + j10 * y3, j10 * y2 + j11 * y3
            n0 = (i00 * r[0] + i10 * r[1]) - (w00 * n2 + w10 * n3)
            n1 = (i10 * r[0] + i11 * r[1]) - (w01 * n2 + w11 * n3)
            f = [jnp.where(row == s + i, -1.0, jnp.where(rows4, 0.0, c[i])) for i in range(4)]
            rest = jnp.where(jnp.logical_or(lanes4, rows4), 0.0, panel)
            panel = rest - ((f[0] * n0 + f[1] * n1) + (f[2] * n2 + f[3] * n3))
        inside = jnp.logical_and(lane >= b * 8, lane < b * 8 + 8)
        panel = jnp.where(inside, -panel, panel)
        change = transposed_product(before, panel)
        for i in range(count):
            old = blocks[i]
            kept = jnp.where(inside, 0.0, old)
            if i == b:
                blocks[i] = panel
            elif i == b + 1:
                t = [lane_of(old, b * 8 + s) * spread(panel, s) for s in range(8)]
                blocks[i] = kept - (((t[0] + t[1]) + (t[2] + t[3])) + ((t[4] + t[5]) + (t[6] + t[7])))
            else:
                blocks[i] = kept - change[i * 8 : i * 8 + 8]
    return jnp.concatenate(blocks, axis=0)


def near(a, b):
    (ah, al), (bh, bl) = split(a), split(b)
    return dot(ah, bh) + dot(al, bh) + dot(ah, bl)


def order_entries(rows, columns, lists_ref, order_ref, line):
    most = lists_ref.shape[1]
    width = order_ref.shape[1]
    tile = order_ref.shape
    line[...] = jnp.full(line.shape, -1, jnp.int32)
    line[0:1, 0:most] = lists_ref[pl.ds(lax.axis_index("gy"), 1), :]
    pencil = jnp.broadcast_to(line[0:1, :].astype(F32), tile)
    lane = lax.broadcasted_iota(jnp.int32, tile, 1)
    row = lax.broadcasted_iota(jnp.int32, tile, 0)
    column = pencil - columns * jnp.floor((pencil + 0.5) / columns)
    listed = pencil >= 0.0
    face = jnp.logical_or(pencil >= (rows - 1) * columns, column == columns - 1)
    kind = jnp.where(listed, jnp.where(face, 0, 1), jnp.where(lane < most, 2, 3))
    flags = jnp.where(kind == row, 1.0, 0.0).astype(BF16)
    square = (width, width)
    first = lax.broadcasted_iota(jnp.int32, square, 0)
    second = lax.broadcasted_iota(jnp.int32, square, 1)
    before = dot(flags, (first < second).astype(F32).astype(BF16))
    totals = dot(flags, jnp.ones(square, BF16))
    faces, number = totals[0:1], totals[0:1] + totals[1:2]
    kind = kind[0:1]
    place = jnp.where(
        kind == 0, before[0:1],
        jnp.where(kind == 1, faces + before[1:2], jnp.where(kind == 2, number + before[2:3], -1.0)),
    )
    moves = (jnp.broadcast_to(place, square) == first.astype(F32)).astype(F32)
    values = jnp.where(row == 0, lane.astype(F32), pencil)
    ordered = lax.dot_general(
        values, moves, (((1,), (1,)), ((), ())), precision=HIGHEST, preferred_element_type=F32
    )
    counts = jnp.where(lane == most, jnp.broadcast_to(faces, tile), jnp.broadcast_to(number, tile))
    tail = jnp.logical_and(row == 0, lane >= most)
    order_ref[...] = jnp.where(tail, counts, ordered).astype(jnp.int32)


def row_blocks(matrix):
    return [matrix[i : i + 8] for i in range(0, matrix.shape[0], 8)]


def half_kernel(rows, columns, modes_ref, weight_ref, modulus_ref, lists_ref, half_ref, order_ref, line):
    order_entries(rows, columns, lists_ref, order_ref, line)
    points, count = modes_ref.shape
    modes = modes_ref[...]
    matrix = exact(modes.T * (weight_ref[...] / points * modulus_ref[...]), modes)
    half_ref[...] = sweep(row_blocks(matrix), 0, count // 16)


def matrices_kernel(
    half_ref, modes_ref, local_ref, weight_ref, modulus_ref, soft_ref,
    start0_ref, start1_ref, high_ref, low_ref, back_ref, stress_ref, wide,
):
    points, count = modes_ref.shape
    modes_t = modes_ref[...].T
    weight = weight_ref[...] / points
    modulus = modulus_ref[...]
    root = jnp.sqrt(soft_ref[...])
    scale = weight * modulus / root
    inverted = -sweep(row_blocks(half_ref[...]), count // 16, count // 8)
    wide[...] = jnp.zeros_like(wide)
    wide[0 : local_ref.shape[0], :] = local_ref[...]
    local = wide[...]
    stress_ref[...] = (local * scale).astype(BF16)
    high, low = split(modes_t * root)
    start0_ref[0:count] = high
    start0_ref[count:] = high
    start1_ref[0:count] = low
    soft_local = local[0:8] * root
    local_high = soft_local.astype(BF16).astype(F32)
    part = [local_high, local_high, soft_local - local_high, jnp.zeros_like(local_high)]
    start1_ref[count:] = jnp.concatenate(part * (count // 32), axis=0).astype(BF16)
    back = near((modes_t * scale).T, inverted)
    high, low = split(back)
    back_ref[:, 0:count] = high
    back_ref[:, count:] = low
    newton = near(back, modes_t * root)
    high, low = split(newton)
    high_ref[...] = high
    low_ref[...] = low


def respond(u):
    return u * lax.rsqrt(1.0 + u * u)


def cells(states, strains, start0, start1, newton_high, newton_low, back, stress_m):
    layers = states[0].shape[1]
    count = states[0].shape[0]
    number = len(states)
    part = min(2, number)
    turned = [state.T for state in states]
    place = lax.broadcasted_iota(jnp.int32, (layers, count), 1) // 32
    strain_parts = []
    each = count // 32
    for q in range(0, number, each):
        rows = []
        for strain in strains[q : q + each]:
            high = strain.astype(BF16).astype(F32)
            rows += [high, strain - high, high, jnp.zeros_like(high)]
        rows = jnp.concatenate(rows, axis=0).T
        strain_parts += [jnp.where(place == g, rows, 0.0).astype(BF16) for g in range(each)]
    new_states, stresses = [None] * number, [None] * number

    def chunk(c):
        high, low = split(jnp.concatenate(turned[c : c + part], axis=0))
        strain = jnp.concatenate(strain_parts[c : c + part], axis=0)
        start = dot(jnp.concatenate([high, low], axis=1), start0)
        start = start + dot(jnp.concatenate([high, strain], axis=1), start1)
        u = start
        yield
        for step in range(ITERS - 1):
            high, low = split(respond(u))
            u = u - (dot(high, newton_high) + dot(low, newton_high) + dot(high, newton_low))
            yield
        h = respond(u)
        last = u - dot(h.astype(BF16), newton_high)
        high, low = split(start - u + h)
        both = dot(high, back)
        change = both[:, 0:count] + both[:, count:] + dot(low, back[:, 0:count])
        yield
        stress = lax.dot_general(
            stress_m, respond(last).astype(BF16), (((1,), (1,)), ((), ())), preferred_element_type=F32
        )
        for g in range(part):
            rows = slice(g * layers, (g + 1) * layers)
            new_states[c + g] = states[c + g] - change[rows].T
            stresses[c + g] = stress[0:8, rows]
        yield

    chunks = [chunk(c) for c in range(0, number, part)]
    for stage in range(ITERS + 2):
        for c in chunks:
            next(c)
    return new_states, stresses


def set_pencil(ref, entry, value):
    groups, count, group, layers = ref.shape
    place = lax.div(entry, group) * (count * group) + lax.rem(entry, group)
    ref.reshape(groups * count * group, layers)[pl.ds(place, count, stride=group), :] = value


def run_group(base, group, order_ref, state_ref, strain_ref, weights, stress_s, spare):
    count = weights[4].shape[1] // 2
    most = state_ref.shape[0] // count
    entries = [order_ref[0, base + g] for g in range(group)]
    pencils = [order_ref[1, base + g] for g in range(group)]
    states = [state_ref[pl.ds(e, count, stride=most), :] for e in entries]
    strains = [
        strain_ref[pl.ds(pl.multiple_of(jnp.maximum(p, 0) * 8, 8), 8), :] for p in pencils
    ]
    new_states, stresses = cells(states, strains, *(w[...] for w in weights))
    for g in range(group):
        spot = jnp.where(pencils[g] >= 0, pencils[g], spare)
        stress_s[pl.ds(pl.multiple_of(spot * 8, 8), 8), :] = stresses[g]
    return entries, [jnp.where(p >= 0, a, 0.0) for p, a in zip(pencils, new_states)]


def fluxes(s, side_mean, side_diff):
    lane_zero = lax.broadcasted_iota(jnp.int32, s[0].shape, 1) == 0

    def along(v):
        down = jnp.where(lane_zero, 0.0, pltpu.roll(v, 1, 1))
        return 0.5 * (v + down), v - down

    first = [along(side_mean(s[c]))[0] for c in (0, 5, 4)]
    second = [along(side_diff(s[c]))[0] for c in (5, 1, 3)]
    third = [along(side_mean(s[c]))[1] for c in (4, 3, 2)]
    half = [0.5 * (second[c] + third[c]) for c in range(3)]
    return [(first[c] + half[c], half[c] - first[c]) for c in range(3)]


def row_fluxes(stress_ref, i, columns):
    s = [stress_ref[pl.ds(i * columns * 8 + c, columns, stride=8), :] for c in range(6)]
    first_sub = lax.broadcasted_iota(jnp.int32, s[0].shape, 0) == 0

    def shift(v):
        return jnp.where(first_sub, 0.0, pltpu.roll(v, 1, 0))

    return fluxes(s, lambda v: 0.5 * (v + shift(v)), lambda v: v - shift(v))


def first_groups(order_ref, most, group):
    return lax.div(order_ref[0, most] + (group - 1), group)


def column_kernel(disp_ref, column_ref):
    for c in range(3):
        column_ref[c] = disp_ref[c, :, 0, :]


def row_kernel(disp_ref, yhalo_ref, row_ref):
    columns = disp_ref.shape[2]
    for c in range(3):
        row_ref[c] = jnp.zeros(row_ref.shape[1:], F32)
        row_ref[c, 0:columns] = disp_ref[c, 0]
        row_ref[c, columns : columns + 1] = yhalo_ref[c, 0:1]


def edge_kernel(
    group, most, order_vmem, disp_ref, xhalo_ref, yhalo_ref, stiff_ref, state_ref,
    start0_ref, start1_ref, high_ref, low_ref, back_ref, stress_ref,
    xface_ref, yface_ref, cface_ref, strain_ref, stress_out, done_ref,
    order_ref, order_sem,
):
    order_copy = pltpu.make_async_copy(order_vmem, order_ref, order_sem)
    order_copy.start()
    rows, columns, layers = stiff_ref.shape
    count = state_ref.shape[0] // most
    weights = (start0_ref, start1_ref, high_ref, low_ref, back_ref, stress_ref)
    tile = (columns, layers)
    lane = lax.broadcasted_iota(jnp.int32, tile, 1)
    sub = lax.broadcasted_iota(jnp.int32, tile, 0)
    last_lane = lane == layers - 1
    last_sub = sub == columns - 1

    more_x = lax.axis_index("gx") < lax.axis_size("gx") - 1
    more_y = lax.axis_index("gy") < lax.axis_size("gy") - 1

    def node_row(c, i):
        own = disp_ref[c, i] if i < rows else jnp.where(more_x, xhalo_ref[c, 0:columns], 0.0)
        edge = yhalo_ref[c, i : i + 1] if i < rows else jnp.where(more_x, xhalo_ref[c, columns : columns + 1], 0.0)
        edge = jnp.where(more_y, edge, 0.0)
        up = jnp.where(last_sub, jnp.broadcast_to(edge, tile), pltpu.roll(own, columns - 1, 0))
        mean, diff = 0.5 * (up + own), up - own
        mean_up = jnp.where(last_lane, 0.0, pltpu.roll(mean, layers - 1, 1))
        diff_up = jnp.where(last_lane, 0.0, pltpu.roll(diff, layers - 1, 1))
        return 0.5 * (mean_up + mean), 0.5 * (diff_up + diff), mean_up - mean

    lower = [node_row(c, 0) for c in range(3)]
    zero_tile = jnp.zeros(tile, F32)
    for i in range(rows):
        upper = [node_row(c, i + 1) for c in range(3)]
        g = [
            (upper[c][0] - lower[c][0], 0.5 * (upper[c][1] + lower[c][1]), 0.5 * (upper[c][2] + lower[c][2]))
            for c in range(3)
        ]
        lower = upper
        strain = [g[0][0], g[1][1], g[2][2], g[1][2] + g[2][1], g[0][2] + g[2][0], g[0][1] + g[1][0]]
        stiffness = stiff_ref[i]
        volume = strain[0] + strain[1] + strain[2]
        for c in range(8):
            place = pl.ds(i * columns * 8 + c, columns, stride=8)
            if c >= 6:
                strain_ref[place, :] = zero_tile
                continue
            strain_ref[place, :] = strain[c]
            stress_out[place, :] = stiffness * (volume + 2.0 * strain[c] if c < 3 else strain[c])

    order_copy.wait()

    def body(q, carry):
        _, states = run_group(
            q * group, group, order_ref, state_ref, strain_ref, weights, stress_out, rows * columns
        )
        for g in range(group):
            done_ref[pl.ds(pl.multiple_of((q * group + g) * count, count), count), :] = states[g]
        return carry

    lax.fori_loop(0, first_groups(order_ref, most, group), body, 0)

    last = row_fluxes(stress_out, rows - 1, columns)
    for c in range(3):
        xface_ref[c] = -last[c][1]
    s = [stress_out[pl.ds((columns - 1) * 8 + c, rows, stride=columns * 8), :] for c in range(6)]
    side = fluxes(s, lambda v: 0.5 * v, lambda v: -v)
    for c in range(3):
        yface_ref[c] = -side[c][0]
        yface_ref[c, 1:rows] = yface_ref[c, 1:rows] - side[c][1][0 : rows - 1]
        cface_ref[c : c + 1] = -side[c][1][rows - 1 : rows]


def inner_kernel(
    rows, columns, order_vmem, state_ref, strain_ref, stress_in, done_ref,
    start0_ref, start1_ref, high_ref, low_ref, back_ref, stress_ref,
    force_ref, out_hbm,
    stress_s, out_s, sems, order_ref, order_sem,
):
    order_copy = pltpu.make_async_copy(order_vmem, order_ref, order_sem)
    order_copy.start()
    groups, count, group, layers = out_s.shape
    most = groups * group
    weights = (start0_ref, start1_ref, high_ref, low_ref, back_ref, stress_ref)
    stress_s[...] = stress_in[...]
    order_copy.wait()
    before = first_groups(order_ref, most, group)
    after = lax.div(order_ref[0, most + 1] + (group - 1), group)

    def store(q):
        return pltpu.make_async_copy(
            out_s.at[q], out_hbm.at[:, pl.ds(q * group, group), :], sems.at[q]
        )

    def copy(q, carry):
        for g in range(group):
            place = q * group + g
            set_pencil(
                out_s, order_ref[0, place],
                done_ref[pl.ds(pl.multiple_of(place * count, count), count), :],
            )
        return carry

    def clear(q, carry):
        for g in range(group):
            set_pencil(out_s, order_ref[0, q * group + g], jnp.zeros((count, layers), F32))
        return carry

    lax.fori_loop(0, before, copy, 0)
    lax.fori_loop(jnp.maximum(before, after), groups, clear, 0)

    def body(q, sent):
        entries, states = run_group(
            q * group, group, order_ref, state_ref, strain_ref, weights, stress_s, rows * columns
        )
        for g in range(group):
            set_pencil(out_s, entries[g], states[g])
        whole = jnp.maximum(sent, lax.div(entries[group - 1] + 1, group))

        def send(chunk, carry):
            store(chunk).start()
            return carry

        lax.fori_loop(sent, whole, send, 0)
        return whole

    sent = lax.fori_loop(before, after, body, 0)

    def send(chunk, carry):
        store(chunk).start()
        return carry

    lax.fori_loop(sent, groups, send, 0)

    below = None
    for i in range(rows):
        here = row_fluxes(stress_s, i, columns)
        for c in range(3):
            force_ref[c, i] = -here[c][0] if below is None else -(here[c][0] + below[c][1])
        below = here
    for q in range(groups):
        store(q).wait()


def update_kernel(
    disp_ref, velocity_ref, external_ref, mass_ref, force_ref, xface_ref, yface_ref, cface_ref,
    disp_hbm, velocity_hbm, disp_out, velocity_out, sems,
):
    rows, columns, layers = mass_ref.shape
    tile = (columns, layers)
    less_x = lax.axis_index("gx") > 0
    first_sub = lax.broadcasted_iota(jnp.int32, tile, 0) == 0
    first_sub = jnp.logical_and(first_sub, lax.axis_index("gy") > 0)
    factors = [STEP / mass_ref[i] for i in range(rows)]
    copies = []
    for c in range(3):
        for i in range(rows):
            edge = yface_ref[c, i : i + 1]
            if i == 0:
                edge = edge + jnp.where(less_x, cface_ref[c : c + 1], 0.0)
            internal = force_ref[c, i] + jnp.where(first_sub, jnp.broadcast_to(edge, tile), 0.0)
            if i == 0:
                internal = internal + jnp.where(less_x, xface_ref[c], 0.0)
            velocity = velocity_ref[c, i] + factors[i] * (external_ref[c, i] - internal)
            velocity_out[c, i] = velocity
            disp_out[c, i] = disp_ref[c, i] + STEP * velocity
        for n, (ours, whole) in enumerate(((velocity_out, velocity_hbm), (disp_out, disp_hbm))):
            copies.append(pltpu.make_async_copy(ours.at[c], whole.at[c], sems.at[n, c]))
            copies[-1].start()
    for copy in copies:
        copy.wait()


def shape(*dims, dtype=F32):
    return jax.ShapeDtypeStruct(dims, dtype)


def on_device(
    displacement, velocity, external_force, node_mass, stiffness, cloak_list, micro_state,
    localization, modes, point_weight, point_modulus, softening,
):
    rows, columns, layers = stiffness.shape
    points, count = modes.shape
    most = cloak_list.shape[2]
    gx, gy = lax.axis_size("gx"), lax.axis_size("gy")
    along_x = [((i + 1) % gx, i) for i in range(gx)]
    along_y = [((j + 1) % gy, j) for j in range(gy)]
    both = [((i + 1) % gx * gy + (j + 1) % gy, i * gy + j) for i in range(gx) for j in range(gy)]
    back = lambda pairs: [(b, a) for a, b in pairs]
    group = 8
    small = pltpu.CompilerParams(vmem_limit_bytes=4 * 2**20)
    medium = pltpu.CompilerParams(vmem_limit_bytes=16 * 2**20)
    long = pl.CostEstimate(flops=10**10, bytes_accessed=10**6, transcendentals=0)
    yhalo = pl.pallas_call(
        column_kernel, out_shape=shape(3, rows, layers), in_specs=[VMEM], out_specs=VMEM,
        compiler_params=small, cost_estimate=long,
    )(displacement)
    yhalo = lax.ppermute(yhalo, "gy", along_y)

    order_shape = shape(8, (most + 2 + 127) // 128 * 128, dtype=jnp.int32)
    weight, modulus, soft = (a.reshape(1, points) for a in (point_weight, point_modulus, softening))
    half, order = pl.pallas_call(
        functools.partial(half_kernel, rows, columns),
        out_shape=(shape(count, count), order_shape),
        in_specs=[VMEM] * 4,
        out_specs=(VMEM,) * 2,
        scratch_shapes=[pltpu.VMEM(order_shape.shape, jnp.int32)],
        compiler_params=medium,
        cost_estimate=long,
    )(modes, weight, modulus, cloak_list[0])

    xhalo = pl.pallas_call(
        row_kernel, out_shape=shape(3, 2 * columns, layers), in_specs=[VMEM] * 2, out_specs=VMEM,
        compiler_params=small,
    )(displacement, yhalo)
    xhalo = lax.ppermute(xhalo, "gx", along_x)

    matrices = pl.pallas_call(
        matrices_kernel,
        out_shape=tuple(shape(n, points, dtype=BF16) for n in (2 * count, 2 * count, points, points))
        + (shape(points, 2 * count, dtype=BF16), shape(16, points, dtype=BF16)),
        in_specs=[VMEM] * 6,
        out_specs=(VMEM,) * 6,
        scratch_shapes=[pltpu.VMEM((16, points), F32)],
        compiler_params=medium,
        cost_estimate=long,
    )(half, modes, localization.T, weight, modulus, soft)

    groups = most // group
    states = micro_state.reshape(count * most, layers)
    strain_shape = shape(rows * columns * 8, layers)
    stress_shape = shape(rows * columns * 8 + 8, layers)
    xface, yface, cface, strain, stress, done = pl.pallas_call(
        functools.partial(edge_kernel, group, most),
        out_shape=(
            shape(3, columns, layers), shape(3, rows, layers), shape(3, layers),
            strain_shape, stress_shape, shape(most * count, layers),
        ),
        in_specs=[VMEM] * 12,
        out_specs=(VMEM,) * 6,
        scratch_shapes=[pltpu.SMEM(order_shape.shape, jnp.int32), pltpu.SemaphoreType.DMA],
        compiler_params=pltpu.CompilerParams(vmem_limit_bytes=30 * 2**20),
        cost_estimate=pl.CostEstimate(flops=10**10, bytes_accessed=10**7, transcendentals=0),
    )(order, displacement, xhalo, yhalo, stiffness, states, *matrices)

    xface = lax.ppermute(xface, "gx", back(along_x))
    yface = lax.ppermute(yface, "gy", back(along_y))
    cface = lax.ppermute(cface, ("gx", "gy"), back(both))

    force, new_state = pl.pallas_call(
        functools.partial(inner_kernel, rows, columns),
        out_shape=(shape(3, rows, columns, layers), shape(count, most, layers)),
        in_specs=[VMEM] * 11,
        out_specs=(VMEM, HBM),
        scratch_shapes=[
            pltpu.VMEM(stress_shape.shape, F32), pltpu.VMEM((groups, count, group, layers), F32),
            pltpu.SemaphoreType.DMA((groups,)),
            pltpu.SMEM(order_shape.shape, jnp.int32), pltpu.SemaphoreType.DMA,
        ],
        compiler_params=pltpu.CompilerParams(vmem_limit_bytes=30 * 2**20),
        cost_estimate=pl.CostEstimate(flops=2 * 10**10, bytes_accessed=10**7, transcendentals=0),
    )(order, states, strain, stress, done, *matrices)

    displacement_next, velocity_next = pl.pallas_call(
        update_kernel,
        out_shape=(shape(3, rows, columns, layers),) * 2,
        in_specs=[VMEM] * 8,
        out_specs=(HBM,) * 2,
        scratch_shapes=[pltpu.VMEM(displacement.shape, F32)] * 2 + [pltpu.SemaphoreType.DMA((2, 3))],
        compiler_params=pltpu.CompilerParams(vmem_limit_bytes=16 * 2**20),
    )(displacement, velocity, external_force, node_mass, force, xface, yface, cface)
    return displacement_next, velocity_next, new_state.reshape(micro_state.shape)


def solution(mesh):
    field = P(None, "gx", "gy", None)
    grid = P("gx", "gy", None)
    state = P("gx", "gy", None, None, None)
    in_specs = (field, field, field, grid, grid, P("gx", None, None), state, P(), P(), P(), P(), P())
    return jax.shard_map(
        on_device, mesh=mesh, in_specs=in_specs, out_specs=(field, field, state), check_vma=False
    )
```

```python
import functools

import jax
import jax.numpy as jnp
from jax import lax
from jax.experimental import pallas as pl
from jax.experimental.pallas import tpu as pltpu
from jax.sharding import PartitionSpec as P

ITERS = 3
STEP = 0.25
HIGHEST = lax.Precision.HIGHEST
F32 = jnp.float32
BF16 = jnp.bfloat16
VMEM = pl.BlockSpec(memory_space=pltpu.VMEM)
HBM = pl.BlockSpec(memory_space=pltpu.HBM)


def split(x):
    high = x.astype(BF16)
    return high, (x - high.astype(F32)).astype(BF16)


def dot(a, b):
    return jnp.dot(a, b, preferred_element_type=F32)


def exact(a, b):
    return jnp.dot(a, b, precision=HIGHEST, preferred_element_type=F32)


def transposed_product(a, b):
    terms = []
    for x in (a, b):
        one = x.astype(BF16).astype(F32)
        two = (x - one).astype(BF16).astype(F32)
        terms.append((one, two, x - one - two))
    (a1, a2, a3), (b1, b2, b3) = terms
    left = jnp.concatenate([a1, a1, a2, a2, a1, a3], axis=0).astype(BF16)
    right = jnp.concatenate([b1, b2, b1, b2, b3, b1], axis=0).astype(BF16)
    return lax.dot_general(left, right, (((0,), (0,)), ((), ())), preferred_element_type=F32)


def lane_of(x, k):
    return jnp.take_along_axis(x, jnp.full(x.shape, k, jnp.int32), axis=1, mode="promise_in_bounds")


def row_of(x, s):
    return jnp.take_along_axis(x, jnp.full(x.shape, s, jnp.int32), axis=0, mode="promise_in_bounds")


def invert_two(a, b, c):
    scale = 1.0 / (a * c - b * b)
    return c * scale, -(b * scale), a * scale


def sweep(blocks, first, last):
    tile = blocks[0].shape
    size = tile[1]
    count = len(blocks)
    lane = lax.broadcasted_iota(jnp.int32, tile, 1)
    row = lax.broadcasted_iota(jnp.int32, tile, 0)

    def spread(x, s):
        return jnp.broadcast_to(x[s : s + 1, :], tile)

    for b in range(first, last):
        before = panel = blocks[b]
        for s in range(0, 8, 4):
            k = b * 8 + s
            lanes4 = jnp.logical_and(lane >= k, lane < k + 4)
            rows4 = jnp.logical_and(row >= s, row < s + 4)
            c = [lane_of(panel, k + i) for i in range(4)]
            r = [
                jnp.where(lane == k + i, 1.0, jnp.where(lanes4, 0.0, spread(panel, s + i)))
                for i in range(4)
            ]
            p = [[row_of(c[j], s + i) for j in range(i + 1)] for i in range(4)]
            (b00, b01), (b10, b11) = p[2][:2], p[3][:2]
            i00, i10, i11 = invert_two(p[0][0], p[1][0], p[1][1])
            w00, w01 = b00 * i00 + b01 * i10, b00 * i10 + b01 * i11
            w10, w11 = b10 * i00 + b11 * i10, b10 * i10 + b11 * i11
            j00, j10, j11 = invert_two(
                p[2][2] - (w00 * b00 + w01 * b01),
                p[3][2] - (w10 * b00 + w11 * b01),
                p[3][3] - (w10 * b10 + w11 * b11),
            )
            y2 = r[2] - (w00 * r[0] + w01 * r[1])
            y3 = r[3] - (w10 * r[0] + w11 * r[1])
            n2, n3 = j00 * y2 + j10 * y3, j10 * y2 + j11 * y3
            n0 = (i00 * r[0] + i10 * r[1]) - (w00 * n2 + w10 * n3)
            n1 = (i10 * r[0] + i11 * r[1]) - (w01 * n2 + w11 * n3)
            f = [jnp.where(row == s + i, -1.0, jnp.where(rows4, 0.0, c[i])) for i in range(4)]
            rest = jnp.where(jnp.logical_or(lanes4, rows4), 0.0, panel)
            panel = rest - ((f[0] * n0 + f[1] * n1) + (f[2] * n2 + f[3] * n3))
        inside = jnp.logical_and(lane >= b * 8, lane < b * 8 + 8)
        panel = jnp.where(inside, -panel, panel)
        change = transposed_product(before, panel)
        for i in range(count):
            old = blocks[i]
            kept = jnp.where(inside, 0.0, old)
            if i == b:
                blocks[i] = panel
            elif i == b + 1:
                t = [lane_of(old, b * 8 + s) * spread(panel, s) for s in range(8)]
                blocks[i] = kept - (((t[0] + t[1]) + (t[2] + t[3])) + ((t[4] + t[5]) + (t[6] + t[7])))
            else:
                blocks[i] = kept - change[i * 8 : i * 8 + 8]
    return jnp.concatenate(blocks, axis=0)


def near(a, b):
    (ah, al), (bh, bl) = split(a), split(b)
    return dot(ah, bh) + dot(al, bh) + dot(ah, bl)


def order_entries(rows, columns, lists_ref, order_ref, line):
    most = lists_ref.shape[1]
    width = order_ref.shape[1]
    tile = order_ref.shape
    line[...] = jnp.full(line.shape, -1, jnp.int32)
    line[0:1, 0:most] = lists_ref[pl.ds(lax.axis_index("gy"), 1), :]
    pencil = jnp.broadcast_to(line[0:1, :].astype(F32), tile)
    lane = lax.broadcasted_iota(jnp.int32, tile, 1)
    row = lax.broadcasted_iota(jnp.int32, tile, 0)
    column = pencil - columns * jnp.floor((pencil + 0.5) / columns)
    listed = pencil >= 0.0
    face = jnp.logical_or(pencil >= (rows - 1) * columns, column == columns - 1)
    kind = jnp.where(listed, jnp.where(face, 0, 1), jnp.where(lane < most, 2, 3))
    flags = jnp.where(kind == row, 1.0, 0.0).astype(BF16)
    square = (width, width)
    first = lax.broadcasted_iota(jnp.int32, square, 0)
    second = lax.broadcasted_iota(jnp.int32, square, 1)
    before = dot(flags, (first < second).astype(F32).astype(BF16))
    totals = dot(flags, jnp.ones(square, BF16))
    faces, number = totals[0:1], totals[0:1] + totals[1:2]
    kind = kind[0:1]
    place = jnp.where(
        kind == 0, before[0:1],
        jnp.where(kind == 1, faces + before[1:2], jnp.where(kind == 2, number + before[2:3], -1.0)),
    )
    moves = (jnp.broadcast_to(place, square) == first.astype(F32)).astype(F32)
    values = jnp.where(row == 0, lane.astype(F32), pencil)
    ordered = lax.dot_general(
        values, moves, (((1,), (1,)), ((), ())), precision=HIGHEST, preferred_element_type=F32
    )
    counts = jnp.where(lane == most, jnp.broadcast_to(faces, tile), jnp.broadcast_to(number, tile))
    tail = jnp.logical_and(row == 0, lane >= most)
    order_ref[...] = jnp.where(tail, counts, ordered).astype(jnp.int32)


def row_blocks(matrix):
    return [matrix[i : i + 8] for i in range(0, matrix.shape[0], 8)]


def half_kernel(rows, columns, modes_ref, weight_ref, modulus_ref, lists_ref, half_ref, order_ref, line):
    order_entries(rows, columns, lists_ref, order_ref, line)
    points, count = modes_ref.shape
    modes = modes_ref[...]
    matrix = exact(modes.T * (weight_ref[...] / points * modulus_ref[...]), modes)
    half_ref[...] = sweep(row_blocks(matrix), 0, count // 16)


def matrices_kernel(
    half_ref, modes_ref, local_ref, weight_ref, modulus_ref, soft_ref,
    start0_ref, start1_ref, high_ref, low_ref, back_ref, stress_ref, wide,
):
    points, count = modes_ref.shape
    modes_t = modes_ref[...].T
    weight = weight_ref[...] / points
    modulus = modulus_ref[...]
    root = jnp.sqrt(soft_ref[...])
    scale = weight * modulus / root
    inverted = -sweep(row_blocks(half_ref[...]), count // 16, count // 8)
    wide[...] = jnp.zeros_like(wide)
    wide[0 : local_ref.shape[0], :] = local_ref[...]
    local = wide[...]
    stress_ref[...] = (local * scale).astype(BF16)
    high, low = split(modes_t * root)
    start0_ref[0:count] = high
    start0_ref[count:] = high
    start1_ref[0:count] = low
    soft_local = local[0:8] * root
    local_high = soft_local.astype(BF16).astype(F32)
    part = [local_high, local_high, soft_local - local_high, jnp.zeros_like(local_high)]
    start1_ref[count:] = jnp.concatenate(part * (count // 32), axis=0).astype(BF16)
    back = near((modes_t * scale).T, inverted)
    high, low = split(back)
    back_ref[:, 0:count] = high
    back_ref[:, count:] = low
    newton = near(back, modes_t * root)
    high, low = split(newton)
    high_ref[...] = high
    low_ref[...] = low


def respond(u):
    return u * lax.rsqrt(1.0 + u * u)


def cells(states, strains, start0, start1, newton_high, newton_low, back, stress_m):
    layers = states[0].shape[1]
    count = states[0].shape[0]
    number = len(states)
    part = min(2, number)
    turned = [state.T for state in states]
    place = lax.broadcasted_iota(jnp.int32, (layers, count), 1) // 32
    strain_parts = []
    each = count // 32
    for q in range(0, number, each):
        rows = []
        for strain in strains[q : q + each]:
            high = strain.astype(BF16).astype(F32)
            rows += [high, strain - high, high, jnp.zeros_like(high)]
        rows = jnp.concatenate(rows, axis=0).T
        strain_parts += [jnp.where(place == g, rows, 0.0).astype(BF16) for g in range(each)]
    new_states, stresses = [None] * number, [None] * number

    def chunk(c):
        high, low = split(jnp.concatenate(turned[c : c + part], axis=0))
        strain = jnp.concatenate(strain_parts[c : c + part], axis=0)
        start = dot(jnp.concatenate([high, low], axis=1), start0)
        start = start + dot(jnp.concatenate([high, strain], axis=1), start1)
        u = start
        yield
        for step in range(ITERS - 1):
            high, low = split(respond(u))
            u = u - (dot(high, newton_high) + dot(low, newton_high) + dot(high, newton_low))
            yield
        h = respond(u)
        last = u - dot(h.astype(BF16), newton_high)
        high, low = split(start - u + h)
        both = dot(high, back)
        change = both[:, 0:count] + both[:, count:] + dot(low, back[:, 0:count])
        yield
        stress = lax.dot_general(
            stress_m, respond(last).astype(BF16), (((1,), (1,)), ((), ())), preferred_element_type=F32
        )
        for g in range(part):
            rows = slice(g * layers, (g + 1) * layers)
            new_states[c + g] = states[c + g] - change[rows].T
            stresses[c + g] = stress[0:8, rows]
        yield

    chunks = [chunk(c) for c in range(0, number, part)]
    for stage in range(ITERS + 2):
        for c in chunks:
            next(c)
    return new_states, stresses


def set_pencil(ref, entry, value):
    groups, count, group, layers = ref.shape
    place = lax.div(entry, group) * (count * group) + lax.rem(entry, group)
    ref.reshape(groups * count * group, layers)[pl.ds(place, count, stride=group), :] = value


def run_group(base, group, order_ref, state_ref, strain_ref, weights, stress_s, spare):
    count = weights[4].shape[1] // 2
    most = state_ref.shape[0] // count
    entries = [order_ref[0, base + g] for g in range(group)]
    pencils = [order_ref[1, base + g] for g in range(group)]
    states = [state_ref[pl.ds(e, count, stride=most), :] for e in entries]
    strains = [
        strain_ref[pl.ds(pl.multiple_of(jnp.maximum(p, 0) * 8, 8), 8), :] for p in pencils
    ]
    new_states, stresses = cells(states, strains, *(w[...] for w in weights))
    for g in range(group):
        spot = jnp.where(pencils[g] >= 0, pencils[g], spare)
        stress_s[pl.ds(pl.multiple_of(spot * 8, 8), 8), :] = stresses[g]
    return entries, [jnp.where(p >= 0, a, 0.0) for p, a in zip(pencils, new_states)]


def fluxes(s, side_mean, side_diff):
    lane_zero = lax.broadcasted_iota(jnp.int32, s[0].shape, 1) == 0

    def along(v):
        down = jnp.where(lane_zero, 0.0, pltpu.roll(v, 1, 1))
        return 0.5 * (v + down), v - down

    first = [along(side_mean(s[c]))[0] for c in (0, 5, 4)]
    second = [along(side_diff(s[c]))[0] for c in (5, 1, 3)]
    third = [along(side_mean(s[c]))[1] for c in (4, 3, 2)]
    half = [0.5 * (second[c] + third[c]) for c in range(3)]
    return [(first[c] + half[c], half[c] - first[c]) for c in range(3)]


def row_fluxes(stress_ref, i, columns):
    s = [stress_ref[pl.ds(i * columns * 8 + c, columns, stride=8), :] for c in range(6)]
    first_sub = lax.broadcasted_iota(jnp.int32, s[0].shape, 0) == 0

    def shift(v):
        return jnp.where(first_sub, 0.0, pltpu.roll(v, 1, 0))

    return fluxes(s, lambda v: 0.5 * (v + shift(v)), lambda v: v - shift(v))


def first_groups(order_ref, most, group):
    return lax.div(order_ref[0, most] + (group - 1), group)


def column_kernel(disp_ref, column_ref):
    for c in range(3):
        column_ref[c] = disp_ref[c, :, 0, :]


def row_kernel(disp_ref, yhalo_ref, row_ref):
    columns = disp_ref.shape[2]
    for c in range(3):
        row_ref[c] = jnp.zeros(row_ref.shape[1:], F32)
        row_ref[c, 0:columns] = disp_ref[c, 0]
        row_ref[c, columns : columns + 1] = yhalo_ref[c, 0:1]


def edge_kernel(
    group, most, order_vmem, disp_ref, xhalo_ref, yhalo_ref, stiff_ref, state_ref,
    start0_ref, start1_ref, high_ref, low_ref, back_ref, stress_ref,
    xface_ref, yface_ref, cface_ref, strain_ref, stress_out, done_ref,
    order_ref, order_sem,
):
    order_copy = pltpu.make_async_copy(order_vmem, order_ref, order_sem)
    order_copy.start()
    rows, columns, layers = stiff_ref.shape
    count = state_ref.shape[0] // most
    weights = (start0_ref, start1_ref, high_ref, low_ref, back_ref, stress_ref)
    tile = (columns, layers)
    lane = lax.broadcasted_iota(jnp.int32, tile, 1)
    sub = lax.broadcasted_iota(jnp.int32, tile, 0)
    last_lane = lane == layers - 1
    last_sub = sub == columns - 1

    more_x = lax.axis_index("gx") < lax.axis_size("gx") - 1
    more_y = lax.axis_index("gy") < lax.axis_size("gy") - 1

    def node_row(c, i):
        own = disp_ref[c, i] if i < rows else jnp.where(more_x, xhalo_ref[c, 0:columns], 0.0)
        edge = yhalo_ref[c, i : i + 1] if i < rows else jnp.where(more_x, xhalo_ref[c, columns : columns + 1], 0.0)
        edge = jnp.where(more_y, edge, 0.0)
        up = jnp.where(last_sub, jnp.broadcast_to(edge, tile), pltpu.roll(own, columns - 1, 0))
        mean, diff = 0.5 * (up + own), up - own
        mean_up = jnp.where(last_lane, 0.0, pltpu.roll(mean, layers - 1, 1))
        diff_up = jnp.where(last_lane, 0.0, pltpu.roll(diff, layers - 1, 1))
        return 0.5 * (mean_up + mean), 0.5 * (diff_up + diff), mean_up - mean

    lower = [node_row(c, 0) for c in range(3)]
    zero_tile = jnp.zeros(tile, F32)
    for i in range(rows):
        upper = [node_row(c, i + 1) for c in range(3)]
        g = [
            (upper[c][0] - lower[c][0], 0.5 * (upper[c][1] + lower[c][1]), 0.5 * (upper[c][2] + lower[c][2]))
            for c in range(3)
        ]
        lower = upper
        strain = [g[0][0], g[1][1], g[2][2], g[1][2] + g[2][1], g[0][2] + g[2][0], g[0][1] + g[1][0]]
        stiffness = stiff_ref[i]
        volume = strain[0] + strain[1] + strain[2]
        for c in range(8):
            place = pl.ds(i * columns * 8 + c, columns, stride=8)
            if c >= 6:
                strain_ref[place, :] = zero_tile
                continue
            strain_ref[place, :] = strain[c]
            stress_out[place, :] = stiffness * (volume + 2.0 * strain[c] if c < 3 else strain[c])

    order_copy.wait()

    def body(q, carry):
        _, states = run_group(
            q * group, group, order_ref, state_ref, strain_ref, weights, stress_out, rows * columns
        )
        for g in range(group):
            done_ref[pl.ds(pl.multiple_of((q * group + g) * count, count), count), :] = states[g]
        return carry

    lax.fori_loop(0, first_groups(order_ref, most, group), body, 0)

    last = row_fluxes(stress_out, rows - 1, columns)
    for c in range(3):
        xface_ref[c] = -last[c][1]
    s = [stress_out[pl.ds((columns - 1) * 8 + c, rows, stride=columns * 8), :] for c in range(6)]
    side = fluxes(s, lambda v: 0.5 * v, lambda v: -v)
    for c in range(3):
        yface_ref[c] = -side[c][0]
        yface_ref[c, 1:rows] = yface_ref[c, 1:rows] - side[c][1][0 : rows - 1]
        cface_ref[c : c + 1] = -side[c][1][rows - 1 : rows]


def late_chunks(groups):
    return min(2, groups)


def inner_kernel(
    rows, columns, order_vmem, state_ref, strain_ref, stress_in, done_ref,
    start0_ref, start1_ref, high_ref, low_ref, back_ref, stress_ref,
    force_ref, out_hbm, out_s,
    stress_s, sems, order_ref, order_sem,
):
    order_copy = pltpu.make_async_copy(order_vmem, order_ref, order_sem)
    order_copy.start()
    groups, count, group, layers = out_s.shape
    most = groups * group
    weights = (start0_ref, start1_ref, high_ref, low_ref, back_ref, stress_ref)
    stress_s[...] = stress_in[...]
    order_copy.wait()
    before = first_groups(order_ref, most, group)
    after = lax.div(order_ref[0, most + 1] + (group - 1), group)

    early = groups - late_chunks(groups)

    def store(q):
        return pltpu.make_async_copy(
            out_s.at[q], out_hbm.at[:, pl.ds(q * group, group), :], sems.at[q]
        )

    def copy(q, carry):
        for g in range(group):
            place = q * group + g
            set_pencil(
                out_s, order_ref[0, place],
                done_ref[pl.ds(pl.multiple_of(place * count, count), count), :],
            )
        return carry

    def clear(q, carry):
        for g in range(group):
            set_pencil(out_s, order_ref[0, q * group + g], jnp.zeros((count, layers), F32))
        return carry

    lax.fori_loop(0, before, copy, 0)
    lax.fori_loop(jnp.maximum(before, after), groups, clear, 0)

    def body(q, sent):
        entries, states = run_group(
            q * group, group, order_ref, state_ref, strain_ref, weights, stress_s, rows * columns
        )
        for g in range(group):
            set_pencil(out_s, entries[g], states[g])
        whole = jnp.maximum(sent, lax.div(entries[group - 1] + 1, group))

        def send(chunk, carry):
            store(chunk).start()
            return carry

        whole = jnp.minimum(whole, early)
        lax.fori_loop(sent, whole, send, 0)
        return whole

    sent = lax.fori_loop(before, after, body, 0)

    def send(chunk, carry):
        store(chunk).start()
        return carry

    lax.fori_loop(sent, early, send, 0)

    below = None
    for i in range(rows):
        here = row_fluxes(stress_s, i, columns)
        for c in range(3):
            force_ref[c, i] = -here[c][0] if below is None else -(here[c][0] + below[c][1])
        below = here
    for q in range(early):
        store(q).wait()


def update_kernel(
    disp_ref, velocity_ref, external_ref, mass_ref, force_ref, xface_ref, yface_ref, cface_ref,
    state_ref, state_in, disp_hbm, velocity_hbm, state_hbm, disp_out, velocity_out, sems, state_sems,
):
    groups, _, group, _ = state_ref.shape
    copies = []
    for n, q in enumerate(range(groups - late_chunks(groups), groups)):
        copies.append(
            pltpu.make_async_copy(
                state_ref.at[q], state_hbm.at[:, pl.ds(q * group, group), :], state_sems.at[n]
            )
        )
        copies[-1].start()
    rows, columns, layers = mass_ref.shape
    tile = (columns, layers)
    less_x = lax.axis_index("gx") > 0
    first_sub = lax.broadcasted_iota(jnp.int32, tile, 0) == 0
    first_sub = jnp.logical_and(first_sub, lax.axis_index("gy") > 0)
    factors = [STEP / mass_ref[i] for i in range(rows)]
    for c in range(3):
        for i in range(rows):
            edge = yface_ref[c, i : i + 1]
            if i == 0:
                edge = edge + jnp.where(less_x, cface_ref[c : c + 1], 0.0)
            internal = force_ref[c, i] + jnp.where(first_sub, jnp.broadcast_to(edge, tile), 0.0)
            if i == 0:
                internal = internal + jnp.where(less_x, xface_ref[c], 0.0)
            velocity = velocity_ref[c, i] + factors[i] * (external_ref[c, i] - internal)
            velocity_out[c, i] = velocity
            disp_out[c, i] = disp_ref[c, i] + STEP * velocity
        for n, (ours, whole) in enumerate(((velocity_out, velocity_hbm), (disp_out, disp_hbm))):
            copies.append(pltpu.make_async_copy(ours.at[c], whole.at[c], sems.at[n, c]))
            copies[-1].start()
    for copy in copies:
        copy.wait()


def shape(*dims, dtype=F32):
    return jax.ShapeDtypeStruct(dims, dtype)


def on_device(
    displacement, velocity, external_force, node_mass, stiffness, cloak_list, micro_state,
    localization, modes, point_weight, point_modulus, softening,
):
    rows, columns, layers = stiffness.shape
    points, count = modes.shape
    most = cloak_list.shape[2]
    gx, gy = lax.axis_size("gx"), lax.axis_size("gy")
    along_x = [((i + 1) % gx, i) for i in range(gx)]
    along_y = [((j + 1) % gy, j) for j in range(gy)]
    both = [((i + 1) % gx * gy + (j + 1) % gy, i * gy + j) for i in range(gx) for j in range(gy)]
    back = lambda pairs: [(b, a) for a, b in pairs]
    group = 8
    small = pltpu.CompilerParams(vmem_limit_bytes=4 * 2**20)
    medium = pltpu.CompilerParams(vmem_limit_bytes=16 * 2**20)
    long = pl.CostEstimate(flops=10**10, bytes_accessed=10**6, transcendentals=0)
    yhalo = pl.pallas_call(
        column_kernel, out_shape=shape(3, rows, layers), in_specs=[VMEM], out_specs=VMEM,
        compiler_params=small, cost_estimate=long,
    )(displacement)
    yhalo = lax.ppermute(yhalo, "gy", along_y)

    order_shape = shape(8, (most + 2 + 127) // 128 * 128, dtype=jnp.int32)
    weight, modulus, soft = (a.reshape(1, points) for a in (point_weight, point_modulus, softening))
    half, order = pl.pallas_call(
        functools.partial(half_kernel, rows, columns),
        out_shape=(shape(count, count), order_shape),
        in_specs=[VMEM] * 4,
        out_specs=(VMEM,) * 2,
        scratch_shapes=[pltpu.VMEM(order_shape.shape, jnp.int32)],
        compiler_params=medium,
        cost_estimate=long,
    )(modes, weight, modulus, cloak_list[0])

    xhalo = pl.pallas_call(
        row_kernel, out_shape=shape(3, 2 * columns, layers), in_specs=[VMEM] * 2, out_specs=VMEM,
        compiler_params=small,
    )(displacement, yhalo)
    xhalo = lax.ppermute(xhalo, "gx", along_x)

    matrices = pl.pallas_call(
        matrices_kernel,
        out_shape=tuple(shape(n, points, dtype=BF16) for n in (2 * count, 2 * count, points, points))
        + (shape(points, 2 * count, dtype=BF16), shape(16, points, dtype=BF16)),
        in_specs=[VMEM] * 6,
        out_specs=(VMEM,) * 6,
        scratch_shapes=[pltpu.VMEM((16, points), F32)],
        compiler_params=medium,
        cost_estimate=long,
    )(half, modes, localization.T, weight, modulus, soft)

    groups = most // group
    states = micro_state.reshape(count * most, layers)
    strain_shape = shape(rows * columns * 8, layers)
    stress_shape = shape(rows * columns * 8 + 8, layers)
    xface, yface, cface, strain, stress, done = pl.pallas_call(
        functools.partial(edge_kernel, group, most),
        out_shape=(
            shape(3, columns, layers), shape(3, rows, layers), shape(3, layers),
            strain_shape, stress_shape, shape(most * count, layers),
        ),
        in_specs=[VMEM] * 12,
        out_specs=(VMEM,) * 6,
        scratch_shapes=[pltpu.SMEM(order_shape.shape, jnp.int32), pltpu.SemaphoreType.DMA],
        compiler_params=pltpu.CompilerParams(vmem_limit_bytes=30 * 2**20),
        cost_estimate=pl.CostEstimate(flops=10**10, bytes_accessed=10**7, transcendentals=0),
    )(order, displacement, xhalo, yhalo, stiffness, states, *matrices)

    xface = lax.ppermute(xface, "gx", back(along_x))
    yface = lax.ppermute(yface, "gy", back(along_y))
    cface = lax.ppermute(cface, ("gx", "gy"), back(both))

    force, new_state, waiting = pl.pallas_call(
        functools.partial(inner_kernel, rows, columns),
        out_shape=(
            shape(3, rows, columns, layers), shape(count, most, layers),
            shape(groups, count, group, layers),
        ),
        in_specs=[VMEM] * 11,
        out_specs=(VMEM, HBM, VMEM),
        scratch_shapes=[
            pltpu.VMEM(stress_shape.shape, F32),
            pltpu.SemaphoreType.DMA((groups,)),
            pltpu.SMEM(order_shape.shape, jnp.int32), pltpu.SemaphoreType.DMA,
        ],
        compiler_params=pltpu.CompilerParams(vmem_limit_bytes=30 * 2**20),
        cost_estimate=pl.CostEstimate(flops=2 * 10**10, bytes_accessed=10**7, transcendentals=0),
    )(order, states, strain, stress, done, *matrices)

    displacement_next, velocity_next, new_state = pl.pallas_call(
        update_kernel,
        out_shape=(shape(3, rows, columns, layers),) * 2 + (shape(count, most, layers),),
        in_specs=[VMEM] * 9 + [HBM],
        out_specs=(HBM,) * 3,
        input_output_aliases={9: 2},
        scratch_shapes=[pltpu.VMEM(displacement.shape, F32)] * 2
        + [pltpu.SemaphoreType.DMA((2, 3)), pltpu.SemaphoreType.DMA((late_chunks(groups),))],
        compiler_params=pltpu.CompilerParams(vmem_limit_bytes=16 * 2**20),
    )(displacement, velocity, external_force, node_mass, force, xface, yface, cface, waiting, new_state)
    return displacement_next, velocity_next, new_state.reshape(micro_state.shape)


def solution(mesh):
    field = P(None, "gx", "gy", None)
    grid = P("gx", "gy", None)
    state = P("gx", "gy", None, None, None)
    in_specs = (field, field, field, grid, grid, P("gx", None, None), state, P(), P(), P(), P(), P())
    return jax.shard_map(
        on_device, mesh=mesh, in_specs=in_specs, out_specs=(field, field, state), check_vma=False
    )
```

```python
import functools

import jax
import jax.numpy as jnp
from jax import lax
from jax.experimental import pallas as pl
from jax.experimental.pallas import tpu as pltpu
from jax.sharding import PartitionSpec as P

ITERS = 3
STEP = 0.25
HIGHEST = lax.Precision.HIGHEST
F32 = jnp.float32
BF16 = jnp.bfloat16
VMEM = pl.BlockSpec(memory_space=pltpu.VMEM)
HBM = pl.BlockSpec(memory_space=pltpu.HBM)


def split(x):
    high = x.astype(BF16)
    return high, (x - high.astype(F32)).astype(BF16)


def dot(a, b):
    return jnp.dot(a, b, preferred_element_type=F32)


def exact(a, b):
    return jnp.dot(a, b, precision=HIGHEST, preferred_element_type=F32)


def transposed_product(a, b):
    terms = []
    for x in (a, b):
        one = x.astype(BF16).astype(F32)
        two = (x - one).astype(BF16).astype(F32)
        terms.append((one, two, x - one - two))
    (a1, a2, a3), (b1, b2, b3) = terms
    left = jnp.concatenate([a1, a1, a2, a2, a1, a3], axis=0).astype(BF16)
    right = jnp.concatenate([b1, b2, b1, b2, b3, b1], axis=0).astype(BF16)
    return lax.dot_general(left, right, (((0,), (0,)), ((), ())), preferred_element_type=F32)


def lane_of(x, k):
    return jnp.take_along_axis(x, jnp.full(x.shape, k, jnp.int32), axis=1, mode="promise_in_bounds")


def row_of(x, s):
    return jnp.take_along_axis(x, jnp.full(x.shape, s, jnp.int32), axis=0, mode="promise_in_bounds")


def invert_two(a, b, c):
    scale = 1.0 / (a * c - b * b)
    return c * scale, -(b * scale), a * scale


def sweep(blocks, first, last):
    tile = blocks[0].shape
    size = tile[1]
    count = len(blocks)
    lane = lax.broadcasted_iota(jnp.int32, tile, 1)
    row = lax.broadcasted_iota(jnp.int32, tile, 0)

    def spread(x, s):
        return jnp.broadcast_to(x[s : s + 1, :], tile)

    for b in range(first, last):
        before = panel = blocks[b]
        for s in range(0, 8, 4):
            k = b * 8 + s
            lanes4 = jnp.logical_and(lane >= k, lane < k + 4)
            rows4 = jnp.logical_and(row >= s, row < s + 4)
            c = [lane_of(panel, k + i) for i in range(4)]
            r = [
                jnp.where(lane == k + i, 1.0, jnp.where(lanes4, 0.0, spread(panel, s + i)))
                for i in range(4)
            ]
            p = [[row_of(c[j], s + i) for j in range(i + 1)] for i in range(4)]
            (b00, b01), (b10, b11) = p[2][:2], p[3][:2]
            i00, i10, i11 = invert_two(p[0][0], p[1][0], p[1][1])
            w00, w01 = b00 * i00 + b01 * i10, b00 * i10 + b01 * i11
            w10, w11 = b10 * i00 + b11 * i10, b10 * i10 + b11 * i11
            j00, j10, j11 = invert_two(
                p[2][2] - (w00 * b00 + w01 * b01),
                p[3][2] - (w10 * b00 + w11 * b01),
                p[3][3] - (w10 * b10 + w11 * b11),
            )
            y2 = r[2] - (w00 * r[0] + w01 * r[1])
            y3 = r[3] - (w10 * r[0] + w11 * r[1])
            n2, n3 = j00 * y2 + j10 * y3, j10 * y2 + j11 * y3
            n0 = (i00 * r[0] + i10 * r[1]) - (w00 * n2 + w10 * n3)
            n1 = (i10 * r[0] + i11 * r[1]) - (w01 * n2 + w11 * n3)
            f = [jnp.where(row == s + i, -1.0, jnp.where(rows4, 0.0, c[i])) for i in range(4)]
            rest = jnp.where(jnp.logical_or(lanes4, rows4), 0.0, panel)
            panel = rest - ((f[0] * n0 + f[1] * n1) + (f[2] * n2 + f[3] * n3))
        inside = jnp.logical_and(lane >= b * 8, lane < b * 8 + 8)
        panel = jnp.where(inside, -panel, panel)
        change = transposed_product(before, panel)
        for i in range(count):
            old = blocks[i]
            kept = jnp.where(inside, 0.0, old)
            if i == b:
                blocks[i] = panel
            elif i == b + 1:
                t = [lane_of(old, b * 8 + s) * spread(panel, s) for s in range(8)]
                blocks[i] = kept - (((t[0] + t[1]) + (t[2] + t[3])) + ((t[4] + t[5]) + (t[6] + t[7])))
            else:
                blocks[i] = kept - change[i * 8 : i * 8 + 8]
    return jnp.concatenate(blocks, axis=0)


def near(a, b):
    (ah, al), (bh, bl) = split(a), split(b)
    return dot(ah, bh) + dot(al, bh) + dot(ah, bl)


def order_entries(rows, columns, lists_ref, order_ref, line):
    most = lists_ref.shape[1]
    width = order_ref.shape[1]
    tile = order_ref.shape
    line[...] = jnp.full(line.shape, -1, jnp.int32)
    line[0:1, 0:most] = lists_ref[pl.ds(lax.axis_index("gy"), 1), :]
    pencil = jnp.broadcast_to(line[0:1, :].astype(F32), tile)
    lane = lax.broadcasted_iota(jnp.int32, tile, 1)
    row = lax.broadcasted_iota(jnp.int32, tile, 0)
    column = pencil - columns * jnp.floor((pencil + 0.5) / columns)
    listed = pencil >= 0.0
    face = jnp.logical_or(pencil >= (rows - 1) * columns, column == columns - 1)
    kind = jnp.where(listed, jnp.where(face, 0, 1), jnp.where(lane < most, 2, 3))
    flags = jnp.where(kind == row, 1.0, 0.0).astype(BF16)
    square = (width, width)
    first = lax.broadcasted_iota(jnp.int32, square, 0)
    second = lax.broadcasted_iota(jnp.int32, square, 1)
    before = dot(flags, (first < second).astype(F32).astype(BF16))
    totals = dot(flags, jnp.ones(square, BF16))
    faces, number = totals[0:1], totals[0:1] + totals[1:2]
    kind = kind[0:1]
    place = jnp.where(
        kind == 0, before[0:1],
        jnp.where(kind == 1, faces + before[1:2], jnp.where(kind == 2, number + before[2:3], -1.0)),
    )
    moves = (jnp.broadcast_to(place, square) == first.astype(F32)).astype(F32)
    values = jnp.where(row == 0, lane.astype(F32), pencil)
    ordered = lax.dot_general(
        values, moves, (((1,), (1,)), ((), ())), precision=HIGHEST, preferred_element_type=F32
    )
    counts = jnp.where(lane == most, jnp.broadcast_to(faces, tile), jnp.broadcast_to(number, tile))
    tail = jnp.logical_and(row == 0, lane >= most)
    order_ref[...] = jnp.where(tail, counts, ordered).astype(jnp.int32)


def row_blocks(matrix):
    return [matrix[i : i + 8] for i in range(0, matrix.shape[0], 8)]


def half_kernel(rows, columns, modes_ref, weight_ref, modulus_ref, lists_ref, half_ref, order_ref, line):
    order_entries(rows, columns, lists_ref, order_ref, line)
    points, count = modes_ref.shape
    modes = modes_ref[...]
    matrix = exact(modes.T * (weight_ref[...] / points * modulus_ref[...]), modes)
    half_ref[...] = sweep(row_blocks(matrix), 0, count // 16)


def matrices_kernel(
    half_ref, modes_ref, local_ref, weight_ref, modulus_ref, soft_ref,
    start0_ref, start1_ref, high_ref, low_ref, back_ref, stress_ref, wide,
):
    points, count = modes_ref.shape
    modes_t = modes_ref[...].T
    weight = weight_ref[...] / points
    modulus = modulus_ref[...]
    root = jnp.sqrt(soft_ref[...])
    scale = weight * modulus / root
    inverted = -sweep(row_blocks(half_ref[...]), count // 16, count // 8)
    wide[...] = jnp.zeros_like(wide)
    wide[0 : local_ref.shape[0], :] = local_ref[...]
    local = wide[...]
    stress_ref[...] = (local * scale).astype(BF16)
    high, low = split(modes_t * root)
    start0_ref[0:count] = high
    start0_ref[count:] = high
    start1_ref[0:count] = low
    soft_local = local[0:8] * root
    local_high = soft_local.astype(BF16).astype(F32)
    part = [local_high, local_high, soft_local - local_high, jnp.zeros_like(local_high)]
    start1_ref[count:] = jnp.concatenate(part * (count // 32), axis=0).astype(BF16)
    back = near((modes_t * scale).T, inverted)
    high, low = split(back)
    back_ref[:, 0:count] = high
    back_ref[:, count:] = low
    newton = near(back, modes_t * root)
    high, low = split(newton)
    high_ref[...] = high
    low_ref[...] = low


def respond(u):
    return u * lax.rsqrt(1.0 + u * u)


def cells(states, strains, start0, start1, newton_high, newton_low, back, stress_m):
    layers = states[0].shape[1]
    count = states[0].shape[0]
    number = len(states)
    part = min(2, number)
    turned = [state.T for state in states]
    place = lax.broadcasted_iota(jnp.int32, (layers, count), 1) // 32
    strain_parts = []
    each = count // 32
    for q in range(0, number, each):
        rows = []
        for strain in strains[q : q + each]:
            high = strain.astype(BF16).astype(F32)
            rows += [high, strain - high, high, jnp.zeros_like(high)]
        rows = jnp.concatenate(rows, axis=0).T
        strain_parts += [jnp.where(place == g, rows, 0.0).astype(BF16) for g in range(each)]
    new_states, stresses = [None] * number, [None] * number

    def chunk(c):
        high, low = split(jnp.concatenate(turned[c : c + part], axis=0))
        strain = jnp.concatenate(strain_parts[c : c + part], axis=0)
        start = dot(jnp.concatenate([high, low], axis=1), start0)
        start = start + dot(jnp.concatenate([high, strain], axis=1), start1)
        u = start
        yield
        for step in range(ITERS - 1):
            high, low = split(respond(u))
            u = u - (dot(high, newton_high) + dot(low, newton_high) + dot(high, newton_low))
            yield
        h = respond(u)
        last = u - dot(h.astype(BF16), newton_high)
        high, low = split(start - u + h)
        both = dot(high, back)
        change = both[:, 0:count] + both[:, count:] + dot(low, back[:, 0:count])
        yield
        stress = lax.dot_general(
            stress_m, respond(last).astype(BF16), (((1,), (1,)), ((), ())), preferred_element_type=F32
        )
        for g in range(part):
            rows = slice(g * layers, (g + 1) * layers)
            new_states[c + g] = states[c + g] - change[rows].T
            stresses[c + g] = stress[0:8, rows]
        yield

    chunks = [chunk(c) for c in range(0, number, part)]
    for stage in range(ITERS + 2):
        for c in chunks:
            next(c)
    return new_states, stresses


def set_pencil(ref, entry, value):
    groups, count, group, layers = ref.shape
    place = lax.div(entry, group) * (count * group) + lax.rem(entry, group)
    ref.reshape(groups * count * group, layers)[pl.ds(place, count, stride=group), :] = value


def run_group(base, group, order_ref, state_ref, strain_ref, weights, stress_s, spare):
    count = weights[4].shape[1] // 2
    most = state_ref.shape[0] // count
    entries = [order_ref[0, base + g] for g in range(group)]
    pencils = [order_ref[1, base + g] for g in range(group)]
    states = [state_ref[pl.ds(e, count, stride=most), :] for e in entries]
    strains = [
        strain_ref[pl.ds(pl.multiple_of(jnp.maximum(p, 0) * 8, 8), 8), :] for p in pencils
    ]
    new_states, stresses = cells(states, strains, *(w[...] for w in weights))
    for g in range(group):
        spot = jnp.where(pencils[g] >= 0, pencils[g], spare)
        stress_s[pl.ds(pl.multiple_of(spot * 8, 8), 8), :] = stresses[g]
    return entries, [jnp.where(p >= 0, a, 0.0) for p, a in zip(pencils, new_states)]


def fluxes(s, side_mean, side_diff):
    lane_zero = lax.broadcasted_iota(jnp.int32, s[0].shape, 1) == 0

    def along(v):
        down = jnp.where(lane_zero, 0.0, pltpu.roll(v, 1, 1))
        return 0.5 * (v + down), v - down

    first = [along(side_mean(s[c]))[0] for c in (0, 5, 4)]
    second = [along(side_diff(s[c]))[0] for c in (5, 1, 3)]
    third = [along(side_mean(s[c]))[1] for c in (4, 3, 2)]
    half = [0.5 * (second[c] + third[c]) for c in range(3)]
    return [(first[c] + half[c], half[c] - first[c]) for c in range(3)]


def row_fluxes(stress_ref, i, columns):
    s = [stress_ref[pl.ds(i * columns * 8 + c, columns, stride=8), :] for c in range(6)]
    first_sub = lax.broadcasted_iota(jnp.int32, s[0].shape, 0) == 0

    def shift(v):
        return jnp.where(first_sub, 0.0, pltpu.roll(v, 1, 0))

    return fluxes(s, lambda v: 0.5 * (v + shift(v)), lambda v: v - shift(v))


def first_groups(order_ref, most, group):
    return lax.div(order_ref[0, most] + (group - 1), group)


def column_kernel(disp_ref, column_ref):
    for c in range(3):
        column_ref[c] = disp_ref[c, :, 0, :]


def row_kernel(disp_ref, yhalo_ref, row_ref):
    columns = disp_ref.shape[2]
    for c in range(3):
        row_ref[c] = jnp.zeros(row_ref.shape[1:], F32)
        row_ref[c, 0:columns] = disp_ref[c, 0]
        row_ref[c, columns : columns + 1] = yhalo_ref[c, 0:1]


def edge_kernel(
    group, most, order_vmem, disp_ref, xhalo_ref, yhalo_ref, stiff_ref, state_ref,
    start0_ref, start1_ref, high_ref, low_ref, back_ref, stress_ref,
    xface_ref, yface_ref, cface_ref, strain_ref, stress_out, done_ref,
    order_ref, order_sem,
):
    order_copy = pltpu.make_async_copy(order_vmem, order_ref, order_sem)
    order_copy.start()
    rows, columns, layers = stiff_ref.shape
    count = state_ref.shape[0] // most
    weights = (start0_ref, start1_ref, high_ref, low_ref, back_ref, stress_ref)
    tile = (columns, layers)
    lane = lax.broadcasted_iota(jnp.int32, tile, 1)
    sub = lax.broadcasted_iota(jnp.int32, tile, 0)
    last_lane = lane == layers - 1
    last_sub = sub == columns - 1

    more_x = lax.axis_index("gx") < lax.axis_size("gx") - 1
    more_y = lax.axis_index("gy") < lax.axis_size("gy") - 1

    def node_row(c, i):
        own = disp_ref[c, i] if i < rows else jnp.where(more_x, xhalo_ref[c, 0:columns], 0.0)
        edge = yhalo_ref[c, i : i + 1] if i < rows else jnp.where(more_x, xhalo_ref[c, columns : columns + 1], 0.0)
        edge = jnp.where(more_y, edge, 0.0)
        up = jnp.where(last_sub, jnp.broadcast_to(edge, tile), pltpu.roll(own, columns - 1, 0))
        mean, diff = 0.5 * (up + own), up - own
        mean_up = jnp.where(last_lane, 0.0, pltpu.roll(mean, layers - 1, 1))
        diff_up = jnp.where(last_lane, 0.0, pltpu.roll(diff, layers - 1, 1))
        return 0.5 * (mean_up + mean), 0.5 * (diff_up + diff), mean_up - mean

    lower = [node_row(c, 0) for c in range(3)]
    zero_tile = jnp.zeros(tile, F32)
    for i in range(rows):
        upper = [node_row(c, i + 1) for c in range(3)]
        g = [
            (upper[c][0] - lower[c][0], 0.5 * (upper[c][1] + lower[c][1]), 0.5 * (upper[c][2] + lower[c][2]))
            for c in range(3)
        ]
        lower = upper
        strain = [g[0][0], g[1][1], g[2][2], g[1][2] + g[2][1], g[0][2] + g[2][0], g[0][1] + g[1][0]]
        stiffness = stiff_ref[i]
        volume = strain[0] + strain[1] + strain[2]
        for c in range(8):
            place = pl.ds(i * columns * 8 + c, columns, stride=8)
            if c >= 6:
                strain_ref[place, :] = zero_tile
                continue
            strain_ref[place, :] = strain[c]
            stress_out[place, :] = stiffness * (volume + 2.0 * strain[c] if c < 3 else strain[c])

    order_copy.wait()

    def body(q, carry):
        _, states = run_group(
            q * group, group, order_ref, state_ref, strain_ref, weights, stress_out, rows * columns
        )
        for g in range(group):
            done_ref[pl.ds(pl.multiple_of((q * group + g) * count, count), count), :] = states[g]
        return carry

    lax.fori_loop(0, first_groups(order_ref, most, group), body, 0)

    last = row_fluxes(stress_out, rows - 1, columns)
    for c in range(3):
        xface_ref[c] = -last[c][1]
    s = [stress_out[pl.ds((columns - 1) * 8 + c, rows, stride=columns * 8), :] for c in range(6)]
    side = fluxes(s, lambda v: 0.5 * v, lambda v: -v)
    for c in range(3):
        yface_ref[c] = -side[c][0]
        yface_ref[c, 1:rows] = yface_ref[c, 1:rows] - side[c][1][0 : rows - 1]
        cface_ref[c : c + 1] = -side[c][1][rows - 1 : rows]


def late_chunks(groups):
    return min(2, groups)


def inner_kernel(
    rows, columns, order_vmem, state_ref, strain_ref, stress_in, done_ref,
    start0_ref, start1_ref, high_ref, low_ref, back_ref, stress_ref,
    stress_s, out_hbm, out_s,
    sems, order_ref, order_sem,
):
    order_copy = pltpu.make_async_copy(order_vmem, order_ref, order_sem)
    order_copy.start()
    groups, count, group, layers = out_s.shape
    most = groups * group
    weights = (start0_ref, start1_ref, high_ref, low_ref, back_ref, stress_ref)
    stress_s[...] = stress_in[...]
    order_copy.wait()
    before = first_groups(order_ref, most, group)
    after = lax.div(order_ref[0, most + 1] + (group - 1), group)

    early = groups - late_chunks(groups)

    def store(q):
        return pltpu.make_async_copy(
            out_s.at[q], out_hbm.at[:, pl.ds(q * group, group), :], sems.at[q]
        )

    def copy(q, carry):
        for g in range(group):
            place = q * group + g
            set_pencil(
                out_s, order_ref[0, place],
                done_ref[pl.ds(pl.multiple_of(place * count, count), count), :],
            )
        return carry

    def clear(q, carry):
        for g in range(group):
            set_pencil(out_s, order_ref[0, q * group + g], jnp.zeros((count, layers), F32))
        return carry

    lax.fori_loop(0, before, copy, 0)
    lax.fori_loop(jnp.maximum(before, after), groups, clear, 0)

    def body(q, sent):
        entries, states = run_group(
            q * group, group, order_ref, state_ref, strain_ref, weights, stress_s, rows * columns
        )
        for g in range(group):
            set_pencil(out_s, entries[g], states[g])
        whole = jnp.maximum(sent, lax.div(entries[group - 1] + 1, group))

        def send(chunk, carry):
            store(chunk).start()
            return carry

        whole = jnp.minimum(whole, early)
        lax.fori_loop(sent, whole, send, 0)
        return whole

    sent = lax.fori_loop(before, after, body, 0)

    def send(chunk, carry):
        store(chunk).start()
        return carry

    lax.fori_loop(sent, early, send, 0)

    for q in range(early):
        store(q).wait()


def update_kernel(
    disp_ref, velocity_ref, external_ref, mass_ref, stress_ref, xface_ref, yface_ref, cface_ref,
    state_ref, state_in, disp_hbm, velocity_hbm, state_hbm, disp_out, velocity_out, sems, state_sems,
):
    groups, _, group, _ = state_ref.shape
    copies = []
    for n, q in enumerate(range(groups - late_chunks(groups), groups)):
        copies.append(
            pltpu.make_async_copy(
                state_ref.at[q], state_hbm.at[:, pl.ds(q * group, group), :], state_sems.at[n]
            )
        )
        copies[-1].start()
    rows, columns, layers = mass_ref.shape
    tile = (columns, layers)
    less_x = lax.axis_index("gx") > 0
    first_sub = lax.broadcasted_iota(jnp.int32, tile, 0) == 0
    first_sub = jnp.logical_and(first_sub, lax.axis_index("gy") > 0)
    below = None
    for i in range(rows):
        factor = STEP / mass_ref[i]
        here = row_fluxes(stress_ref, i, columns)
        for c in range(3):
            internal = -here[c][0] if below is None else -(here[c][0] + below[c][1])
            edge = yface_ref[c, i : i + 1]
            if i == 0:
                edge = edge + jnp.where(less_x, cface_ref[c : c + 1], 0.0)
                internal = internal + jnp.where(less_x, xface_ref[c], 0.0)
            internal = internal + jnp.where(first_sub, jnp.broadcast_to(edge, tile), 0.0)
            velocity = velocity_ref[c, i] + factor * (external_ref[c, i] - internal)
            velocity_out[c, i] = velocity
            disp_out[c, i] = disp_ref[c, i] + STEP * velocity
        below = here
    for c in range(3):
        for n, (ours, whole) in enumerate(((velocity_out, velocity_hbm), (disp_out, disp_hbm))):
            copies.append(pltpu.make_async_copy(ours.at[c], whole.at[c], sems.at[n, c]))
            copies[-1].start()
    for copy in copies:
        copy.wait()


def shape(*dims, dtype=F32):
    return jax.ShapeDtypeStruct(dims, dtype)


def on_device(
    displacement, velocity, external_force, node_mass, stiffness, cloak_list, micro_state,
    localization, modes, point_weight, point_modulus, softening,
):
    rows, columns, layers = stiffness.shape
    points, count = modes.shape
    most = cloak_list.shape[2]
    gx, gy = lax.axis_size("gx"), lax.axis_size("gy")
    along_x = [((i + 1) % gx, i) for i in range(gx)]
    along_y = [((j + 1) % gy, j) for j in range(gy)]
    both = [((i + 1) % gx * gy + (j + 1) % gy, i * gy + j) for i in range(gx) for j in range(gy)]
    back = lambda pairs: [(b, a) for a, b in pairs]
    group = 8
    small = pltpu.CompilerParams(vmem_limit_bytes=4 * 2**20)
    medium = pltpu.CompilerParams(vmem_limit_bytes=16 * 2**20)
    long = pl.CostEstimate(flops=10**10, bytes_accessed=10**6, transcendentals=0)
    yhalo = pl.pallas_call(
        column_kernel, out_shape=shape(3, rows, layers), in_specs=[VMEM], out_specs=VMEM,
        compiler_params=small, cost_estimate=long,
    )(displacement)
    yhalo = lax.ppermute(yhalo, "gy", along_y)

    order_shape = shape(8, (most + 2 + 127) // 128 * 128, dtype=jnp.int32)
    weight, modulus, soft = (a.reshape(1, points) for a in (point_weight, point_modulus, softening))
    half, order = pl.pallas_call(
        functools.partial(half_kernel, rows, columns),
        out_shape=(shape(count, count), order_shape),
        in_specs=[VMEM] * 4,
        out_specs=(VMEM,) * 2,
        scratch_shapes=[pltpu.VMEM(order_shape.shape, jnp.int32)],
        compiler_params=medium,
        cost_estimate=long,
    )(modes, weight, modulus, cloak_list[0])

    xhalo = pl.pallas_call(
        row_kernel, out_shape=shape(3, 2 * columns, layers), in_specs=[VMEM] * 2, out_specs=VMEM,
        compiler_params=small,
    )(displacement, yhalo)
    xhalo = lax.ppermute(xhalo, "gx", along_x)

    matrices = pl.pallas_call(
        matrices_kernel,
        out_shape=tuple(shape(n, points, dtype=BF16) for n in (2 * count, 2 * count, points, points))
        + (shape(points, 2 * count, dtype=BF16), shape(16, points, dtype=BF16)),
        in_specs=[VMEM] * 6,
        out_specs=(VMEM,) * 6,
        scratch_shapes=[pltpu.VMEM((16, points), F32)],
        compiler_params=medium,
        cost_estimate=long,
    )(half, modes, localization.T, weight, modulus, soft)

    groups = most // group
    states = micro_state.reshape(count * most, layers)
    strain_shape = shape(rows * columns * 8, layers)
    stress_shape = shape(rows * columns * 8 + 8, layers)
    xface, yface, cface, strain, stress, done = pl.pallas_call(
        functools.partial(edge_kernel, group, most),
        out_shape=(
            shape(3, columns, layers), shape(3, rows, layers), shape(3, layers),
            strain_shape, stress_shape, shape(most * count, layers),
        ),
        in_specs=[VMEM] * 12,
        out_specs=(VMEM,) * 6,
        scratch_shapes=[pltpu.SMEM(order_shape.shape, jnp.int32), pltpu.SemaphoreType.DMA],
        compiler_params=pltpu.CompilerParams(vmem_limit_bytes=30 * 2**20),
        cost_estimate=pl.CostEstimate(flops=10**10, bytes_accessed=10**7, transcendentals=0),
    )(order, displacement, xhalo, yhalo, stiffness, states, *matrices)

    xface = lax.ppermute(xface, "gx", back(along_x))
    yface = lax.ppermute(yface, "gy", back(along_y))
    cface = lax.ppermute(cface, ("gx", "gy"), back(both))

    stress, new_state, waiting = pl.pallas_call(
        functools.partial(inner_kernel, rows, columns),
        out_shape=(
            stress_shape, shape(count, most, layers), shape(groups, count, group, layers),
        ),
        in_specs=[VMEM] * 11,
        out_specs=(VMEM, HBM, VMEM),
        scratch_shapes=[
            pltpu.SemaphoreType.DMA((groups,)),
            pltpu.SMEM(order_shape.shape, jnp.int32), pltpu.SemaphoreType.DMA,
        ],
        compiler_params=pltpu.CompilerParams(vmem_limit_bytes=30 * 2**20),
        cost_estimate=pl.CostEstimate(flops=2 * 10**10, bytes_accessed=10**7, transcendentals=0),
    )(order, states, strain, stress, done, *matrices)

    displacement_next, velocity_next, new_state = pl.pallas_call(
        update_kernel,
        out_shape=(shape(3, rows, columns, layers),) * 2 + (shape(count, most, layers),),
        in_specs=[VMEM] * 9 + [HBM],
        out_specs=(HBM,) * 3,
        input_output_aliases={9: 2},
        scratch_shapes=[pltpu.VMEM(displacement.shape, F32)] * 2
        + [pltpu.SemaphoreType.DMA((2, 3)), pltpu.SemaphoreType.DMA((late_chunks(groups),))],
        compiler_params=pltpu.CompilerParams(vmem_limit_bytes=16 * 2**20),
    )(displacement, velocity, external_force, node_mass, stress, xface, yface, cface, waiting, new_state)
    return displacement_next, velocity_next, new_state.reshape(micro_state.shape)


def solution(mesh):
    field = P(None, "gx", "gy", None)
    grid = P("gx", "gy", None)
    state = P("gx", "gy", None, None, None)
    in_specs = (field, field, field, grid, grid, P("gx", None, None), state, P(), P(), P(), P(), P())
    return jax.shard_map(
        on_device, mesh=mesh, in_specs=in_specs, out_specs=(field, field, state), check_vma=False
    )
```

```python
import functools

import jax
import jax.numpy as jnp
from jax import lax
from jax.experimental import pallas as pl
from jax.experimental.pallas import tpu as pltpu
from jax.sharding import PartitionSpec as P

ITERS = 3
STEP = 0.25
HIGHEST = lax.Precision.HIGHEST
F32 = jnp.float32
BF16 = jnp.bfloat16
VMEM = pl.BlockSpec(memory_space=pltpu.VMEM)
HBM = pl.BlockSpec(memory_space=pltpu.HBM)


def split(x):
    high = x.astype(BF16)
    return high, (x - high.astype(F32)).astype(BF16)


def dot(a, b):
    return jnp.dot(a, b, preferred_element_type=F32)


def exact(a, b):
    return jnp.dot(a, b, precision=HIGHEST, preferred_element_type=F32)


def transposed_product(a, b):
    terms = []
    for x in (a, b):
        one = x.astype(BF16).astype(F32)
        two = (x - one).astype(BF16).astype(F32)
        terms.append((one, two, x - one - two))
    (a1, a2, a3), (b1, b2, b3) = terms
    left = jnp.concatenate([a1, a1, a2, a2, a1, a3], axis=0).astype(BF16)
    right = jnp.concatenate([b1, b2, b1, b2, b3, b1], axis=0).astype(BF16)
    return lax.dot_general(left, right, (((0,), (0,)), ((), ())), preferred_element_type=F32)


def lane_of(x, k):
    return jnp.take_along_axis(x, jnp.full(x.shape, k, jnp.int32), axis=1, mode="promise_in_bounds")


def row_of(x, s):
    return jnp.take_along_axis(x, jnp.full(x.shape, s, jnp.int32), axis=0, mode="promise_in_bounds")


def invert_two(a, b, c):
    scale = 1.0 / (a * c - b * b)
    return c * scale, -(b * scale), a * scale


def sweep(blocks, first, last):
    tile = blocks[0].shape
    size = tile[1]
    count = len(blocks)
    lane = lax.broadcasted_iota(jnp.int32, tile, 1)
    row = lax.broadcasted_iota(jnp.int32, tile, 0)

    def spread(x, s):
        return jnp.broadcast_to(x[s : s + 1, :], tile)

    for b in range(first, last):
        before = panel = blocks[b]
        for s in range(0, 8, 4):
            k = b * 8 + s
            lanes4 = jnp.logical_and(lane >= k, lane < k + 4)
            rows4 = jnp.logical_and(row >= s, row < s + 4)
            c = [lane_of(panel, k + i) for i in range(4)]
            r = [
                jnp.where(lane == k + i, 1.0, jnp.where(lanes4, 0.0, spread(panel, s + i)))
                for i in range(4)
            ]
            p = [[row_of(c[j], s + i) for j in range(i + 1)] for i in range(4)]
            (b00, b01), (b10, b11) = p[2][:2], p[3][:2]
            i00, i10, i11 = invert_two(p[0][0], p[1][0], p[1][1])
            w00, w01 = b00 * i00 + b01 * i10, b00 * i10 + b01 * i11
            w10, w11 = b10 * i00 + b11 * i10, b10 * i10 + b11 * i11
            j00, j10, j11 = invert_two(
                p[2][2] - (w00 * b00 + w01 * b01),
                p[3][2] - (w10 * b00 + w11 * b01),
                p[3][3] - (w10 * b10 + w11 * b11),
            )
            y2 = r[2] - (w00 * r[0] + w01 * r[1])
            y3 = r[3] - (w10 * r[0] + w11 * r[1])
            n2, n3 = j00 * y2 + j10 * y3, j10 * y2 + j11 * y3
            n0 = (i00 * r[0] + i10 * r[1]) - (w00 * n2 + w10 * n3)
            n1 = (i10 * r[0] + i11 * r[1]) - (w01 * n2 + w11 * n3)
            f = [jnp.where(row == s + i, -1.0, jnp.where(rows4, 0.0, c[i])) for i in range(4)]
            rest = jnp.where(jnp.logical_or(lanes4, rows4), 0.0, panel)
            panel = rest - ((f[0] * n0 + f[1] * n1) + (f[2] * n2 + f[3] * n3))
        inside = jnp.logical_and(lane >= b * 8, lane < b * 8 + 8)
        panel = jnp.where(inside, -panel, panel)
        change = transposed_product(before, panel)
        for i in range(count):
            old = blocks[i]
            kept = jnp.where(inside, 0.0, old)
            if i == b:
                blocks[i] = panel
            elif i == b + 1:
                t = [lane_of(old, b * 8 + s) * spread(panel, s) for s in range(8)]
                blocks[i] = kept - (((t[0] + t[1]) + (t[2] + t[3])) + ((t[4] + t[5]) + (t[6] + t[7])))
            else:
                blocks[i] = kept - change[i * 8 : i * 8 + 8]
    return jnp.concatenate(blocks, axis=0)


def near(a, b):
    (ah, al), (bh, bl) = split(a), split(b)
    return dot(ah, bh) + dot(al, bh) + dot(ah, bl)


def order_entries(rows, columns, lists_ref, order_ref, line):
    most = lists_ref.shape[1]
    width = order_ref.shape[1]
    tile = order_ref.shape
    line[...] = jnp.full(line.shape, -1, jnp.int32)
    line[0:1, 0:most] = lists_ref[pl.ds(lax.axis_index("gy"), 1), :]
    pencil = jnp.broadcast_to(line[0:1, :].astype(F32), tile)
    lane = lax.broadcasted_iota(jnp.int32, tile, 1)
    row = lax.broadcasted_iota(jnp.int32, tile, 0)
    column = pencil - columns * jnp.floor((pencil + 0.5) / columns)
    listed = pencil >= 0.0
    face = jnp.logical_or(pencil >= (rows - 1) * columns, column == columns - 1)
    kind = jnp.where(listed, jnp.where(face, 0, 1), jnp.where(lane < most, 2, 3))
    flags = jnp.where(kind == row, 1.0, 0.0).astype(BF16)
    square = (width, width)
    first = lax.broadcasted_iota(jnp.int32, square, 0)
    second = lax.broadcasted_iota(jnp.int32, square, 1)
    before = dot(flags, (first < second).astype(F32).astype(BF16))
    totals = dot(flags, jnp.ones(square, BF16))
    faces, number = totals[0:1], totals[0:1] + totals[1:2]
    kind = kind[0:1]
    place = jnp.where(
        kind == 0, before[0:1],
        jnp.where(kind == 1, faces + before[1:2], jnp.where(kind == 2, number + before[2:3], -1.0)),
    )
    moves = (jnp.broadcast_to(place, square) == first.astype(F32)).astype(F32)
    values = jnp.where(row == 0, lane.astype(F32), pencil)
    ordered = lax.dot_general(
        values, moves, (((1,), (1,)), ((), ())), precision=HIGHEST, preferred_element_type=F32
    )
    counts = jnp.where(lane == most, jnp.broadcast_to(faces, tile), jnp.broadcast_to(number, tile))
    tail = jnp.logical_and(row == 0, lane >= most)
    order_ref[...] = jnp.where(tail, counts, ordered).astype(jnp.int32)


def row_blocks(matrix):
    return [matrix[i : i + 8] for i in range(0, matrix.shape[0], 8)]


def half_kernel(rows, columns, modes_ref, weight_ref, modulus_ref, lists_ref, half_ref, order_ref, line):
    order_entries(rows, columns, lists_ref, order_ref, line)
    points, count = modes_ref.shape
    modes = modes_ref[...]
    matrix = exact(modes.T * (weight_ref[...] / points * modulus_ref[...]), modes)
    half_ref[...] = sweep(row_blocks(matrix), 0, count * 5 // 64)


def matrices_kernel(
    half_ref, modes_ref, local_ref, weight_ref, modulus_ref, soft_ref,
    start0_ref, start1_ref, high_ref, low_ref, back_ref, stress_ref, wide,
):
    points, count = modes_ref.shape
    modes_t = modes_ref[...].T
    weight = weight_ref[...] / points
    modulus = modulus_ref[...]
    root = jnp.sqrt(soft_ref[...])
    scale = weight * modulus / root
    inverted = -sweep(row_blocks(half_ref[...]), count * 5 // 64, count // 8)
    wide[...] = jnp.zeros_like(wide)
    wide[0 : local_ref.shape[0], :] = local_ref[...]
    local = wide[...]
    stress_ref[...] = (local * scale).astype(BF16)
    high, low = split(modes_t * root)
    start0_ref[0:count] = high
    start0_ref[count:] = high
    start1_ref[0:count] = low
    soft_local = local[0:8] * root
    local_high = soft_local.astype(BF16).astype(F32)
    part = [local_high, local_high, soft_local - local_high, jnp.zeros_like(local_high)]
    start1_ref[count:] = jnp.concatenate(part * (count // 32), axis=0).astype(BF16)
    back = near((modes_t * scale).T, inverted)
    high, low = split(back)
    back_ref[:, 0:count] = high
    back_ref[:, count:] = low
    newton = near(back, modes_t * root)
    high, low = split(newton)
    high_ref[...] = high
    low_ref[...] = low


def respond(u):
    return u * lax.rsqrt(1.0 + u * u)


def cells(states, strains, start0, start1, newton_high, newton_low, back, stress_m):
    layers = states[0].shape[1]
    count = states[0].shape[0]
    number = len(states)
    part = min(2, number)
    turned = [state.T for state in states]
    place = lax.broadcasted_iota(jnp.int32, (layers, count), 1) // 32
    strain_parts = []
    each = count // 32
    for q in range(0, number, each):
        rows = []
        for strain in strains[q : q + each]:
            high = strain.astype(BF16).astype(F32)
            rows += [high, strain - high, high, jnp.zeros_like(high)]
        rows = jnp.concatenate(rows, axis=0).T
        strain_parts += [jnp.where(place == g, rows, 0.0).astype(BF16) for g in range(each)]
    new_states, stresses = [None] * number, [None] * number

    def chunk(c):
        high, low = split(jnp.concatenate(turned[c : c + part], axis=0))
        strain = jnp.concatenate(strain_parts[c : c + part], axis=0)
        start = dot(jnp.concatenate([high, low], axis=1), start0)
        start = start + dot(jnp.concatenate([high, strain], axis=1), start1)
        u = start
        yield
        for step in range(ITERS - 1):
            high, low = split(respond(u))
            u = u - (dot(high, newton_high) + dot(low, newton_high) + dot(high, newton_low))
            yield
        h = respond(u)
        last = u - dot(h.astype(BF16), newton_high)
        high, low = split(start - u + h)
        both = dot(high, back)
        change = both[:, 0:count] + both[:, count:] + dot(low, back[:, 0:count])
        yield
        stress = lax.dot_general(
            stress_m, respond(last).astype(BF16), (((1,), (1,)), ((), ())), preferred_element_type=F32
        )
        for g in range(part):
            rows = slice(g * layers, (g + 1) * layers)
            new_states[c + g] = states[c + g] - change[rows].T
            stresses[c + g] = stress[0:8, rows]
        yield

    chunks = [chunk(c) for c in range(0, number, part)]
    for stage in range(ITERS + 2):
        for c in chunks:
            next(c)
    return new_states, stresses


def set_pencil(ref, entry, value):
    groups, count, group, layers = ref.shape
    place = lax.div(entry, group) * (count * group) + lax.rem(entry, group)
    ref.reshape(groups * count * group, layers)[pl.ds(place, count, stride=group), :] = value


def run_group(base, group, order_ref, state_ref, strain_ref, weights, stress_s, spare):
    count = weights[4].shape[1] // 2
    most = state_ref.shape[0] // count
    entries = [order_ref[0, base + g] for g in range(group)]
    pencils = [order_ref[1, base + g] for g in range(group)]
    states = [state_ref[pl.ds(e, count, stride=most), :] for e in entries]
    strains = [
        strain_ref[pl.ds(pl.multiple_of(jnp.maximum(p, 0) * 8, 8), 8), :] for p in pencils
    ]
    new_states, stresses = cells(states, strains, *(w[...] for w in weights))
    for g in range(group):
        spot = jnp.where(pencils[g] >= 0, pencils[g], spare)
        stress_s[pl.ds(pl.multiple_of(spot * 8, 8), 8), :] = stresses[g]
    return entries, [jnp.where(p >= 0, a, 0.0) for p, a in zip(pencils, new_states)]


def fluxes(s, side_mean, side_diff):
    lane_zero = lax.broadcasted_iota(jnp.int32, s[0].shape, 1) == 0

    def along(v):
        down = jnp.where(lane_zero, 0.0, pltpu.roll(v, 1, 1))
        return 0.5 * (v + down), v - down

    first = [along(side_mean(s[c]))[0] for c in (0, 5, 4)]
    second = [along(side_diff(s[c]))[0] for c in (5, 1, 3)]
    third = [along(side_mean(s[c]))[1] for c in (4, 3, 2)]
    half = [0.5 * (second[c] + third[c]) for c in range(3)]
    return [(first[c] + half[c], half[c] - first[c]) for c in range(3)]


def row_fluxes(stress_ref, i, columns):
    s = [stress_ref[pl.ds(i * columns * 8 + c, columns, stride=8), :] for c in range(6)]
    first_sub = lax.broadcasted_iota(jnp.int32, s[0].shape, 0) == 0

    def shift(v):
        return jnp.where(first_sub, 0.0, pltpu.roll(v, 1, 0))

    return fluxes(s, lambda v: 0.5 * (v + shift(v)), lambda v: v - shift(v))


def first_groups(order_ref, most, group):
    return lax.div(order_ref[0, most] + (group - 1), group)


def column_kernel(disp_ref, column_ref):
    for c in range(3):
        column_ref[c] = disp_ref[c, :, 0, :]


def row_kernel(disp_ref, yhalo_ref, row_ref):
    columns = disp_ref.shape[2]
    for c in range(3):
        row_ref[c] = jnp.zeros(row_ref.shape[1:], F32)
        row_ref[c, 0:columns] = disp_ref[c, 0]
        row_ref[c, columns : columns + 1] = yhalo_ref[c, 0:1]


def edge_kernel(
    group, most, order_vmem, disp_ref, xhalo_ref, yhalo_ref, stiff_ref, state_ref,
    start0_ref, start1_ref, high_ref, low_ref, back_ref, stress_ref,
    xface_ref, yface_ref, cface_ref, strain_ref, stress_out, done_ref,
    order_ref, order_sem,
):
    order_copy = pltpu.make_async_copy(order_vmem, order_ref, order_sem)
    order_copy.start()
    rows, columns, layers = stiff_ref.shape
    count = state_ref.shape[0] // most
    weights = (start0_ref, start1_ref, high_ref, low_ref, back_ref, stress_ref)
    tile = (columns, layers)
    lane = lax.broadcasted_iota(jnp.int32, tile, 1)
    sub = lax.broadcasted_iota(jnp.int32, tile, 0)
    last_lane = lane == layers - 1
    last_sub = sub == columns - 1

    more_x = lax.axis_index("gx") < lax.axis_size("gx") - 1
    more_y = lax.axis_index("gy") < lax.axis_size("gy") - 1

    def node_row(c, i):
        own = disp_ref[c, i] if i < rows else jnp.where(more_x, xhalo_ref[c, 0:columns], 0.0)
        edge = yhalo_ref[c, i : i + 1] if i < rows else jnp.where(more_x, xhalo_ref[c, columns : columns + 1], 0.0)
        edge = jnp.where(more_y, edge, 0.0)
        up = jnp.where(last_sub, jnp.broadcast_to(edge, tile), pltpu.roll(own, columns - 1, 0))
        mean, diff = 0.5 * (up + own), up - own
        mean_up = jnp.where(last_lane, 0.0, pltpu.roll(mean, layers - 1, 1))
        diff_up = jnp.where(last_lane, 0.0, pltpu.roll(diff, layers - 1, 1))
        return 0.5 * (mean_up + mean), 0.5 * (diff_up + diff), mean_up - mean

    lower = [node_row(c, 0) for c in range(3)]
    zero_tile = jnp.zeros(tile, F32)
    for i in range(rows):
        upper = [node_row(c, i + 1) for c in range(3)]
        g = [
            (upper[c][0] - lower[c][0], 0.5 * (upper[c][1] + lower[c][1]), 0.5 * (upper[c][2] + lower[c][2]))
            for c in range(3)
        ]
        lower = upper
        strain = [g[0][0], g[1][1], g[2][2], g[1][2] + g[2][1], g[0][2] + g[2][0], g[0][1] + g[1][0]]
        stiffness = stiff_ref[i]
        volume = strain[0] + strain[1] + strain[2]
        for c in range(8):
            place = pl.ds(i * columns * 8 + c, columns, stride=8)
            if c >= 6:
                strain_ref[place, :] = zero_tile
                continue
            strain_ref[place, :] = strain[c]
            stress_out[place, :] = stiffness * (volume + 2.0 * strain[c] if c < 3 else strain[c])

    order_copy.wait()

    def body(q, carry):
        _, states = run_group(
            q * group, group, order_ref, state_ref, strain_ref, weights, stress_out, rows * columns
        )
        for g in range(group):
            done_ref[pl.ds(pl.multiple_of((q * group + g) * count, count), count), :] = states[g]
        return carry

    lax.fori_loop(0, first_groups(order_ref, most, group), body, 0)

    last = row_fluxes(stress_out, rows - 1, columns)
    for c in range(3):
        xface_ref[c] = -last[c][1]
    s = [stress_out[pl.ds((columns - 1) * 8 + c, rows, stride=columns * 8), :] for c in range(6)]
    side = fluxes(s, lambda v: 0.5 * v, lambda v: -v)
    for c in range(3):
        yface_ref[c] = -side[c][0]
        yface_ref[c, 1:rows] = yface_ref[c, 1:rows] - side[c][1][0 : rows - 1]
        cface_ref[c : c + 1] = -side[c][1][rows - 1 : rows]


def late_chunks(groups):
    return min(2, groups)


def inner_kernel(
    rows, columns, order_vmem, state_ref, strain_ref, stress_in, done_ref,
    start0_ref, start1_ref, high_ref, low_ref, back_ref, stress_ref,
    force_ref, out_hbm, out_s,
    stress_s, sems, order_ref, order_sem,
):
    order_copy = pltpu.make_async_copy(order_vmem, order_ref, order_sem)
    order_copy.start()
    groups, count, group, layers = out_s.shape
    most = groups * group
    weights = (start0_ref, start1_ref, high_ref, low_ref, back_ref, stress_ref)
    stress_s[...] = stress_in[...]
    order_copy.wait()
    before = first_groups(order_ref, most, group)
    after = lax.div(order_ref[0, most + 1] + (group - 1), group)

    early = groups - late_chunks(groups)

    def store(q):
        return pltpu.make_async_copy(
            out_s.at[q], out_hbm.at[:, pl.ds(q * group, group), :], sems.at[q]
        )

    def copy(q, carry):
        for g in range(group):
            place = q * group + g
            set_pencil(
                out_s, order_ref[0, place],
                done_ref[pl.ds(pl.multiple_of(place * count, count), count), :],
            )
        return carry

    def clear(q, carry):
        for g in range(group):
            set_pencil(out_s, order_ref[0, q * group + g], jnp.zeros((count, layers), F32))
        return carry

    lax.fori_loop(0, before, copy, 0)
    lax.fori_loop(jnp.maximum(before, after), groups, clear, 0)

    def body(q, sent):
        entries, states = run_group(
            q * group, group, order_ref, state_ref, strain_ref, weights, stress_s, rows * columns
        )
        for g in range(group):
            set_pencil(out_s, entries[g], states[g])
        whole = jnp.maximum(sent, lax.div(entries[group - 1] + 1, group))

        def send(chunk, carry):
            store(chunk).start()
            return carry

        whole = jnp.minimum(whole, early)
        lax.fori_loop(sent, whole, send, 0)
        return whole

    sent = lax.fori_loop(before, after, body, 0)

    def send(chunk, carry):
        store(chunk).start()
        return carry

    lax.fori_loop(sent, early, send, 0)

    below = None
    for i in range(rows):
        here = row_fluxes(stress_s, i, columns)
        for c in range(3):
            force_ref[c, i] = -here[c][0] if below is None else -(here[c][0] + below[c][1])
        below = here
    for q in range(early):
        store(q).wait()


def update_kernel(
    disp_ref, velocity_ref, external_ref, mass_ref, force_ref, xface_ref, yface_ref, cface_ref,
    state_ref, state_in, disp_hbm, velocity_hbm, state_hbm, disp_out, velocity_out, sems, state_sems,
):
    groups, _, group, _ = state_ref.shape
    copies = []
    for n, q in enumerate(range(groups - late_chunks(groups), groups)):
        copies.append(
            pltpu.make_async_copy(
                state_ref.at[q], state_hbm.at[:, pl.ds(q * group, group), :], state_sems.at[n]
            )
        )
        copies[-1].start()
    rows, columns, layers = mass_ref.shape
    tile = (columns, layers)
    less_x = lax.axis_index("gx") > 0
    first_sub = lax.broadcasted_iota(jnp.int32, tile, 0) == 0
    first_sub = jnp.logical_and(first_sub, lax.axis_index("gy") > 0)
    factors = [STEP / mass_ref[i] for i in range(rows)]
    for c in range(3):
        for i in range(rows):
            edge = yface_ref[c, i : i + 1]
            if i == 0:
                edge = edge + jnp.where(less_x, cface_ref[c : c + 1], 0.0)
            internal = force_ref[c, i] + jnp.where(first_sub, jnp.broadcast_to(edge, tile), 0.0)
            if i == 0:
                internal = internal + jnp.where(less_x, xface_ref[c], 0.0)
            velocity = velocity_ref[c, i] + factors[i] * (external_ref[c, i] - internal)
            velocity_out[c, i] = velocity
            disp_out[c, i] = disp_ref[c, i] + STEP * velocity
        for n, (ours, whole) in enumerate(((velocity_out, velocity_hbm), (disp_out, disp_hbm))):
            copies.append(pltpu.make_async_copy(ours.at[c], whole.at[c], sems.at[n, c]))
            copies[-1].start()
    for copy in copies:
        copy.wait()


def shape(*dims, dtype=F32):
    return jax.ShapeDtypeStruct(dims, dtype)


def on_device(
    displacement, velocity, external_force, node_mass, stiffness, cloak_list, micro_state,
    localization, modes, point_weight, point_modulus, softening,
):
    rows, columns, layers = stiffness.shape
    points, count = modes.shape
    most = cloak_list.shape[2]
    gx, gy = lax.axis_size("gx"), lax.axis_size("gy")
    along_x = [((i + 1) % gx, i) for i in range(gx)]
    along_y = [((j + 1) % gy, j) for j in range(gy)]
    both = [((i + 1) % gx * gy + (j + 1) % gy, i * gy + j) for i in range(gx) for j in range(gy)]
    back = lambda pairs: [(b, a) for a, b in pairs]
    group = 8
    small = pltpu.CompilerParams(vmem_limit_bytes=4 * 2**20)
    medium = pltpu.CompilerParams(vmem_limit_bytes=16 * 2**20)
    long = pl.CostEstimate(flops=10**10, bytes_accessed=10**6, transcendentals=0)
    yhalo = pl.pallas_call(
        column_kernel, out_shape=shape(3, rows, layers), in_specs=[VMEM], out_specs=VMEM,
        compiler_params=small, cost_estimate=long,
    )(displacement)
    yhalo = lax.ppermute(yhalo, "gy", along_y)

    order_shape = shape(8, (most + 2 + 127) // 128 * 128, dtype=jnp.int32)
    weight, modulus, soft = (a.reshape(1, points) for a in (point_weight, point_modulus, softening))
    half, order = pl.pallas_call(
        functools.partial(half_kernel, rows, columns),
        out_shape=(shape(count, count), order_shape),
        in_specs=[VMEM] * 4,
        out_specs=(VMEM,) * 2,
        scratch_shapes=[pltpu.VMEM(order_shape.shape, jnp.int32)],
        compiler_params=medium,
        cost_estimate=long,
    )(modes, weight, modulus, cloak_list[0])

    xhalo = pl.pallas_call(
        row_kernel, out_shape=shape(3, 2 * columns, layers), in_specs=[VMEM] * 2, out_specs=VMEM,
        compiler_params=small,
    )(displacement, yhalo)
    xhalo = lax.ppermute(xhalo, "gx", along_x)

    matrices = pl.pallas_call(
        matrices_kernel,
        out_shape=tuple(shape(n, points, dtype=BF16) for n in (2 * count, 2 * count, points, points))
        + (shape(points, 2 * count, dtype=BF16), shape(16, points, dtype=BF16)),
        in_specs=[VMEM] * 6,
        out_specs=(VMEM,) * 6,
        scratch_shapes=[pltpu.VMEM((16, points), F32)],
        compiler_params=medium,
        cost_estimate=long,
    )(half, modes, localization.T, weight, modulus, soft)

    groups = most // group
    states = micro_state.reshape(count * most, layers)
    strain_shape = shape(rows * columns * 8, layers)
    stress_shape = shape(rows * columns * 8 + 8, layers)
    xface, yface, cface, strain, stress, done = pl.pallas_call(
        functools.partial(edge_kernel, group, most),
        out_shape=(
            shape(3, columns, layers), shape(3, rows, layers), shape(3, layers),
            strain_shape, stress_shape, shape(most * count, layers),
        ),
        in_specs=[VMEM] * 12,
        out_specs=(VMEM,) * 6,
        scratch_shapes=[pltpu.SMEM(order_shape.shape, jnp.int32), pltpu.SemaphoreType.DMA],
        compiler_params=pltpu.CompilerParams(vmem_limit_bytes=30 * 2**20),
        cost_estimate=pl.CostEstimate(flops=10**10, bytes_accessed=10**7, transcendentals=0),
    )(order, displacement, xhalo, yhalo, stiffness, states, *matrices)

    xface = lax.ppermute(xface, "gx", back(along_x))
    yface = lax.ppermute(yface, "gy", back(along_y))
    cface = lax.ppermute(cface, ("gx", "gy"), back(both))

    force, new_state, waiting = pl.pallas_call(
        functools.partial(inner_kernel, rows, columns),
        out_shape=(
            shape(3, rows, columns, layers), shape(count, most, layers),
            shape(groups, count, group, layers),
        ),
        in_specs=[VMEM] * 11,
        out_specs=(VMEM, HBM, VMEM),
        scratch_shapes=[
            pltpu.VMEM(stress_shape.shape, F32),
            pltpu.SemaphoreType.DMA((groups,)),
            pltpu.SMEM(order_shape.shape, jnp.int32), pltpu.SemaphoreType.DMA,
        ],
        compiler_params=pltpu.CompilerParams(vmem_limit_bytes=30 * 2**20),
        cost_estimate=pl.CostEstimate(flops=2 * 10**10, bytes_accessed=10**7, transcendentals=0),
    )(order, states, strain, stress, done, *matrices)

    displacement_next, velocity_next, new_state = pl.pallas_call(
        update_kernel,
        out_shape=(shape(3, rows, columns, layers),) * 2 + (shape(count, most, layers),),
        in_specs=[VMEM] * 9 + [HBM],
        out_specs=(HBM,) * 3,
        input_output_aliases={9: 2},
        scratch_shapes=[pltpu.VMEM(displacement.shape, F32)] * 2
        + [pltpu.SemaphoreType.DMA((2, 3)), pltpu.SemaphoreType.DMA((late_chunks(groups),))],
        compiler_params=pltpu.CompilerParams(vmem_limit_bytes=16 * 2**20),
    )(displacement, velocity, external_force, node_mass, force, xface, yface, cface, waiting, new_state)
    return displacement_next, velocity_next, new_state.reshape(micro_state.shape)


def solution(mesh):
    field = P(None, "gx", "gy", None)
    grid = P("gx", "gy", None)
    state = P("gx", "gy", None, None, None)
    in_specs = (field, field, field, grid, grid, P("gx", None, None), state, P(), P(), P(), P(), P())
    return jax.shard_map(
        on_device, mesh=mesh, in_specs=in_specs, out_specs=(field, field, state), check_vma=False
    )
```
